512 devices in a mesh: row: 32 (over y, x), col: 16 (over z, core).
Axes of the slice: x: 4, y: 8, z: 8, core: 2. Of those that a mesh axis runs over, the one named last changes fastest.
Arguments:
- a_blocks: bfloat16 [16384, 64, 512], P(('row', 'col')), may hold values from -0.25 to 0.25
- a_index: int32 [16384, 8], P(('row', 'col')), may hold values from 0 to 16383, as said below
- p_blocks: bfloat16 [16384, 64, 128], P(('row', 'col')), may hold values from -0.75 to 0.75
- p_index: int32 [16384, 2], P(('row', 'col')), may hold values from 0 to 4095, as said below
Outputs:
- coarse: float32 [4096, 64, 320], P(('row', 'col'))
The draws below stay inside these ranges and needn't reach their ends.
Inputs may be any that keep to these rules, and one draw needn't show every extreme that they name: a_index[r, k] lies within 4 of r, counted modulo 16384; every row names r - 4 and r + 4. p_index[r, k] is r // 4 or r // 4 + 1, counted modulo 4096.
All inputs are finite; a program needn't handle non-finite values.
Results may differ from the reference program's by a relative error of at most 0.0042.
Values may be sent and summed in bfloat16 or wider, within the bound.
No kernel may reach another device: no remote copies, remote signals or barrier semaphores. Data moves between devices by JAX's collectives and lax.ppermute only.
A program may use at most 128 MiB of HBM per device.

```python
import jax
import jax.numpy as jnp
from jax import lax

BS = 64
RB = 32
KA = 8
KP = 2
RATIO = 4
HALO = 4
BAND = 5
NFB = 16384
NCB = 4096
N_ROW = 32
N_COL = 16


def draw_a_index(key, part):
    key = jax.random.fold_in(key, 11)
    total_rows = RB * N_ROW * N_COL
    row_ids = jnp.arange(total_rows, dtype=jnp.int32)
    extras = jax.random.randint(key, (total_rows, KA - 5), -HALO, HALO + 1)
    columns = [row_ids[:, None], row_ids[:, None] - 1, row_ids[:, None] + 1, row_ids[:, None] - HALO, row_ids[:, None] + HALO, row_ids[:, None] + extras]
    return (jnp.concatenate(columns, 1) % total_rows).astype(jnp.int32)


def draw_p_index(key, part):
    key = jax.random.fold_in(key, 23)
    total_rows = RB * N_ROW * N_COL
    coarse_count = total_rows // RATIO
    row_ids = jnp.arange(total_rows, dtype=jnp.int32)
    centre = row_ids // RATIO
    offsets = jax.random.randint(key, (total_rows, KP), 0, 2)
    at_edges = (row_ids == 0) | (row_ids == total_rows - 1)
    leading = jnp.where(at_edges, 0, offsets[:, 0])
    offsets = jnp.concatenate([leading[:, None], offsets[:, 1:]], 1)
    return ((centre[:, None] + offsets) % coarse_count).astype(jnp.int32)


def steps_of(rng, extent, pieces, smallest, largest):
    loudness, own = 1.0, jax.random.fold_in(rng, 6)
    for position, blocks in pieces:
        steps = jnp.exp(jax.random.uniform(jax.random.fold_in(own, position), (blocks,), jnp.float32, smallest / len(pieces), largest / len(pieces)))
        loudness = loudness * jnp.repeat(steps, extent[position] // blocks).reshape([-1 if axis == position else 1 for axis in range(len(extent))])
    return loudness


def scatter_about(key, extent, width, most, cuts=(), kind=jnp.bfloat16):
    gain = steps_of(key, extent, cuts, -0.22, 0.18) if cuts else 1.0
    drawn = jax.random.normal(key, extent, jnp.float32) * width * gain
    return jnp.minimum(jnp.maximum(drawn, -most), most).astype(kind)


def setup_inputs(seed: int = 0) -> dict:
    splits = jax.random.split(jax.random.key(seed), 5)
    a_blocks = scatter_about(splits[0], (NFB, BS, KA * BS), (BS * KA) ** -0.5, 0.25, ((0, 512),))
    a_index = draw_a_index(jax.random.fold_in(splits[4], 71), 0)
    p_blocks = scatter_about(splits[2], (NFB, BS, KP * BS), BS ** -0.5, 0.75, ((0, 512),))
    p_index = draw_p_index(jax.random.fold_in(splits[4], 71), 0)
    return dict(a_blocks=a_blocks, a_index=a_index, p_blocks=p_blocks, p_index=p_index)


def reference(a_blocks, a_index, p_blocks, p_index):
    block_size = p_blocks.shape[1]
    row_ids = jnp.arange(NFB, dtype=jnp.int32)
    centre = row_ids // RATIO
    offset = (p_index - centre[:, None] + NCB) % NCB
    chosen = (offset[:, :, None] == jnp.arange(2, dtype=jnp.int32)[None, None, :]).astype(jnp.float32)
    p_wide = p_blocks.astype(jnp.float32).reshape(NFB, block_size, KP, block_size)
    paired = jnp.einsum('rko,rbkd->rbod', chosen, p_wide, precision=lax.Precision.HIGHEST).astype(jnp.bfloat16)

    def one_group(group_start):
        a_part = lax.dynamic_slice_in_dim(a_blocks, group_start, RB, 0).astype(jnp.float32)
        a_part = a_part.reshape(RB, block_size, KA, block_size)
        col_ids = lax.dynamic_slice_in_dim(a_index, group_start, RB, 0)
        paired_part = lax.dynamic_slice_in_dim(paired, group_start, RB, 0).astype(jnp.float32)
        fetched = paired[col_ids].astype(jnp.float32)
        partial_terms = jnp.einsum('rakb,rkbod->rkoad', a_part, fetched, precision=lax.Precision.HIGHEST)
        own_centre = (group_start + jnp.arange(RB, dtype=jnp.int32)) // RATIO
        placed = (col_ids[:, :, None] // RATIO + jnp.arange(2, dtype=jnp.int32)[None, None, :]
                  - own_centre[:, None, None] + 1 + NCB) % NCB
        onehot = (placed[..., None] == jnp.arange(4, dtype=jnp.int32)).astype(jnp.float32)
        product = jnp.einsum('rkot,rkoad->ratd', onehot, partial_terms, precision=lax.Precision.HIGHEST)
        product = lax.optimization_barrier(product.astype(jnp.bfloat16)).astype(jnp.float32)
        contrib = jnp.einsum('rbod,rbtx->rodtx', paired_part, product, precision=lax.Precision.HIGHEST)
        return contrib.reshape(RB // RATIO, RATIO, 2, block_size, 4, block_size).sum(1)

    group_starts = jnp.arange(NFB // RB, dtype=jnp.int32) * RB
    summed = lax.map(one_group, group_starts).reshape(NCB, 2, block_size, 4, block_size)
    zero_col = jnp.zeros((NCB, block_size, 1, block_size), jnp.float32)
    lower_part = jnp.concatenate([zero_col, summed[:, 0]], 2)
    upper_part = jnp.concatenate([summed[:, 1], zero_col], 2)
    coarse = lower_part + jnp.roll(upper_part, 1, axis=0)
    return coarse.reshape(NCB, block_size, BAND * block_size)
```

```python
import jax
import jax.numpy as jnp
from jax import lax
from jax.experimental import pallas as pl
from jax.experimental.pallas import tpu as pltpu
from jax.sharding import PartitionSpec as P

BS = 64
KA = 8
RATIO = 4
GROUPS = 8
ROWS = RATIO * GROUPS
HALF = 2 * BS
WIDE = 4 * BS
BAND = 5 * BS
F32, BF16 = jnp.float32, jnp.bfloat16
SMEM = pl.BlockSpec(memory_space=pltpu.SMEM)
VMEM = pl.BlockSpec(memory_space=pltpu.VMEM)
ANY = pl.BlockSpec(memory_space=pl.ANY)


def low_half(rows):
    return lax.broadcasted_iota(jnp.int32, (rows, HALF), 1) < BS


def dot(x, y):
    return jnp.dot(x, y, preferred_element_type=F32)


def dot_rows(x, y):
    return lax.dot_general(x, y, (((0,), (0,)), ((), ())), preferred_element_type=F32)


def pair(p_idx, row, block):
    first = ((p_idx[0, row] - row // RATIO) & 1).astype(F32)
    second = ((p_idx[1, row] - row // RATIO) & 1).astype(F32)
    low = low_half(BS)
    x = block.astype(F32)
    y = pltpu.roll(x, BS, 1)
    here = x * jnp.where(low, 1.0 - first, second) + y * jnp.where(low, 1.0 - second, first)
    there = y * jnp.where(low, second, 1.0 - first) + x * jnp.where(low, first, 1.0 - second)
    return here.astype(BF16), there


def centred(there):
    low = low_half(BS)
    zero = jnp.zeros_like(there)
    return jnp.concatenate([jnp.where(low, zero, there), jnp.where(low, there, zero)], 1).astype(BF16)


def column(a_idx, k, row):
    return row + ((a_idx[k, row] - row + RATIO) & 15)


def spread(a_row, places):
    low = low_half(BS)
    tiles = [jnp.zeros((BS, HALF), F32)] * 2
    for j in range(KA // 2):
        x = a_row[:, j * HALF : (j + 1) * HALF].astype(F32)
        y = pltpu.roll(x, BS, 1)
        for blocks, at in ((x, (2 * j, 2 * j + 1)), (y, (2 * j + 1, 2 * j))):
            place = jnp.where(low, places[at[0]], places[at[1]])
            for t in range(2):
                wanted = jnp.where(low, 2 * t, 2 * t + 1)
                tiles[t] = tiles[t] + jnp.where(place == wanted, blocks, 0.0)
    return jnp.concatenate(tiles, 1).astype(BF16)


def shifted(x):
    return pltpu.roll(jnp.concatenate([x, jnp.zeros((BS, HALF), F32)], 1), BS, 1)[:, :BAND]


def padded(x):
    return jnp.concatenate([x, jnp.zeros((BS, BS), F32)], 1)


def edge_kernel(a_idx, p_idx, a_ref, p_high, p_low, inter, intra, part7, h7, pt7, p0, table, p7):
    first = ROWS - 2 * RATIO
    zero = jnp.zeros((BS, HALF), BF16)
    for i in range(RATIO):
        here, _ = pair(p_idx, first + i, p_high[i])
        table[i] = jnp.concatenate([here, zero], 1)
    for i in range(RATIO):
        here, there = pair(p_idx, first + RATIO + i, p_high[RATIO + i])
        table[RATIO + i] = centred(there)
        p7[i * BS : (i + 1) * BS] = here
    table[2 * RATIO] = jnp.zeros((BS, WIDE), BF16)
    for i in range(RATIO):
        here, _ = pair(p_idx, i, p_low[i])
        p0[i * BS : (i + 1) * BS] = here
    for i in range(RATIO):
        row = ROWS - RATIO + i
        places = [column(a_idx, k, row) - RATIO - first for k in range(KA)]
        weights = jnp.concatenate([table[jnp.minimum(place, 2 * RATIO)] for place in places], 0)
        part7[i * BS : (i + 1) * BS] = dot(a_ref[i], weights)
        h7[i * BS : (i + 1) * BS] = spread(a_ref[i], [place - 2 * RATIO for place in places])
    turned = p7[...].T
    pt7[...] = turned
    after = turned[BS:]
    spill = dot(after, part7[...].astype(BF16)).astype(BF16)
    factor = dot(after, h7[...]).astype(BF16)
    core = lax.axis_index("col") & 1
    for mine, (down, up) in enumerate(((inter, intra), (intra, inter))):

        @pl.when(core == mine)
        def _(down=down, up=up):
            down[0 : 4 * BS] = p0[...]
            down[4 * BS :] = jnp.zeros((4 * BS, HALF), BF16)
            up[0 : 4 * BS] = p7[...]
            up[4 * BS : 5 * BS] = spill[:, :HALF]
            up[5 * BS : 6 * BS] = spill[:, HALF:]
            up[6 * BS : 7 * BS] = factor[:, :HALF]
            up[7 * BS :] = factor[:, HALF:]


def edge(a_blocks, a_idx, p_blocks, p_idx):
    out = lambda shape, dtype: pltpu.VMEM(shape, dtype)
    return pl.pallas_call(
        edge_kernel,
        grid=(1,),
        in_specs=[
            SMEM,
            SMEM,
            pl.BlockSpec((RATIO, BS, KA * BS), lambda i: (GROUPS - 1, 0, 0)),
            pl.BlockSpec((2 * RATIO, BS, HALF), lambda i: (GROUPS // 2 - 1, 0, 0)),
            pl.BlockSpec((RATIO, BS, HALF), lambda i: (0, 0, 0)),
        ],
        out_specs=[VMEM] * 6,
        out_shape=[
            out((8 * BS, HALF), BF16),
            out((8 * BS, HALF), BF16),
            out((4 * BS, WIDE), F32),
            out((4 * BS, WIDE), BF16),
            out((HALF, 4 * BS), BF16),
            out((4 * BS, HALF), BF16),
        ],
        scratch_shapes=[pltpu.VMEM((2 * RATIO + 1, BS, WIDE), BF16), pltpu.VMEM((4 * BS, HALF), BF16)],
        compiler_params=pltpu.CompilerParams(vmem_limit_bytes=16 << 20),
        cost_estimate=pl.CostEstimate(flops=1 << 28, bytes_accessed=1 << 20, transcendentals=0),
        name="edge",
    )(a_idx, p_idx, a_blocks, p_blocks, p_blocks)


def inner_kernel(a_idx, p_idx, p_ref, a_hbm, out_hbm, part0, h0, pt0, row1, row7, table, pairs, a_ref, rows, a_sem, out_sem):
    a_copies = [
        pltpu.make_async_copy(
            a_hbm.at[pl.ds(g * RATIO, RATIO)], a_ref.at[pl.ds(g * RATIO, RATIO)], a_sem.at[g]
        )
        for g in range(GROUPS - 1)
    ]
    for copy in a_copies:
        copy.start()
    zero = jnp.zeros((BS, HALF), BF16)
    table[3 * ROWS] = jnp.zeros((BS, WIDE), BF16)

    @pl.loop(0, GROUPS)
    def _(g):
        for i in range(RATIO):
            row = g * RATIO + i
            here, there = pair(p_idx, row, p_ref[row])
            table[row] = jnp.concatenate([here, zero], 1)
            table[ROWS + row] = centred(there)
            table[2 * ROWS + row] = jnp.concatenate([zero, here], 1)
            pairs[g, i * BS : (i + 1) * BS] = here

    def product(g, i):
        row = g * RATIO + i
        blocks = []
        for k in range(KA):
            at = column(a_idx, k, row)
            place = (at // RATIO - g) * ROWS + at - RATIO
            if g == 0:
                place = jnp.where(at < RATIO, 3 * ROWS, place)
            blocks.append(table[place])
        return dot(a_ref[row], jnp.concatenate(blocks, 0))

    a_copies[0].wait()
    for i in range(RATIO):
        part0[i * BS : (i + 1) * BS] = product(0, i)
        places = [column(a_idx, k, i) for k in range(KA)]
        h0[i * BS : (i + 1) * BS] = spread(a_ref[i], places)
    pt0[...] = pairs[0].T
    before = None
    out_copies = []
    for g in range(1, GROUPS - 1):
        a_copies[g].wait()
        both = dot_rows(pairs[g], jnp.concatenate([product(g, i).astype(BF16) for i in range(RATIO)], 0))
        row = shifted(both[:BS])
        if g == 1:
            row1[...] = row
        else:
            rows[g - 2] = row + padded(before)
            copy = pltpu.make_async_copy(rows.at[g - 2], out_hbm.at[g], out_sem.at[g - 2])
            copy.start()
            out_copies.append(copy)
        before = both[BS:]
    row7[...] = padded(before)
    for copy in out_copies:
        copy.wait()


def inner(a_blocks, a_idx, p_blocks, p_idx):
    out = lambda shape, dtype: pltpu.VMEM(shape, dtype)
    return pl.pallas_call(
        inner_kernel,
        in_specs=[SMEM, SMEM, VMEM, ANY],
        out_specs=[ANY] + [VMEM] * 5,
        out_shape=[
            jax.ShapeDtypeStruct((GROUPS, BS, BAND), F32),
            out((4 * BS, WIDE), F32),
            out((4 * BS, WIDE), BF16),
            out((HALF, 4 * BS), BF16),
            out((BS, BAND), F32),
            out((BS, BAND), F32),
        ],
        scratch_shapes=[
            pltpu.VMEM((3 * ROWS + 1, BS, WIDE), BF16),
            pltpu.VMEM((GROUPS, 4 * BS, HALF), BF16),
            pltpu.VMEM((ROWS, BS, KA * BS), BF16),
            pltpu.VMEM((GROUPS - 3, BS, BAND), F32),
            pltpu.SemaphoreType.DMA((GROUPS - 1,)),
            pltpu.SemaphoreType.DMA((GROUPS - 3,)),
        ],
        compiler_params=pltpu.CompilerParams(vmem_limit_bytes=24 << 20),
        cost_estimate=pl.CostEstimate(flops=1 << 30, bytes_accessed=1 << 22, transcendentals=0),
        name="inner",
    )(a_idx, p_idx, p_blocks, a_blocks)


def last_kernel(inter, intra, part7, h7, pt7, p0, part0, h0, pt0, row1, row7, out_in, out_hbm, rows, sem):
    core = lax.axis_index("col") & 1
    from_before = jnp.where(core == 0, inter[...], intra[...])
    from_after = jnp.where(core == 0, intra[...], inter[...])
    edge0 = part0[:, :HALF] + dot(h0[...], from_before[: 4 * BS])
    product0 = jnp.concatenate([edge0.astype(BF16), part0[:, HALF:].astype(BF16)], 1)
    edge7 = part7[:, HALF:] + dot(h7[...], from_after[: 4 * BS])
    product7 = jnp.concatenate([part7[:, :HALF].astype(BF16), edge7.astype(BF16)], 1)
    both0 = dot(pt0[...], product0)
    lower7 = dot(pt7[:BS], product7)
    factor = jnp.concatenate([from_before[6 * BS : 7 * BS], from_before[7 * BS :]], 1)
    spill0 = from_before[4 * BS : 5 * BS].astype(F32)
    spill1 = from_before[5 * BS : 6 * BS].astype(F32) + dot(factor, p0[...])
    rows[0] = shifted(both0[:BS]) + padded(jnp.concatenate([spill0, spill1], 1))
    rows[1] = row1[...] + padded(both0[BS:])
    rows[2] = row7[...] + shifted(lower7)
    copies = [
        pltpu.make_async_copy(rows.at[pl.ds(0, 2)], out_hbm.at[pl.ds(0, 2)], sem.at[0]),
        pltpu.make_async_copy(rows.at[2], out_hbm.at[GROUPS - 1], sem.at[1]),
    ]
    for copy in copies:
        copy.start()
    for copy in copies:
        copy.wait()


def last(*args):
    return pl.pallas_call(
        last_kernel,
        in_specs=[VMEM] * 11 + [ANY],
        out_specs=ANY,
        out_shape=jax.ShapeDtypeStruct((GROUPS, BS, BAND), F32),
        input_output_aliases={11: 0},
        scratch_shapes=[pltpu.VMEM((3, BS, BAND), F32), pltpu.SemaphoreType.DMA((2,))],
        compiler_params=pltpu.CompilerParams(vmem_limit_bytes=16 << 20),
        cost_estimate=pl.CostEstimate(flops=1 << 26, bytes_accessed=1 << 19, transcendentals=0),
        name="last",
    )(*args)


def shards(a_blocks, a_index, p_blocks, p_index):
    a_idx, p_idx = a_index.T, p_index.T
    devices = lax.axis_size(("row", "col"))
    inter, intra, *ends = edge(a_blocks, a_idx, p_blocks, p_idx)
    across = [(d, (d + 1 if d % 2 else d - 1) % devices) for d in range(devices)]
    within = [(d, d ^ 1) for d in range(devices)]
    inter = lax.ppermute(inter, ("row", "col"), across)
    intra = lax.ppermute(intra, ("row", "col"), within)
    out, *starts = inner(a_blocks, a_idx, p_blocks, p_idx)
    return last(inter, intra, *ends, *starts, out)


def solution(mesh):
    blocks = P(("row", "col"), None, None)
    index = P(("row", "col"), None)
    return jax.shard_map(
        shards, mesh=mesh, in_specs=(blocks, index, blocks, index), out_specs=blocks, check_vma=False
    )
```

```python
import jax
import jax.numpy as jnp
from jax import lax
from jax.experimental import pallas as pl
from jax.experimental.pallas import tpu as pltpu
from jax.sharding import PartitionSpec as P

BS = 64
KA = 8
RATIO = 4
GROUPS = 8
ROWS = RATIO * GROUPS
HALF = 2 * BS
WIDE = 4 * BS
BAND = 5 * BS
F32, BF16 = jnp.float32, jnp.bfloat16
SMEM = pl.BlockSpec(memory_space=pltpu.SMEM)
VMEM = pl.BlockSpec(memory_space=pltpu.VMEM)
ANY = pl.BlockSpec(memory_space=pl.ANY)


def low_half(rows):
    return lax.broadcasted_iota(jnp.int32, (rows, HALF), 1) < BS


def dot(x, y):
    return jnp.dot(x, y, preferred_element_type=F32)


def dot_rows(x, y):
    return lax.dot_general(x, y, (((0,), (0,)), ((), ())), preferred_element_type=F32)


def pair(p_idx, row, block):
    first = ((p_idx[0, row] - row // RATIO) & 1).astype(F32)
    second = ((p_idx[1, row] - row // RATIO) & 1).astype(F32)
    low = low_half(BS)
    x = block.astype(F32)
    y = pltpu.roll(x, BS, 1)
    here = x * jnp.where(low, 1.0 - first, second) + y * jnp.where(low, 1.0 - second, first)
    there = y * jnp.where(low, second, 1.0 - first) + x * jnp.where(low, first, 1.0 - second)
    return here.astype(BF16), there


def centred(there):
    low = low_half(BS)
    zero = jnp.zeros_like(there)
    return jnp.concatenate([jnp.where(low, zero, there), jnp.where(low, there, zero)], 1).astype(BF16)


def column(a_idx, k, row):
    return row + ((a_idx[k, row] - row + RATIO) & 15)


def spread(a_row, places):
    low = low_half(BS)
    tiles = [jnp.zeros((BS, HALF), F32)] * 2
    for j in range(KA // 2):
        x = a_row[:, j * HALF : (j + 1) * HALF].astype(F32)
        y = pltpu.roll(x, BS, 1)
        for blocks, at in ((x, (2 * j, 2 * j + 1)), (y, (2 * j + 1, 2 * j))):
            place = jnp.where(low, places[at[0]], places[at[1]])
            for t in range(2):
                wanted = jnp.where(low, 2 * t, 2 * t + 1)
                tiles[t] = tiles[t] + jnp.where(place == wanted, blocks, 0.0)
    return jnp.concatenate(tiles, 1).astype(BF16)


def shifted(x):
    return pltpu.roll(jnp.concatenate([x, jnp.zeros((BS, HALF), F32)], 1), BS, 1)[:, :BAND]


def padded(x):
    return jnp.concatenate([x, jnp.zeros((BS, BS), F32)], 1)


def edge_body(a_idx, p_idx, a_ref, p_ref, intra, inter, final, part7, h7, pt7, p0, table, p7):
    first = ROWS - 2 * RATIO
    zero = jnp.zeros((BS, HALF), BF16)
    for i in range(RATIO):
        here, _ = pair(p_idx, first + i, p_ref[first + i])
        table[i] = jnp.concatenate([here, zero], 1)
    for i in range(RATIO):
        here, there = pair(p_idx, first + RATIO + i, p_ref[first + RATIO + i])
        table[RATIO + i] = centred(there)
        p7[i * BS : (i + 1) * BS] = here
    table[2 * RATIO] = jnp.zeros((BS, WIDE), BF16)
    for i in range(RATIO):
        here, _ = pair(p_idx, i, p_ref[i])
        p0[i * BS : (i + 1) * BS] = here
    for i in range(RATIO):
        row = ROWS - RATIO + i
        places = [column(a_idx, k, row) - RATIO - first for k in range(KA)]
        weights = jnp.concatenate([table[jnp.minimum(place, 2 * RATIO)] for place in places], 0)
        part7[i * BS : (i + 1) * BS] = dot(a_ref[row], weights)
        h7[i * BS : (i + 1) * BS] = spread(a_ref[row], [place - 2 * RATIO for place in places])
    turned = p7[...].T
    pt7[...] = turned
    after = turned[BS:]
    spill = dot(after, part7[...].astype(BF16)).astype(BF16)
    factor = dot(after, h7[...]).astype(BF16)
    at = lax.axis_index("col")
    late = at >= lax.axis_size("col") - 2
    for core, last, down, up in (
        (0, False, inter, intra),
        (1, False, intra, inter),
        (0, True, inter, final),
        (1, True, final, inter),
    ):

        @pl.when(jnp.logical_and(at & 1 == core, late == last))
        def _(down=down, up=up):
            down[0 : 4 * BS] = p0[...]
            down[4 * BS :] = jnp.zeros((4 * BS, HALF), BF16)
            up[0 : 4 * BS] = p7[...]
            up[4 * BS : 5 * BS] = spill[:, :HALF]
            up[5 * BS : 6 * BS] = spill[:, HALF:]
            up[6 * BS : 7 * BS] = factor[:, :HALF]
            up[7 * BS :] = factor[:, HALF:]


def inner_body(a_idx, p_idx, a_ref, p_ref, wait_rows, out_hbm, part0, h0, pt0, row1, row7, table, pairs, rows, out_sem):
    zero = jnp.zeros((BS, HALF), BF16)
    table[3 * ROWS] = jnp.zeros((BS, WIDE), BF16)

    @pl.loop(0, GROUPS)
    def _(g):
        for i in range(RATIO):
            row = g * RATIO + i
            here, there = pair(p_idx, row, p_ref[row])
            table[row] = jnp.concatenate([here, zero], 1)
            table[ROWS + row] = centred(there)
            table[2 * ROWS + row] = jnp.concatenate([zero, here], 1)
            pairs[g, i * BS : (i + 1) * BS] = here

    def product(g, i):
        row = g * RATIO + i
        blocks = []
        for k in range(KA):
            at = column(a_idx, k, row)
            place = (at // RATIO - g) * ROWS + at - RATIO
            if g == 0:
                place = jnp.where(at < RATIO, 3 * ROWS, place)
            blocks.append(table[place])
        return dot(a_ref[row], jnp.concatenate(blocks, 0))

    wait_rows()
    for i in range(RATIO):
        part0[i * BS : (i + 1) * BS] = product(0, i)
        places = [column(a_idx, k, i) for k in range(KA)]
        h0[i * BS : (i + 1) * BS] = spread(a_ref[i], places)
    pt0[...] = pairs[0].T
    before = None
    out_copies = []
    for g in range(1, GROUPS - 1):
        both = dot_rows(pairs[g], jnp.concatenate([product(g, i).astype(BF16) for i in range(RATIO)], 0))
        row = shifted(both[:BS])
        if g == 1:
            row1[...] = row
        else:
            rows[g - 2] = row + padded(before)
            copy = pltpu.make_async_copy(rows.at[g - 2], out_hbm.at[g], out_sem.at[g - 2])
            copy.start()
            out_copies.append(copy)
        before = both[BS:]
    row7[...] = padded(before)
    for copy in out_copies:
        copy.wait()


def early():
    return lax.axis_index("col") < 2


INNER_SCRATCH = [
    pltpu.SMEM((KA, ROWS), jnp.int32),
    pltpu.SMEM((2, ROWS), jnp.int32),
    pltpu.VMEM((ROWS, BS, KA * BS), BF16),
    pltpu.VMEM((ROWS, BS, HALF), BF16),
    pltpu.VMEM((3 * ROWS + 1, BS, WIDE), BF16),
    pltpu.VMEM((GROUPS, 4 * BS, HALF), BF16),
    pltpu.VMEM((GROUPS - 3, BS, BAND), F32),
    pltpu.SemaphoreType.DMA((8,)),
    pltpu.SemaphoreType.DMA((GROUPS - 3,)),
]
vmem = lambda *shape: pltpu.VMEM(shape[:-1], shape[-1])
INNER_SHAPES = [
    jax.ShapeDtypeStruct((GROUPS, BS, BAND), F32),
    vmem(4 * BS, WIDE, F32),
    vmem(4 * BS, WIDE, BF16),
    vmem(HALF, 4 * BS, BF16),
    vmem(BS, BAND, F32),
    vmem(BS, BAND, F32),
]
EDGE_SHAPES = [
    vmem(8 * BS, HALF, BF16),
    vmem(8 * BS, HALF, BF16),
    vmem(8 * BS, HALF, BF16),
    vmem(4 * BS, WIDE, F32),
    vmem(4 * BS, WIDE, BF16),
    vmem(HALF, 4 * BS, BF16),
    vmem(4 * BS, HALF, BF16),
]


def edge_kernel(a_idx_hbm, p_idx_hbm, a_hbm, p_hbm, *refs):
    edge_out, inner_out = refs[:7], refs[7:13]
    a_idx, p_idx, a_ref, p_ref, table, pairs, rows, sem, out_sem, edge_table, p7 = refs[13:]

    def part(source, to, at, size, n):
        return pltpu.make_async_copy(source.at[pl.ds(at, size)], to.at[pl.ds(at, size)], sem.at[n])

    index = [pltpu.make_async_copy(a_idx_hbm, a_idx, sem.at[0]), pltpu.make_async_copy(p_idx_hbm, p_idx, sem.at[1])]
    ends = [part(p_hbm, p_ref, ROWS - 8, 8, 2), part(p_hbm, p_ref, 0, 4, 3), part(a_hbm, a_ref, ROWS - 4, 4, 4)]
    rest = [part(p_hbm, p_ref, 4, ROWS - 12, 5), part(a_hbm, a_ref, 0, ROWS - 4, 6)]
    for copy in index + ends:
        copy.start()

    @pl.when(early())
    def _():
        for copy in rest:
            copy.start()

    for copy in index + ends:
        copy.wait()
    edge_body(a_idx, p_idx, a_ref, p_ref, *edge_out, edge_table, p7)

    @pl.when(early())
    def _():
        rest[0].wait()
        inner_body(a_idx, p_idx, a_ref, p_ref, rest[1].wait, *inner_out, table, pairs, rows, out_sem)


def edge(a_blocks, a_idx, p_blocks, p_idx):
    return pl.pallas_call(
        edge_kernel,
        in_specs=[ANY] * 4,
        out_specs=[VMEM] * 7 + [ANY] + [VMEM] * 5,
        out_shape=EDGE_SHAPES + INNER_SHAPES,
        scratch_shapes=INNER_SCRATCH + [pltpu.VMEM((2 * RATIO + 1, BS, WIDE), BF16), pltpu.VMEM((4 * BS, HALF), BF16)],
        compiler_params=pltpu.CompilerParams(vmem_limit_bytes=24 << 20),
        cost_estimate=pl.CostEstimate(flops=1 << 28, bytes_accessed=1 << 20, transcendentals=0),
        name="edge",
    )(a_idx, p_idx, a_blocks, p_blocks)


def inner_kernel(a_idx_hbm, p_idx_hbm, a_hbm, p_hbm, *refs):
    inner_out = refs[1:7]
    a_idx, p_idx, a_ref, p_ref, table, pairs, rows, sem, out_sem = refs[7:]

    @pl.when(jnp.logical_not(early()))
    def _():
        pieces = [(p_hbm, p_ref), (a_idx_hbm, a_idx), (p_idx_hbm, p_idx), (a_hbm, a_ref)]
        copies = [pltpu.make_async_copy(x, y, sem.at[n]) for n, (x, y) in enumerate(pieces)]
        for copy in copies:
            copy.start()
        for copy in copies[:3]:
            copy.wait()
        inner_body(a_idx, p_idx, a_ref, p_ref, copies[3].wait, *inner_out, table, pairs, rows, out_sem)


def inner(a_blocks, a_idx, p_blocks, p_idx, out):
    return pl.pallas_call(
        inner_kernel,
        in_specs=[ANY] * 5,
        out_specs=[ANY] + [VMEM] * 5,
        out_shape=INNER_SHAPES,
        input_output_aliases={4: 0},
        scratch_shapes=INNER_SCRATCH,
        compiler_params=pltpu.CompilerParams(vmem_limit_bytes=24 << 20),
        cost_estimate=pl.CostEstimate(flops=1 << 30, bytes_accessed=1 << 22, transcendentals=0),
        name="inner",
    )(a_idx, p_idx, a_blocks, p_blocks, out)


def last_kernel(inter, intra, final, part7, h7, pt7, p0, *refs):
    starts, late_starts, (_, out_hbm, rows, sem) = refs[:5], refs[5:10], refs[10:]
    at = lax.axis_index("col")
    core = at & 1
    beside = jnp.where(at < lax.axis_size("col") - 2, intra[...], final[...])
    from_before = jnp.where(core == 0, inter[...], beside)
    from_after = jnp.where(core == 0, beside, inter[...])

    def finish(part0, h0, pt0, row1, row7):
        edge0 = part0[:, :HALF] + dot(h0[...], from_before[: 4 * BS])
        product0 = jnp.concatenate([edge0.astype(BF16), part0[:, HALF:].astype(BF16)], 1)
        edge7 = part7[:, HALF:] + dot(h7[...], from_after[: 4 * BS])
        product7 = jnp.concatenate([part7[:, :HALF].astype(BF16), edge7.astype(BF16)], 1)
        both0 = dot(pt0[...], product0)
        lower7 = dot(pt7[:BS], product7)
        factor = jnp.concatenate([from_before[6 * BS : 7 * BS], from_before[7 * BS :]], 1)
        spill0 = from_before[4 * BS : 5 * BS].astype(F32)
        spill1 = from_before[5 * BS : 6 * BS].astype(F32) + dot(factor, p0[...])
        rows[0] = shifted(both0[:BS]) + padded(jnp.concatenate([spill0, spill1], 1))
        rows[1] = row1[...] + padded(both0[BS:])
        rows[2] = row7[...] + shifted(lower7)

    @pl.when(early())
    def _():
        finish(*starts)

    @pl.when(jnp.logical_not(early()))
    def _():
        finish(*late_starts)

    copies = [
        pltpu.make_async_copy(rows.at[pl.ds(0, 2)], out_hbm.at[pl.ds(0, 2)], sem.at[0]),
        pltpu.make_async_copy(rows.at[2], out_hbm.at[GROUPS - 1], sem.at[1]),
    ]
    for copy in copies:
        copy.start()
    for copy in copies:
        copy.wait()


def last(*args):
    return pl.pallas_call(
        last_kernel,
        in_specs=[VMEM] * 17 + [ANY],
        out_specs=ANY,
        out_shape=jax.ShapeDtypeStruct((GROUPS, BS, BAND), F32),
        input_output_aliases={17: 0},
        scratch_shapes=[pltpu.VMEM((3, BS, BAND), F32), pltpu.SemaphoreType.DMA((2,))],
        compiler_params=pltpu.CompilerParams(vmem_limit_bytes=16 << 20),
        cost_estimate=pl.CostEstimate(flops=1 << 26, bytes_accessed=1 << 19, transcendentals=0),
        name="last",
    )(*args)


def shards(a_blocks, a_index, p_blocks, p_index):
    hbm = lambda x: pltpu.with_memory_space_constraint(x, pltpu.HBM)
    operands = hbm(a_blocks), hbm(a_index.T), hbm(p_blocks), hbm(p_index.T)
    axes = ("row", "col")
    devices, line = lax.axis_size(axes), lax.axis_size("col")
    intra, inter, final, part7, h7, pt7, p0, out, *starts = edge(*operands)
    within = [(d, d ^ 1) for d in range(devices)]
    most = [(s, t) for s, t in within if s % line < line - 2]
    others = [(s, t) for s, t in within if s % line >= line - 2]
    across = [(d, (d + 1 if d % 2 else d - 1) % devices) for d in range(devices)]
    from_most = lax.ppermute(intra, axes, most)
    from_across = lax.ppermute(inter, axes, across)
    from_final = lax.ppermute(final, axes, others)
    out, *late_starts = inner(*operands, out)
    return last(from_across, from_most, from_final, part7, h7, pt7, p0, *starts, *late_starts, out)


def solution(mesh):
    blocks = P(("row", "col"), None, None)
    index = P(("row", "col"), None)
    return jax.shard_map(
        shards, mesh=mesh, in_specs=(blocks, index, blocks, index), out_specs=blocks, check_vma=False
    )
```

```python
import functools

import jax
import jax.numpy as jnp
from jax import lax
from jax.experimental import pallas as pl
from jax.experimental.pallas import tpu as pltpu
from jax.sharding import PartitionSpec as P

BS = 64
KA = 8
RATIO = 4
GROUPS = 8
ROWS = RATIO * GROUPS
HALF = 2 * BS
WIDE = 4 * BS
BAND = 5 * BS
F32, BF16 = jnp.float32, jnp.bfloat16
SMEM = pl.BlockSpec(memory_space=pltpu.SMEM)
VMEM = pl.BlockSpec(memory_space=pltpu.VMEM)
ANY = pl.BlockSpec(memory_space=pl.ANY)


def low_half(rows):
    return lax.broadcasted_iota(jnp.int32, (rows, HALF), 1) < BS


def dot(x, y):
    return jnp.dot(x, y, preferred_element_type=F32)


def dot_rows(x, y):
    return lax.dot_general(x, y, (((0,), (0,)), ((), ())), preferred_element_type=F32)


def pair(p_idx, row, block):
    first = ((p_idx[0, row] - row // RATIO) & 1).astype(F32)
    second = ((p_idx[1, row] - row // RATIO) & 1).astype(F32)
    low = low_half(BS)
    x = block.astype(F32)
    y = pltpu.roll(x, BS, 1)
    here = x * jnp.where(low, 1.0 - first, second) + y * jnp.where(low, 1.0 - second, first)
    there = y * jnp.where(low, second, 1.0 - first) + x * jnp.where(low, first, 1.0 - second)
    return here.astype(BF16), there


def centred(there):
    low = low_half(BS)
    zero = jnp.zeros_like(there)
    return jnp.concatenate([jnp.where(low, zero, there), jnp.where(low, there, zero)], 1).astype(BF16)


def column(a_idx, k, row):
    return row + ((a_idx[k, row] - row + RATIO) & 15)


def spread(a_row, places):
    low = low_half(BS)
    tiles = [jnp.zeros((BS, HALF), F32)] * 2
    for j in range(KA // 2):
        x = a_row[:, j * HALF : (j + 1) * HALF].astype(F32)
        y = pltpu.roll(x, BS, 1)
        for blocks, at in ((x, (2 * j, 2 * j + 1)), (y, (2 * j + 1, 2 * j))):
            place = jnp.where(low, places[at[0]], places[at[1]])
            for t in range(2):
                wanted = jnp.where(low, 2 * t, 2 * t + 1)
                tiles[t] = tiles[t] + jnp.where(place == wanted, blocks, 0.0)
    return jnp.concatenate(tiles, 1).astype(BF16)


def shifted(x):
    return pltpu.roll(jnp.concatenate([x, jnp.zeros((BS, HALF), F32)], 1), BS, 1)[:, :BAND]


def padded(x):
    return jnp.concatenate([x, jnp.zeros((BS, BS), F32)], 1)


def edge_body(a_idx, p_idx, a_ref, p_ref, intra, inter, final, part7, h7, pt7, p0, table, p7):
    first = ROWS - 2 * RATIO
    zero = jnp.zeros((BS, HALF), BF16)
    for i in range(RATIO):
        here, _ = pair(p_idx, first + i, p_ref[first + i])
        table[i] = jnp.concatenate([here, zero], 1)
    for i in range(RATIO):
        here, there = pair(p_idx, first + RATIO + i, p_ref[first + RATIO + i])
        table[RATIO + i] = centred(there)
        p7[i * BS : (i + 1) * BS] = here
    table[2 * RATIO] = jnp.zeros((BS, WIDE), BF16)
    for i in range(RATIO):
        here, _ = pair(p_idx, i, p_ref[i])
        p0[i * BS : (i + 1) * BS] = here
    for i in range(RATIO):
        row = ROWS - RATIO + i
        places = [column(a_idx, k, row) - RATIO - first for k in range(KA)]
        weights = jnp.concatenate([table[jnp.minimum(place, 2 * RATIO)] for place in places], 0)
        part7[i * BS : (i + 1) * BS] = dot(a_ref[row], weights)
        h7[i * BS : (i + 1) * BS] = spread(a_ref[row], [place - 2 * RATIO for place in places])
    turned = p7[...].T
    pt7[...] = turned
    after = turned[BS:]
    spill = dot(after, part7[...].astype(BF16)).astype(BF16)
    factor = dot(after, h7[...]).astype(BF16)
    at = lax.axis_index("col")
    late = at >= lax.axis_size("col") - 2
    for core, last, down, up in (
        (0, False, inter, intra),
        (1, False, intra, inter),
        (0, True, inter, final),
        (1, True, final, inter),
    ):

        @pl.when(jnp.logical_and(at & 1 == core, late == last))
        def _(down=down, up=up):
            down[0 : 4 * BS] = p0[...]
            down[4 * BS :] = jnp.zeros((4 * BS, HALF), BF16)
            up[0 : 4 * BS] = p7[...]
            up[4 * BS : 5 * BS] = spill[:, :HALF]
            up[5 * BS : 6 * BS] = spill[:, HALF:]
            up[6 * BS : 7 * BS] = factor[:, :HALF]
            up[7 * BS :] = factor[:, HALF:]


def inner_body(a_idx, p_idx, a_ref, p_ref, wait_rows, out_hbm, part0, h0, pt0, row1, row7, table, pairs, rows, out_sem):
    zero = jnp.zeros((BS, HALF), BF16)
    table[3 * ROWS] = jnp.zeros((BS, WIDE), BF16)

    @pl.loop(0, GROUPS)
    def _(g):
        for i in range(RATIO):
            row = g * RATIO + i
            here, there = pair(p_idx, row, p_ref[row])
            table[row] = jnp.concatenate([here, zero], 1)
            table[ROWS + row] = centred(there)
            table[2 * ROWS + row] = jnp.concatenate([zero, here], 1)
            pairs[g, i * BS : (i + 1) * BS] = here

    def product(g, i):
        row = g * RATIO + i
        blocks = []
        for k in range(KA):
            at = column(a_idx, k, row)
            place = (at // RATIO - g) * ROWS + at - RATIO
            if g == 0:
                place = jnp.where(at < RATIO, 3 * ROWS, place)
            blocks.append(table[place])
        return dot(a_ref[row], jnp.concatenate(blocks, 0))

    wait_rows()
    for i in range(RATIO):
        part0[i * BS : (i + 1) * BS] = product(0, i)
        places = [column(a_idx, k, i) for k in range(KA)]
        h0[i * BS : (i + 1) * BS] = spread(a_ref[i], places)
    pt0[...] = pairs[0].T
    before = None
    out_copies = []
    for g in range(1, GROUPS - 1):
        both = dot_rows(pairs[g], jnp.concatenate([product(g, i).astype(BF16) for i in range(RATIO)], 0))
        row = shifted(both[:BS])
        if g == 1:
            row1[...] = row
        else:
            rows[g - 2] = row + padded(before)
            copy = pltpu.make_async_copy(rows.at[g - 2], out_hbm.at[g], out_sem.at[g - 2])
            copy.start()
            out_copies.append(copy)
        before = both[BS:]
    row7[...] = padded(before)
    for copy in out_copies:
        copy.wait()


def turn():
    at = lax.axis_index("col")
    return jnp.where(at == 0, 1, jnp.where(at == 1, 0, 2))


INNER_SCRATCH = [
    pltpu.SMEM((KA, ROWS), jnp.int32),
    pltpu.SMEM((2, ROWS), jnp.int32),
    pltpu.VMEM((ROWS, BS, KA * BS), BF16),
    pltpu.VMEM((ROWS, BS, HALF), BF16),
    pltpu.VMEM((3 * ROWS + 1, BS, WIDE), BF16),
    pltpu.VMEM((GROUPS, 4 * BS, HALF), BF16),
    pltpu.VMEM((GROUPS - 3, BS, BAND), F32),
    pltpu.SemaphoreType.DMA((8,)),
    pltpu.SemaphoreType.DMA((GROUPS - 3,)),
]
vmem = lambda *shape: pltpu.VMEM(shape[:-1], shape[-1])
INNER_SHAPES = [
    jax.ShapeDtypeStruct((GROUPS, BS, BAND), F32),
    vmem(4 * BS, WIDE, F32),
    vmem(4 * BS, WIDE, BF16),
    vmem(HALF, 4 * BS, BF16),
    vmem(BS, BAND, F32),
    vmem(BS, BAND, F32),
]
EDGE_SHAPES = [
    vmem(8 * BS, HALF, BF16),
    vmem(8 * BS, HALF, BF16),
    vmem(8 * BS, HALF, BF16),
    vmem(4 * BS, WIDE, F32),
    vmem(4 * BS, WIDE, BF16),
    vmem(HALF, 4 * BS, BF16),
    vmem(4 * BS, HALF, BF16),
]


def edge_kernel(a_idx_hbm, p_idx_hbm, a_hbm, p_hbm, *refs):
    edge_out, inner_out = refs[:7], refs[7:13]
    a_idx, p_idx, a_ref, p_ref, table, pairs, rows, sem, out_sem, edge_table, p7 = refs[13:]

    def part(source, to, at, size, n):
        return pltpu.make_async_copy(source.at[pl.ds(at, size)], to.at[pl.ds(at, size)], sem.at[n])

    index = [pltpu.make_async_copy(a_idx_hbm, a_idx, sem.at[0]), pltpu.make_async_copy(p_idx_hbm, p_idx, sem.at[1])]
    ends = [part(p_hbm, p_ref, ROWS - 8, 8, 2), part(p_hbm, p_ref, 0, 4, 3), part(a_hbm, a_ref, ROWS - 4, 4, 4)]
    rest = [part(p_hbm, p_ref, 4, ROWS - 12, 5), part(a_hbm, a_ref, 0, ROWS - 4, 6)]
    for copy in index + ends:
        copy.start()

    @pl.when(turn() == 0)
    def _():
        for copy in rest:
            copy.start()

    for copy in index + ends:
        copy.wait()
    edge_body(a_idx, p_idx, a_ref, p_ref, *edge_out, edge_table, p7)

    @pl.when(turn() == 0)
    def _():
        rest[0].wait()
        inner_body(a_idx, p_idx, a_ref, p_ref, rest[1].wait, *inner_out, table, pairs, rows, out_sem)


def edge(*operands):
    return pl.pallas_call(
        edge_kernel,
        in_specs=[ANY] * 4,
        out_specs=[VMEM] * 7 + [ANY] + [VMEM] * 5,
        out_shape=EDGE_SHAPES + INNER_SHAPES,
        scratch_shapes=INNER_SCRATCH + [pltpu.VMEM((2 * RATIO + 1, BS, WIDE), BF16), pltpu.VMEM((4 * BS, HALF), BF16)],
        compiler_params=pltpu.CompilerParams(vmem_limit_bytes=24 << 20),
        cost_estimate=pl.CostEstimate(flops=1 << 28, bytes_accessed=1 << 20, transcendentals=0),
        name="edge",
    )(*operands)


def inner_kernel(mine, a_idx_hbm, p_idx_hbm, a_hbm, p_hbm, *refs):
    kept = 5 - 2 * mine
    inner_out = refs[kept : kept + 6]
    a_idx, p_idx, a_ref, p_ref, table, pairs, rows, sem, out_sem = refs[2 * kept + 5 :]

    @pl.when(turn() == mine)
    def _():
        pieces = [(p_hbm, p_ref), (a_idx_hbm, a_idx), (p_idx_hbm, p_idx), (a_hbm, a_ref)]
        copies = [pltpu.make_async_copy(x, y, sem.at[n]) for n, (x, y) in enumerate(pieces)]
        for copy in copies:
            copy.start()
        for copy in copies[:3]:
            copy.wait()
        inner_body(a_idx, p_idx, a_ref, p_ref, copies[3].wait, *inner_out, table, pairs, rows, out_sem)


def inner(mine, operands, *kept):
    passed = [jax.ShapeDtypeStruct(kept[0].shape, kept[0].dtype)] + [vmem(*x.shape, x.dtype) for x in kept[1:]]
    return pl.pallas_call(
        functools.partial(inner_kernel, mine),
        in_specs=[ANY] * 5 + [VMEM] * (len(kept) - 1),
        out_specs=[ANY] + [VMEM] * 5 + [ANY] * (len(kept) - 1),
        out_shape=INNER_SHAPES + passed[1:],
        input_output_aliases={4: 0} | {4 + i: 5 + i for i in range(1, len(kept))},
        scratch_shapes=INNER_SCRATCH,
        compiler_params=pltpu.CompilerParams(vmem_limit_bytes=24 << 20),
        cost_estimate=pl.CostEstimate(flops=1 << 30, bytes_accessed=1 << 22, transcendentals=0),
        name="inner",
    )(*operands, *kept)


def last_kernel(inter, intra, final, part7, h7, pt7, p0, *refs):
    starts, (_, out_hbm, rows, sem) = [refs[:5], refs[5:10], refs[10:15]], refs[15:]
    at = lax.axis_index("col")
    core = at & 1
    beside = jnp.where(at < lax.axis_size("col") - 2, intra[...], final[...])
    from_before = jnp.where(core == 0, inter[...], beside)
    from_after = jnp.where(core == 0, beside, inter[...])

    def finish(part0, h0, pt0, row1, row7):
        edge0 = part0[:, :HALF] + dot(h0[...], from_before[: 4 * BS])
        product0 = jnp.concatenate([edge0.astype(BF16), part0[:, HALF:].astype(BF16)], 1)
        edge7 = part7[:, HALF:] + dot(h7[...], from_after[: 4 * BS])
        product7 = jnp.concatenate([part7[:, :HALF].astype(BF16), edge7.astype(BF16)], 1)
        both0 = dot(pt0[...], product0)
        lower7 = dot(pt7[:BS], product7)
        factor = jnp.concatenate([from_before[6 * BS : 7 * BS], from_before[7 * BS :]], 1)
        spill0 = from_before[4 * BS : 5 * BS].astype(F32)
        spill1 = from_before[5 * BS : 6 * BS].astype(F32) + dot(factor, p0[...])
        rows[0] = shifted(both0[:BS]) + padded(jnp.concatenate([spill0, spill1], 1))
        rows[1] = row1[...] + padded(both0[BS:])
        rows[2] = row7[...] + shifted(lower7)

    for mine in range(3):

        @pl.when(turn() == mine)
        def _(mine=mine):
            finish(*starts[mine])

    copies = [
        pltpu.make_async_copy(rows.at[pl.ds(0, 2)], out_hbm.at[pl.ds(0, 2)], sem.at[0]),
        pltpu.make_async_copy(rows.at[2], out_hbm.at[GROUPS - 1], sem.at[1]),
    ]
    for copy in copies:
        copy.start()
    for copy in copies:
        copy.wait()


def last(*args):
    return pl.pallas_call(
        last_kernel,
        in_specs=[VMEM] * 22 + [ANY],
        out_specs=ANY,
        out_shape=jax.ShapeDtypeStruct((GROUPS, BS, BAND), F32),
        input_output_aliases={22: 0},
        scratch_shapes=[pltpu.VMEM((3, BS, BAND), F32), pltpu.SemaphoreType.DMA((2,))],
        compiler_params=pltpu.CompilerParams(vmem_limit_bytes=16 << 20),
        cost_estimate=pl.CostEstimate(flops=1 << 26, bytes_accessed=1 << 19, transcendentals=0),
        name="last",
    )(*args)


def shards(a_blocks, a_index, p_blocks, p_index):
    hbm = lambda x: pltpu.with_memory_space_constraint(x, pltpu.HBM)
    operands = hbm(a_index.T), hbm(p_index.T), hbm(a_blocks), hbm(p_blocks)
    axes = ("row", "col")
    devices, line = lax.axis_size(axes), lax.axis_size("col")
    intra, inter, final, part7, h7, pt7, p0, out, *starts = edge(*operands)
    within = [(d, d ^ 1) for d in range(devices)]
    most = [(s, t) for s, t in within if s % line < line - 2]
    others = [(s, t) for s, t in within if s % line >= line - 2]
    across = [(d, (d + 1 if d % 2 else d - 1) % devices) for d in range(devices)]
    from_most = lax.ppermute(intra, axes, most)
    out, *middle, inter, final = inner(1, operands, out, inter, final)
    from_across = lax.ppermute(inter, axes, across)
    from_final = lax.ppermute(final, axes, others)
    out, *ends = inner(2, operands, out)
    return last(from_across, from_most, from_final, part7, h7, pt7, p0, *starts, *middle, *ends, out)


def solution(mesh):
    blocks = P(("row", "col"), None, None)
    index = P(("row", "col"), None)
    return jax.shard_map(
        shards, mesh=mesh, in_specs=(blocks, index, blocks, index), out_specs=blocks, check_vma=False
    )
```

```python
import functools

import jax
import jax.numpy as jnp
from jax import lax
from jax.experimental import pallas as pl
from jax.experimental.pallas import tpu as pltpu
from jax.sharding import PartitionSpec as P

BS = 64
KA = 8
RATIO = 4
GROUPS = 8
ROWS = RATIO * GROUPS
HALF = 2 * BS
WIDE = 4 * BS
BAND = 5 * BS
F32, BF16 = jnp.float32, jnp.bfloat16
SMEM = pl.BlockSpec(memory_space=pltpu.SMEM)
VMEM = pl.BlockSpec(memory_space=pltpu.VMEM)
ANY = pl.BlockSpec(memory_space=pl.ANY)


def low_half(rows):
    return lax.broadcasted_iota(jnp.int32, (rows, HALF), 1) < BS


def dot(x, y):
    return jnp.dot(x, y, preferred_element_type=F32)


def dot_rows(x, y):
    return lax.dot_general(x, y, (((0,), (0,)), ((), ())), preferred_element_type=F32)


def pair(p_idx, row, block):
    first = ((p_idx[0, row] - row // RATIO) & 1).astype(F32)
    second = ((p_idx[1, row] - row // RATIO) & 1).astype(F32)
    low = low_half(BS)
    x = block.astype(F32)
    y = pltpu.roll(x, BS, 1)
    here = x * jnp.where(low, 1.0 - first, second) + y * jnp.where(low, 1.0 - second, first)
    there = y * jnp.where(low, second, 1.0 - first) + x * jnp.where(low, first, 1.0 - second)
    return here.astype(BF16), there


def centred(there):
    low = low_half(BS)
    zero = jnp.zeros_like(there)
    return jnp.concatenate([jnp.where(low, zero, there), jnp.where(low, there, zero)], 1).astype(BF16)


def column(a_idx, k, row):
    return row + ((a_idx[k, row] - row + RATIO) & 15)


def spread(a_row, places):
    low = low_half(BS)
    tiles = [jnp.zeros((BS, HALF), F32)] * 2
    for j in range(KA // 2):
        x = a_row[:, j * HALF : (j + 1) * HALF].astype(F32)
        y = pltpu.roll(x, BS, 1)
        for blocks, at in ((x, (2 * j, 2 * j + 1)), (y, (2 * j + 1, 2 * j))):
            place = jnp.where(low, places[at[0]], places[at[1]])
            for t in range(2):
                wanted = jnp.where(low, 2 * t, 2 * t + 1)
                tiles[t] = tiles[t] + jnp.where(place == wanted, blocks, 0.0)
    return jnp.concatenate(tiles, 1).astype(BF16)


def shifted(x):
    return pltpu.roll(jnp.concatenate([x, jnp.zeros((BS, HALF), F32)], 1), BS, 1)[:, :BAND]


def padded(x):
    return jnp.concatenate([x, jnp.zeros((BS, BS), F32)], 1)


def edge_body(a_idx, p_idx, a_ref, p_ref, intra, inter, final, part7, h7, pt7, p0, table, p7):
    first = ROWS - 2 * RATIO
    zero = jnp.zeros((BS, HALF), BF16)
    for i in range(RATIO):
        here, _ = pair(p_idx, first + i, p_ref[first + i])
        table[i] = jnp.concatenate([here, zero], 1)
    for i in range(RATIO):
        here, there = pair(p_idx, first + RATIO + i, p_ref[first + RATIO + i])
        table[RATIO + i] = centred(there)
        p7[i * BS : (i + 1) * BS] = here
    table[2 * RATIO] = jnp.zeros((BS, WIDE), BF16)
    for i in range(RATIO):
        here, _ = pair(p_idx, i, p_ref[i])
        p0[i * BS : (i + 1) * BS] = here
    for i in range(RATIO):
        row = ROWS - RATIO + i
        places = [column(a_idx, k, row) - RATIO - first for k in range(KA)]
        weights = jnp.concatenate([table[jnp.minimum(place, 2 * RATIO)] for place in places], 0)
        part7[i * BS : (i + 1) * BS] = dot(a_ref[row], weights)
        h7[i * BS : (i + 1) * BS] = spread(a_ref[row], [place - 2 * RATIO for place in places])
    turned = p7[...].T
    pt7[...] = turned
    after = turned[BS:]
    spill = dot(after, part7[...].astype(BF16)).astype(BF16)
    factor = dot(after, h7[...]).astype(BF16)
    at = lax.axis_index("col")
    late = at >= lax.axis_size("col") - 2
    for core, last, down, up in (
        (0, False, inter, intra),
        (1, False, intra, inter),
        (0, True, inter, final),
        (1, True, final, inter),
    ):

        @pl.when(jnp.logical_and(at & 1 == core, late == last))
        def _(down=down, up=up):
            down[0 : 4 * BS] = p0[...]
            down[4 * BS :] = jnp.zeros((4 * BS, HALF), BF16)
            up[0 : 4 * BS] = p7[...]
            up[4 * BS : 5 * BS] = spill[:, :HALF]
            up[5 * BS : 6 * BS] = spill[:, HALF:]
            up[6 * BS : 7 * BS] = factor[:, :HALF]
            up[7 * BS :] = factor[:, HALF:]


def inner_body(a_idx, p_idx, a_ref, p_ref, wait_rows, out_hbm, part0, h0, pt0, row1, row7, table, pairs, rows, out_sem):
    zero = jnp.zeros((BS, HALF), BF16)
    table[3 * ROWS] = jnp.zeros((BS, WIDE), BF16)

    @pl.loop(0, GROUPS)
    def _(g):
        for i in range(RATIO):
            row = g * RATIO + i
            here, there = pair(p_idx, row, p_ref[row])
            table[row] = jnp.concatenate([here, zero], 1)
            table[ROWS + row] = centred(there)
            table[2 * ROWS + row] = jnp.concatenate([zero, here], 1)
            pairs[g, i * BS : (i + 1) * BS] = here

    def product(g, i):
        row = g * RATIO + i
        blocks = []
        for k in range(KA):
            at = column(a_idx, k, row)
            place = (at // RATIO - g) * ROWS + at - RATIO
            if g == 0:
                place = jnp.where(at < RATIO, 3 * ROWS, place)
            blocks.append(table[place])
        return dot(a_ref[row], jnp.concatenate(blocks, 0))

    wait_rows()
    for i in range(RATIO):
        part0[i * BS : (i + 1) * BS] = product(0, i)
        places = [column(a_idx, k, i) for k in range(KA)]
        h0[i * BS : (i + 1) * BS] = spread(a_ref[i], places)
    pt0[...] = pairs[0].T
    before = None
    out_copies = []
    for g in range(1, GROUPS - 1):
        both = dot_rows(pairs[g], jnp.concatenate([product(g, i).astype(BF16) for i in range(RATIO)], 0))
        row = shifted(both[:BS])
        if g == 1:
            row1[...] = row
        else:
            rows[g - 2] = row + padded(before)
            copy = pltpu.make_async_copy(rows.at[g - 2], out_hbm.at[g], out_sem.at[g - 2])
            copy.start()
            out_copies.append(copy)
        before = both[BS:]
    row7[...] = padded(before)
    for copy in out_copies:
        copy.wait()


def turn():
    return jnp.where(lax.axis_index("col") == 0, 0, 1)


INNER_SCRATCH = [
    pltpu.SMEM((KA, ROWS), jnp.int32),
    pltpu.SMEM((2, ROWS), jnp.int32),
    pltpu.VMEM((ROWS, BS, KA * BS), BF16),
    pltpu.VMEM((ROWS, BS, HALF), BF16),
    pltpu.VMEM((3 * ROWS + 1, BS, WIDE), BF16),
    pltpu.VMEM((GROUPS, 4 * BS, HALF), BF16),
    pltpu.VMEM((GROUPS - 3, BS, BAND), F32),
    pltpu.SemaphoreType.DMA((8,)),
    pltpu.SemaphoreType.DMA((GROUPS - 3,)),
]
vmem = lambda *shape: pltpu.VMEM(shape[:-1], shape[-1])
INNER_SHAPES = [
    jax.ShapeDtypeStruct((GROUPS, BS, BAND), F32),
    vmem(4 * BS, WIDE, F32),
    vmem(4 * BS, WIDE, BF16),
    vmem(HALF, 4 * BS, BF16),
    vmem(BS, BAND, F32),
    vmem(BS, BAND, F32),
]
EDGE_SHAPES = [
    vmem(8 * BS, HALF, BF16),
    vmem(8 * BS, HALF, BF16),
    vmem(8 * BS, HALF, BF16),
    vmem(4 * BS, WIDE, F32),
    vmem(4 * BS, WIDE, BF16),
    vmem(HALF, 4 * BS, BF16),
    vmem(4 * BS, HALF, BF16),
]


def edge_kernel(a_idx_hbm, p_idx_hbm, a_hbm, p_hbm, *refs):
    edge_out = refs[:7]
    a_idx, p_idx, a_ref, p_ref, sem, edge_table, p7 = refs[7:]

    def part(source, to, at, size, n):
        return pltpu.make_async_copy(source.at[pl.ds(at, size)], to.at[pl.ds(at, size)], sem.at[n])

    copies = [
        pltpu.make_async_copy(a_idx_hbm, a_idx, sem.at[0]),
        pltpu.make_async_copy(p_idx_hbm, p_idx, sem.at[1]),
        part(p_hbm, p_ref, ROWS - 8, 8, 2),
        part(p_hbm, p_ref, 0, 4, 3),
        part(a_hbm, a_ref, ROWS - 4, 4, 4),
    ]
    for copy in copies:
        copy.start()
    for copy in copies:
        copy.wait()
    edge_body(a_idx, p_idx, a_ref, p_ref, *edge_out, edge_table, p7)


def edge(*operands):
    return pl.pallas_call(
        edge_kernel,
        in_specs=[ANY] * 4,
        out_specs=[VMEM] * 7,
        out_shape=EDGE_SHAPES,
        scratch_shapes=INNER_SCRATCH[:4]
        + [
            pltpu.SemaphoreType.DMA((5,)),
            pltpu.VMEM((2 * RATIO + 1, BS, WIDE), BF16),
            pltpu.VMEM((4 * BS, HALF), BF16),
        ],
        compiler_params=pltpu.CompilerParams(vmem_limit_bytes=16 << 20),
        cost_estimate=pl.CostEstimate(flops=1 << 28, bytes_accessed=1 << 20, transcendentals=0),
        name="edge",
    )(*operands)


def inner_kernel(mine, skip, a_idx_hbm, p_idx_hbm, a_hbm, p_hbm, *refs):
    inner_out = refs[skip : skip + 6]
    a_idx, p_idx, a_ref, p_ref, table, pairs, rows, sem, out_sem = refs[-9:]

    @pl.when(turn() == mine)
    def _():
        pieces = [(p_hbm, p_ref), (a_idx_hbm, a_idx), (p_idx_hbm, p_idx), (a_hbm, a_ref)]
        copies = [pltpu.make_async_copy(x, y, sem.at[n]) for n, (x, y) in enumerate(pieces)]
        for copy in copies:
            copy.start()
        for copy in copies[:3]:
            copy.wait()
        inner_body(a_idx, p_idx, a_ref, p_ref, copies[3].wait, *inner_out, table, pairs, rows, out_sem)


def inner(mine, operands, out=None, sent=()):
    given = [] if out is None else [out]
    return pl.pallas_call(
        functools.partial(inner_kernel, mine, len(given) + len(sent)),
        in_specs=[ANY] * (4 + len(given) + len(sent)),
        out_specs=[ANY] + [VMEM] * 5 + [ANY] * len(sent),
        out_shape=INNER_SHAPES + [vmem(*x.shape, x.dtype) for x in sent],
        input_output_aliases={4: 0} if given else {4 + i: 6 + i for i in range(len(sent))},
        scratch_shapes=INNER_SCRATCH,
        compiler_params=pltpu.CompilerParams(vmem_limit_bytes=24 << 20),
        cost_estimate=pl.CostEstimate(flops=1 << 30, bytes_accessed=1 << 22, transcendentals=0),
        name="inner",
    )(*operands, *given, *sent)


def last_kernel(inter, intra, final, part7, h7, pt7, p0, *refs):
    starts, (_, out_hbm, rows, sem) = [refs[:5], refs[5:10]], refs[10:]
    at = lax.axis_index("col")
    core = at & 1
    beside = jnp.where(at < lax.axis_size("col") - 2, intra[...], final[...])
    from_before = jnp.where(core == 0, inter[...], beside)
    from_after = jnp.where(core == 0, beside, inter[...])

    def finish(part0, h0, pt0, row1, row7):
        edge0 = part0[:, :HALF] + dot(h0[...], from_before[: 4 * BS])
        product0 = jnp.concatenate([edge0.astype(BF16), part0[:, HALF:].astype(BF16)], 1)
        edge7 = part7[:, HALF:] + dot(h7[...], from_after[: 4 * BS])
        product7 = jnp.concatenate([part7[:, :HALF].astype(BF16), edge7.astype(BF16)], 1)
        both0 = dot(pt0[...], product0)
        lower7 = dot(pt7[:BS], product7)
        factor = jnp.concatenate([from_before[6 * BS : 7 * BS], from_before[7 * BS :]], 1)
        spill0 = from_before[4 * BS : 5 * BS].astype(F32)
        spill1 = from_before[5 * BS : 6 * BS].astype(F32) + dot(factor, p0[...])
        rows[0] = shifted(both0[:BS]) + padded(jnp.concatenate([spill0, spill1], 1))
        rows[1] = row1[...] + padded(both0[BS:])
        rows[2] = row7[...] + shifted(lower7)

    for mine in range(2):

        @pl.when(turn() == mine)
        def _(mine=mine):
            finish(*starts[mine])

    copies = [
        pltpu.make_async_copy(rows.at[pl.ds(0, 2)], out_hbm.at[pl.ds(0, 2)], sem.at[0]),
        pltpu.make_async_copy(rows.at[2], out_hbm.at[GROUPS - 1], sem.at[1]),
    ]
    for copy in copies:
        copy.start()
    for copy in copies:
        copy.wait()


def last(*args):
    return pl.pallas_call(
        last_kernel,
        in_specs=[VMEM] * 17 + [ANY],
        out_specs=ANY,
        out_shape=jax.ShapeDtypeStruct((GROUPS, BS, BAND), F32),
        input_output_aliases={17: 0},
        scratch_shapes=[pltpu.VMEM((3, BS, BAND), F32), pltpu.SemaphoreType.DMA((2,))],
        compiler_params=pltpu.CompilerParams(vmem_limit_bytes=16 << 20),
        cost_estimate=pl.CostEstimate(flops=1 << 26, bytes_accessed=1 << 19, transcendentals=0),
        name="last",
    )(*args)


def shards(a_blocks, a_index, p_blocks, p_index):
    hbm = lambda x: pltpu.with_memory_space_constraint(x, pltpu.HBM)
    operands = hbm(a_index.T), hbm(p_index.T), hbm(a_blocks), hbm(p_blocks)
    axes = ("row", "col")
    devices, line = lax.axis_size(axes), lax.axis_size("col")
    intra, inter, final, part7, h7, pt7, p0 = edge(*operands)
    within = [(d, d ^ 1) for d in range(devices)]
    most = [(s, t) for s, t in within if s % line < line - 2]
    others = [(s, t) for s, t in within if s % line >= line - 2]
    across = [(d, (d + 1 if d % 2 else d - 1) % devices) for d in range(devices)]
    from_most = lax.ppermute(intra, axes, most)
    out, *starts, inter, final = inner(0, operands, sent=(inter, final))
    from_across = lax.ppermute(inter, axes, across)
    from_final = lax.ppermute(final, axes, others)
    out, *ends = inner(1, operands, out)
    return last(from_across, from_most, from_final, part7, h7, pt7, p0, *starts, *ends, out)


def solution(mesh):
    blocks = P(("row", "col"), None, None)
    index = P(("row", "col"), None)
    return jax.shard_map(
        shards, mesh=mesh, in_specs=(blocks, index, blocks, index), out_specs=blocks, check_vma=False
    )
```

```python
import jax
import jax.numpy as jnp
from jax import lax
from jax.experimental import pallas as pl
from jax.experimental.pallas import tpu as pltpu
from jax.sharding import PartitionSpec as P

BS = 64
KA = 8
RATIO = 4
GROUPS = 8
ROWS = RATIO * GROUPS
HALF = 2 * BS
WIDE = 4 * BS
BAND = 5 * BS
F32, BF16 = jnp.float32, jnp.bfloat16
SMEM = pl.BlockSpec(memory_space=pltpu.SMEM)
VMEM = pl.BlockSpec(memory_space=pltpu.VMEM)
ANY = pl.BlockSpec(memory_space=pl.ANY)


def low_half(rows):
    return lax.broadcasted_iota(jnp.int32, (rows, HALF), 1) < BS


def dot(x, y):
    return jnp.dot(x, y, preferred_element_type=F32)


def dot_rows(x, y):
    return lax.dot_general(x, y, (((0,), (0,)), ((), ())), preferred_element_type=F32)


def pair(p_idx, row, block):
    first = ((p_idx[0, row] - row // RATIO) & 1).astype(F32)
    second = ((p_idx[1, row] - row // RATIO) & 1).astype(F32)
    low = low_half(BS)
    x = block.astype(F32)
    y = pltpu.roll(x, BS, 1)
    here = x * jnp.where(low, 1.0 - first, second) + y * jnp.where(low, 1.0 - second, first)
    there = y * jnp.where(low, second, 1.0 - first) + x * jnp.where(low, first, 1.0 - second)
    return here.astype(BF16), there


def centred(there):
    low = low_half(BS)
    zero = jnp.zeros_like(there)
    return jnp.concatenate([jnp.where(low, zero, there), jnp.where(low, there, zero)], 1).astype(BF16)


def column(a_idx, k, row):
    return row + ((a_idx[k, row] - row + RATIO) & 15)


def spread(a_row, places):
    low = low_half(BS)
    tiles = [jnp.zeros((BS, HALF), F32)] * 2
    for j in range(KA // 2):
        x = a_row[:, j * HALF : (j + 1) * HALF].astype(F32)
        y = pltpu.roll(x, BS, 1)
        for blocks, at in ((x, (2 * j, 2 * j + 1)), (y, (2 * j + 1, 2 * j))):
            place = jnp.where(low, places[at[0]], places[at[1]])
            for t in range(2):
                wanted = jnp.where(low, 2 * t, 2 * t + 1)
                tiles[t] = tiles[t] + jnp.where(place == wanted, blocks, 0.0)
    return jnp.concatenate(tiles, 1).astype(BF16)


def shifted(x):
    return pltpu.roll(jnp.concatenate([x, jnp.zeros((BS, HALF), F32)], 1), BS, 1)[:, :BAND]


def padded(x):
    return jnp.concatenate([x, jnp.zeros((BS, BS), F32)], 1)


def edge_body(a_idx, p_idx, a_ref, p_ref, in_chip, inter, part7, h7, pt7, p0, table, p7):
    first = ROWS - 2 * RATIO
    zero = jnp.zeros((BS, HALF), BF16)
    for i in range(RATIO):
        here, _ = pair(p_idx, first + i, p_ref[first + i])
        table[i] = jnp.concatenate([here, zero], 1)
    for i in range(RATIO):
        here, there = pair(p_idx, first + RATIO + i, p_ref[first + RATIO + i])
        table[RATIO + i] = centred(there)
        p7[i * BS : (i + 1) * BS] = here
    table[2 * RATIO] = jnp.zeros((BS, WIDE), BF16)
    for i in range(RATIO):
        here, _ = pair(p_idx, i, p_ref[i])
        p0[i * BS : (i + 1) * BS] = here
    for i in range(RATIO):
        row = ROWS - RATIO + i
        places = [column(a_idx, k, row) - RATIO - first for k in range(KA)]
        weights = jnp.concatenate([table[jnp.minimum(place, 2 * RATIO)] for place in places], 0)
        part7[i * BS : (i + 1) * BS] = dot(a_ref[row], weights)
        h7[i * BS : (i + 1) * BS] = spread(a_ref[row], [place - 2 * RATIO for place in places])
    turned = p7[...].T
    pt7[...] = turned
    after = turned[BS:]
    spill = dot(after, part7[...].astype(BF16)).astype(BF16)
    factor = dot(after, h7[...]).astype(BF16)
    core = lax.axis_index("col") & 1
    for mine, (down, up) in enumerate(((inter, in_chip), (in_chip, inter))):

        @pl.when(core == mine)
        def _(down=down, up=up):
            down[0 : 4 * BS] = p0[...]
            down[4 * BS :] = jnp.zeros((4 * BS, HALF), BF16)
            up[0 : 4 * BS] = p7[...]
            up[4 * BS : 5 * BS] = spill[:, :HALF]
            up[5 * BS : 6 * BS] = spill[:, HALF:]
            up[6 * BS : 7 * BS] = factor[:, :HALF]
            up[7 * BS :] = factor[:, HALF:]


def inner_body(a_idx, p_idx, a_ref, p_ref, edges, out_hbm, row0, row1, row7, k0, k7, table, pairs, rows, out_sem):
    part7, h7, pt7 = edges
    zero = jnp.zeros((BS, HALF), BF16)
    table[3 * ROWS] = jnp.zeros((BS, WIDE), BF16)

    @pl.loop(0, GROUPS)
    def _(g):
        for i in range(RATIO):
            row = g * RATIO + i
            here, there = pair(p_idx, row, p_ref[row])
            table[row] = jnp.concatenate([here, zero], 1)
            table[ROWS + row] = centred(there)
            table[2 * ROWS + row] = jnp.concatenate([zero, here], 1)
            pairs[g, i * BS : (i + 1) * BS] = here

    def product(g, i):
        row = g * RATIO + i
        blocks = []
        for k in range(KA):
            at = column(a_idx, k, row)
            place = (at // RATIO - g) * ROWS + at - RATIO
            if g == 0:
                place = jnp.where(at < RATIO, 3 * ROWS, place)
            blocks.append(table[place])
        return dot(a_ref[row], jnp.concatenate(blocks, 0))

    before = None
    out_copies = []
    for g in range(1, GROUPS - 1):
        both = dot_rows(pairs[g], jnp.concatenate([product(g, i).astype(BF16) for i in range(RATIO)], 0))
        row = shifted(both[:BS])
        if g == 1:
            row1[...] = row
        else:
            rows[g - 2] = row + padded(before)
            copy = pltpu.make_async_copy(rows.at[g - 2], out_hbm.at[g], out_sem.at[g - 2])
            copy.start()
            out_copies.append(copy)
        before = both[BS:]
    row7[...] = padded(before) + shifted(dot(pt7[:BS], part7[...].astype(BF16)))
    k7[...] = dot(pt7[:BS], h7[...]).astype(BF16)
    both = dot_rows(pairs[0], jnp.concatenate([product(0, i).astype(BF16) for i in range(RATIO)], 0))
    row0[...] = shifted(both[:BS])
    row1[...] += padded(both[BS:])
    h0 = jnp.concatenate([spread(a_ref[i], [column(a_idx, k, i) for k in range(KA)]) for i in range(RATIO)], 0)
    k0[...] = dot_rows(pairs[0], h0).astype(BF16)
    for copy in out_copies:
        copy.wait()


def turn():
    return jnp.where(jnp.logical_and(lax.axis_index("col") == 0, lax.axis_index("row") > 0), 0, 1)


def late():
    return lax.axis_index("col") >= lax.axis_size("col") - 2


vmem = lambda *shape: pltpu.VMEM(shape[:-1], shape[-1])
INDEX_SCRATCH = [pltpu.SMEM((KA, ROWS), jnp.int32), pltpu.SMEM((2, ROWS), jnp.int32), pltpu.SemaphoreType.DMA((5,))]
EDGE_SCRATCH = [vmem(2 * RATIO + 1, BS, WIDE, BF16), vmem(4 * BS, HALF, BF16)]
INNER_SCRATCH = [
    vmem(3 * ROWS + 1, BS, WIDE, BF16),
    vmem(GROUPS, 4 * BS, HALF, BF16),
    vmem(GROUPS - 3, BS, BAND, F32),
    pltpu.SemaphoreType.DMA((GROUPS - 3,)),
]
PAYLOAD = vmem(8 * BS, HALF, BF16)
EDGE_SHAPES = [
    PAYLOAD,
    vmem(4 * BS, WIDE, F32),
    vmem(4 * BS, WIDE, BF16),
    vmem(HALF, 4 * BS, BF16),
    vmem(4 * BS, HALF, BF16),
]
INNER_SHAPES = [jax.ShapeDtypeStruct((GROUPS, BS, BAND), F32)] + [vmem(BS, BAND, F32)] * 3
INNER_SHAPES += [vmem(HALF, WIDE, BF16), vmem(BS, WIDE, BF16)]


def run(kernel, name, flops, **settings):
    return pl.pallas_call(
        kernel,
        compiler_params=pltpu.CompilerParams(vmem_limit_bytes=20 << 20),
        cost_estimate=pl.CostEstimate(flops=flops, bytes_accessed=1 << 20, transcendentals=0),
        name=name,
        **settings,
    )


def index_copies(a_idx_from, p_idx_from, a_idx, p_idx, sem):
    copies = [pltpu.make_async_copy(a_idx_from, a_idx, sem.at[0]), pltpu.make_async_copy(p_idx_from, p_idx, sem.at[1])]
    for copy in copies:
        copy.start()
    return copies


def edge_kernel(a_idx_hbm, p_idx_hbm, a_hbm, p_hbm, *refs):
    edge_out = refs[:6]
    a_idx, p_idx, sem, edge_table, p7, a_ref, p_ref = refs[6:]

    @pl.when(jnp.logical_not(late()))
    def _():
        copies = index_copies(a_idx_hbm, p_idx_hbm, a_idx, p_idx, sem)
        pieces = [(p_hbm, p_ref, ROWS - 8, 8), (p_hbm, p_ref, 0, 4), (a_hbm, a_ref, ROWS - 4, 4)]
        for n, (source, to, at, size) in enumerate(pieces):
            part = pl.ds(at, size)
            copies.append(pltpu.make_async_copy(source.at[part], to.at[part], sem.at[2 + n]))
            copies[-1].start()
        for copy in copies:
            copy.wait()
        edge_body(a_idx, p_idx, a_ref, p_ref, *edge_out, edge_table, p7)


def edge(operands):
    return run(
        edge_kernel,
        "edge",
        1 << 28,
        in_specs=[ANY] * 4,
        out_specs=[VMEM] * 6,
        out_shape=[PAYLOAD] + EDGE_SHAPES,
        scratch_shapes=INDEX_SCRATCH + EDGE_SCRATCH + [vmem(ROWS, BS, KA * BS, BF16), vmem(ROWS, BS, HALF, BF16)],
    )(*operands)


def middle_kernel(a_idx_from, p_idx_from, a_ref, p_ref, *refs):
    given, final, edge_out, inner_out = refs[:5], refs[5], refs[6:11], refs[11:17]
    a_idx, p_idx, sem, edge_table, p7, *inner_scratch = refs[17:]
    copies = index_copies(a_idx_from, p_idx_from, a_idx, p_idx, sem)

    @pl.when(jnp.logical_not(late()))
    def _():
        for x, y in zip(given, edge_out, strict=True):
            y[...] = x[...]

    for copy in copies:
        copy.wait()

    @pl.when(late())
    def _():
        edge_body(a_idx, p_idx, a_ref, p_ref, final, *edge_out, edge_table, p7)

    @pl.when(turn() == 0)
    def _():
        inner_body(a_idx, p_idx, a_ref, p_ref, edge_out[1:4], *inner_out, *inner_scratch)


def middle(operands, given):
    return run(
        middle_kernel,
        "middle",
        1 << 30,
        in_specs=[VMEM] * 9,
        out_specs=[VMEM] * 6 + [ANY] + [VMEM] * 5,
        out_shape=[PAYLOAD] + EDGE_SHAPES + INNER_SHAPES,
        scratch_shapes=INDEX_SCRATCH + EDGE_SCRATCH + INNER_SCRATCH,
    )(*operands, *given)


def inner_kernel(a_idx_from, p_idx_from, a_ref, p_ref, *refs):
    edges, inner_out = refs[:3], refs[4:10]
    a_idx, p_idx, sem, *inner_scratch = refs[10:]

    @pl.when(turn() == 1)
    def _():
        for copy in index_copies(a_idx_from, p_idx_from, a_idx, p_idx, sem):
            copy.wait()
        inner_body(a_idx, p_idx, a_ref, p_ref, edges, *inner_out, *inner_scratch)


def inner(operands, edges, out):
    return run(
        inner_kernel,
        "inner",
        1 << 30,
        in_specs=[VMEM] * 7 + [ANY],
        out_specs=[ANY] + [VMEM] * 5,
        out_shape=INNER_SHAPES,
        input_output_aliases={7: 0},
        scratch_shapes=INDEX_SCRATCH + INNER_SCRATCH,
    )(*operands, *edges, out)


def last_kernel(inter, intra, final, p0, *refs):
    starts, (_, out_hbm, rows, sem) = [refs[:5], refs[5:10]], refs[10:]
    core = lax.axis_index("col") & 1

    def finish(from_before, from_after, row0, row1, row7, k0, k7):
        both0 = dot(k0[...], from_before[: 4 * BS])
        lower7 = dot(k7[...], from_after[: 4 * BS])
        spill0 = from_before[4 * BS : 5 * BS].astype(F32)
        spill1 = from_before[5 * BS : 6 * BS].astype(F32)
        spill1 += dot(from_before[6 * BS : 7 * BS], p0[:HALF]) + dot(from_before[7 * BS :], p0[HALF:])
        zero = jnp.zeros((BS, HALF), F32)
        rows[0] = row0[...] + shifted(jnp.concatenate([both0[:BS], zero], 1))
        rows[0] += padded(jnp.concatenate([spill0, spill1], 1))
        rows[1] = row1[...] + padded(jnp.concatenate([both0[BS:], zero], 1))
        rows[2] = row7[...] + shifted(jnp.concatenate([zero, lower7], 1))

    in_chip = jnp.where(late(), final[...], intra[...])
    from_before = jnp.where(core == 0, inter[...], in_chip)
    from_after = jnp.where(core == 0, in_chip, inter[...])
    for mine in range(2):

        @pl.when(turn() == mine)
        def _(mine=mine):
            finish(from_before, from_after, *starts[mine])

    copies = [
        pltpu.make_async_copy(rows.at[pl.ds(0, 2)], out_hbm.at[pl.ds(0, 2)], sem.at[0]),
        pltpu.make_async_copy(rows.at[2], out_hbm.at[GROUPS - 1], sem.at[1]),
    ]
    for copy in copies:
        copy.start()
    for copy in copies:
        copy.wait()


def last(*args):
    return run(
        last_kernel,
        "last",
        1 << 26,
        in_specs=[VMEM] * 14 + [ANY],
        out_specs=ANY,
        out_shape=INNER_SHAPES[0],
        input_output_aliases={14: 0},
        scratch_shapes=[vmem(3, BS, BAND, F32), pltpu.SemaphoreType.DMA((2,))],
    )(*args)


def shards(a_blocks, a_index, p_blocks, p_index):
    operands = a_index.T, p_index.T, a_blocks, p_blocks
    in_hbm = [pltpu.with_memory_space_constraint(x, pltpu.HBM) for x in operands]
    in_vmem = [pltpu.with_memory_space_constraint(x, pltpu.VMEM) for x in operands]
    axes = ("row", "col")
    devices, line = lax.axis_size(axes), lax.axis_size("col")
    intra, *given = edge(in_hbm)
    within = [(d, d ^ 1) for d in range(devices)]
    most = [(s, t) for s, t in within if s % line < line - 2]
    others = [(s, t) for s, t in within if s % line >= line - 2]
    across = [(d, (d + 1 if d % 2 else d - 1) % devices) for d in range(devices)]
    from_most = lax.ppermute(intra, axes, most)
    final, inter, part7, h7, pt7, p0, out, *starts = middle(in_vmem, given)
    from_across = lax.ppermute(inter, axes, across)
    from_final = lax.ppermute(final, axes, others)
    out, *ends = inner(in_vmem, (part7, h7, pt7), out)
    return last(from_across, from_most, from_final, p0, *starts, *ends, out)


def solution(mesh):
    blocks = P(("row", "col"), None, None)
    index = P(("row", "col"), None)
    return jax.shard_map(
        shards, mesh=mesh, in_specs=(blocks, index, blocks, index), out_specs=blocks, check_vma=False
    )
```

```python
import functools

import jax
import jax.numpy as jnp
from jax import lax
from jax.experimental import pallas as pl
from jax.experimental.pallas import tpu as pltpu
from jax.sharding import PartitionSpec as P

BS = 64
KA = 8
RATIO = 4
GROUPS = 8
ROWS = RATIO * GROUPS
HALF = 2 * BS
WIDE = 4 * BS
BAND = 5 * BS
F32, BF16 = jnp.float32, jnp.bfloat16
SMEM = pl.BlockSpec(memory_space=pltpu.SMEM)
VMEM = pl.BlockSpec(memory_space=pltpu.VMEM)
ANY = pl.BlockSpec(memory_space=pl.ANY)


def low_half(rows):
    return lax.broadcasted_iota(jnp.int32, (rows, HALF), 1) < BS


def dot(x, y):
    return jnp.dot(x, y, preferred_element_type=F32)


def dot_rows(x, y):
    return lax.dot_general(x, y, (((0,), (0,)), ((), ())), preferred_element_type=F32)


def pair(p_idx, row, block):
    first = ((p_idx[0, row] - row // RATIO) & 1).astype(F32)
    second = ((p_idx[1, row] - row // RATIO) & 1).astype(F32)
    low = low_half(BS)
    x = block.astype(F32)
    y = pltpu.roll(x, BS, 1)
    here = x * jnp.where(low, 1.0 - first, second) + y * jnp.where(low, 1.0 - second, first)
    there = y * jnp.where(low, second, 1.0 - first) + x * jnp.where(low, first, 1.0 - second)
    return here.astype(BF16), there


def centred(there):
    low = low_half(BS)
    zero = jnp.zeros_like(there)
    return jnp.concatenate([jnp.where(low, zero, there), jnp.where(low, there, zero)], 1).astype(BF16)


def column(a_idx, k, row):
    return row + ((a_idx[k, row] - row + RATIO) & 15)


def spread(a_row, places):
    low = low_half(BS)
    tiles = [jnp.zeros((BS, HALF), F32)] * 2
    for j in range(KA // 2):
        x = a_row[:, j * HALF : (j + 1) * HALF].astype(F32)
        y = pltpu.roll(x, BS, 1)
        for blocks, at in ((x, (2 * j, 2 * j + 1)), (y, (2 * j + 1, 2 * j))):
            place = jnp.where(low, places[at[0]], places[at[1]])
            for t in range(2):
                wanted = jnp.where(low, 2 * t, 2 * t + 1)
                tiles[t] = tiles[t] + jnp.where(place == wanted, blocks, 0.0)
    return jnp.concatenate(tiles, 1).astype(BF16)


def shifted(x):
    return pltpu.roll(jnp.concatenate([x, jnp.zeros((BS, HALF), F32)], 1), BS, 1)[:, :BAND]


def padded(x):
    return jnp.concatenate([x, jnp.zeros((BS, BS), F32)], 1)


def edge_body(a_idx, p_idx, a_last, p_ref, wait_rows, intra, inter, final, low7, k7, p0, table, p7):
    first = ROWS - 2 * RATIO
    zero = jnp.zeros((BS, HALF), BF16)
    for i in range(RATIO):
        here, there = pair(p_idx, first + RATIO + i, p_ref[first + RATIO + i])
        table[RATIO + i] = centred(there)
        p7[i * BS : (i + 1) * BS] = here
    for i in range(RATIO):
        here, _ = pair(p_idx, first + i, p_ref[first + i])
        table[i] = jnp.concatenate([here, zero], 1)
    table[2 * RATIO] = jnp.zeros((BS, WIDE), BF16)
    for i in range(RATIO):
        here, _ = pair(p_idx, i, p_ref[i])
        p0[i * BS : (i + 1) * BS] = here
    turned = p7[...].T
    wait_rows()
    parts, halos = [], []
    for i in range(RATIO):
        row = ROWS - RATIO + i
        places = [column(a_idx, k, row) - RATIO - first for k in range(KA)]
        weights = jnp.concatenate([table[jnp.minimum(place, 2 * RATIO)] for place in places], 0)
        parts.append(dot(a_last[i], weights).astype(BF16))
        halos.append(spread(a_last[i], [place - 2 * RATIO for place in places]))
    factor = dot(turned, jnp.concatenate(halos, 0)).astype(BF16)
    tiles = dot(turned, jnp.concatenate(parts, 0))
    low7[...] = tiles[:BS]
    k7[...] = factor[:BS]
    spill = tiles[BS:].astype(BF16)
    core = lax.axis_index("col") & 1
    for mine, last, down, up in ((0, 0, inter, intra), (1, 0, intra, inter), (0, 1, inter, final), (1, 1, final, inter)):

        @pl.when(jnp.logical_and(core == mine, late().astype(jnp.int32) == last))
        def _(down=down, up=up):
            down[0 : 4 * BS] = p0[...]
            down[4 * BS :] = jnp.zeros((4 * BS, HALF), BF16)
            up[0 : 4 * BS] = p7[...]
            up[4 * BS : 5 * BS] = spill[:, :HALF]
            up[5 * BS : 6 * BS] = spill[:, HALF:]
            up[6 * BS : 7 * BS] = factor[BS:, :HALF]
            up[7 * BS :] = factor[BS:, HALF:]


def inner_body(a_idx, p_idx, a_ref, p_ref, wait_rows, out_hbm, row0, row1, up6, k0, table, pairs, rows, out_sem):
    zero = jnp.zeros((BS, HALF), BF16)
    table[3 * ROWS] = jnp.zeros((BS, WIDE), BF16)

    @pl.loop(0, GROUPS)
    def _(g):
        for i in range(RATIO):
            row = g * RATIO + i
            here, there = pair(p_idx, row, p_ref[row])
            table[row] = jnp.concatenate([here, zero], 1)
            table[ROWS + row] = centred(there)
            table[2 * ROWS + row] = jnp.concatenate([zero, here], 1)
            pairs[g, i * BS : (i + 1) * BS] = here

    def product(g, i):
        row = g * RATIO + i
        blocks = []
        for k in range(KA):
            at = column(a_idx, k, row)
            place = (at // RATIO - g) * ROWS + at - RATIO
            if g == 0:
                place = jnp.where(at < RATIO, 3 * ROWS, place)
            blocks.append(table[place])
        return dot(a_ref[row], jnp.concatenate(blocks, 0))

    wait_rows()
    before = None
    out_copies = []
    for g in range(1, GROUPS - 1):
        both = dot_rows(pairs[g], jnp.concatenate([product(g, i).astype(BF16) for i in range(RATIO)], 0))
        row = shifted(both[:BS])
        if g == 1:
            row1[...] = row
        else:
            rows[g - 2] = row + padded(before)
            copy = pltpu.make_async_copy(rows.at[g - 2], out_hbm.at[g], out_sem.at[g - 2])
            copy.start()
            out_copies.append(copy)
        before = both[BS:]
    up6[...] = before
    both = dot_rows(pairs[0], jnp.concatenate([product(0, i).astype(BF16) for i in range(RATIO)], 0))
    row0[...] = shifted(both[:BS])
    row1[...] += padded(both[BS:])
    h0 = jnp.concatenate([spread(a_ref[i], [column(a_idx, k, i) for k in range(KA)]) for i in range(RATIO)], 0)
    k0[...] = dot_rows(pairs[0], h0).astype(BF16)
    for copy in out_copies:
        copy.wait()


def turn():
    row, col = lax.axis_index("row"), lax.axis_index("col")
    return jnp.where(col >= 2, 2, jnp.where(row * 2 + 1 - col == 0, 0, 1))


def late():
    return lax.axis_index("col") >= lax.axis_size("col") - 2


vmem = lambda *shape: pltpu.VMEM(shape[:-1], shape[-1])
PAYLOAD = vmem(8 * BS, HALF, BF16)
EDGE_SHAPES = [PAYLOAD] * 3 + [vmem(BS, WIDE, F32), vmem(BS, WIDE, BF16), vmem(4 * BS, HALF, BF16)]
OUT = jax.ShapeDtypeStruct((GROUPS, BS, BAND), F32)
INNER_SHAPES = [OUT, vmem(BS, BAND, F32), vmem(BS, BAND, F32), vmem(BS, WIDE, F32), vmem(HALF, WIDE, BF16)]
INNER_SPECS = [ANY] + [VMEM] * 4
FETCH_SCRATCH = [
    pltpu.SMEM((KA, ROWS), jnp.int32),
    pltpu.SMEM((2, ROWS), jnp.int32),
    vmem(ROWS, BS, KA * BS, BF16),
    vmem(ROWS, BS, HALF, BF16),
    pltpu.SemaphoreType.DMA((4,)),
]
INNER_SCRATCH = [
    vmem(3 * ROWS + 1, BS, WIDE, BF16),
    vmem(GROUPS, 4 * BS, HALF, BF16),
    vmem(GROUPS - 3, BS, BAND, F32),
    pltpu.SemaphoreType.DMA((GROUPS - 3,)),
]


def run(kernel, name, flops, **settings):
    return pl.pallas_call(
        kernel,
        compiler_params=pltpu.CompilerParams(vmem_limit_bytes=20 << 20),
        cost_estimate=pl.CostEstimate(flops=flops, bytes_accessed=1 << 20, transcendentals=0),
        name=name,
        **settings,
    )


def fetch(sources, places, sem):
    copies = [pltpu.make_async_copy(x, y, sem.at[n]) for n, (x, y) in enumerate(zip(sources, places, strict=True))]
    for copy in copies:
        copy.start()
    return copies


def inner_groups(sources, inner_out, scratch):
    a_idx, p_idx, a_ref, p_ref, sem, *rest = scratch
    a_idx_hbm, p_idx_hbm, a_hbm, p_hbm = sources
    copies = fetch((p_hbm, a_idx_hbm, p_idx_hbm, a_hbm), (p_ref, a_idx, p_idx, a_ref), sem)
    for copy in copies[:3]:
        copy.wait()
    inner_body(a_idx, p_idx, a_ref, p_ref, copies[3].wait, *inner_out, *rest)


def edge_kernel(*refs):
    sources, edge_out, inner_out, scratch = refs[:4], refs[4:10], refs[10:15], refs[15:]
    a_idx_hbm, p_idx_hbm, a_hbm, p_hbm = sources
    *inner_scratch, table, p7, a_last, p_ends, sem = scratch
    a_idx, p_idx = inner_scratch[:2]
    near = pl.ds(0, RATIO)
    far = pl.ds(ROWS - 2 * RATIO, 2 * RATIO)
    copies = fetch(
        (p_idx_hbm, a_idx_hbm, p_hbm.at[far], p_hbm.at[near], a_hbm.at[pl.ds(ROWS - RATIO, RATIO)]),
        (p_idx, a_idx, p_ends.at[far], p_ends.at[near], a_last),
        sem,
    )
    for copy in copies[:4]:
        copy.wait()
    edge_body(a_idx, p_idx, a_last, p_ends, copies[4].wait, *edge_out, table, p7)

    @pl.when(turn() == 0)
    def _():
        inner_groups(sources, inner_out, inner_scratch)


def edge(operands):
    return run(
        edge_kernel,
        "edge",
        1 << 28,
        in_specs=[ANY] * 4,
        out_specs=[VMEM] * 6 + INNER_SPECS,
        out_shape=EDGE_SHAPES + INNER_SHAPES,
        scratch_shapes=FETCH_SCRATCH
        + INNER_SCRATCH
        + [
            vmem(2 * RATIO + 1, BS, WIDE, BF16),
            vmem(4 * BS, HALF, BF16),
            vmem(RATIO, BS, KA * BS, BF16),
            vmem(ROWS, BS, HALF, BF16),
            pltpu.SemaphoreType.DMA((5,)),
        ],
    )(*operands)


def inner_kernel(mine, handed, *refs):
    sources, inner_out, scratch = refs[:4], refs[5 + handed : 10 + handed], refs[10 + 2 * handed :]

    @pl.when(turn() == mine)
    def _():
        inner_groups(sources, inner_out, scratch)


def inner(mine, operands, out, *sent):
    return run(
        functools.partial(inner_kernel, mine, len(sent)),
        "inner",
        1 << 30,
        in_specs=[ANY] * (5 + len(sent)),
        out_specs=INNER_SPECS + [ANY] * len(sent),
        out_shape=INNER_SHAPES + [PAYLOAD] * len(sent),
        input_output_aliases={4: 0} | {5 + i: 5 + i for i in range(len(sent))},
        scratch_shapes=FETCH_SCRATCH + INNER_SCRATCH,
    )(*operands, out, *sent)


def last_kernel(inter, intra, final, low7, k7, p0, *refs):
    starts, (_, out_hbm, rows, sem) = [refs[:4], refs[4:8], refs[8:12]], refs[12:]
    core = lax.axis_index("col") & 1

    def finish(from_before, from_after, row0, row1, up6, k0):
        both0 = dot(k0[...], from_before[: 4 * BS])
        lower7 = dot(k7[...], from_after)
        spill0 = from_before[4 * BS : 5 * BS].astype(F32)
        spill1 = from_before[5 * BS : 6 * BS].astype(F32)
        spill1 += dot(from_before[6 * BS : 7 * BS], p0[:HALF]) + dot(from_before[7 * BS :], p0[HALF:])
        zero = jnp.zeros((BS, HALF), F32)
        rows[0] = row0[...] + shifted(jnp.concatenate([both0[:BS], zero], 1))
        rows[0] += padded(jnp.concatenate([spill0, spill1], 1))
        rows[1] = row1[...] + padded(jnp.concatenate([both0[BS:], zero], 1))
        rows[2] = padded(up6[...]) + shifted(low7[...] + jnp.concatenate([zero, lower7], 1))

    in_chip = jnp.where(late(), final[...], intra[...])
    between = inter[...]
    from_before = jnp.where(core == 0, between, in_chip)
    from_after = jnp.where(core == 0, in_chip[: 4 * BS], between[: 4 * BS])
    for mine in range(3):

        @pl.when(turn() == mine)
        def _(mine=mine):
            finish(from_before, from_after, *starts[mine])

    copies = [
        pltpu.make_async_copy(rows.at[pl.ds(0, 2)], out_hbm.at[pl.ds(0, 2)], sem.at[0]),
        pltpu.make_async_copy(rows.at[2], out_hbm.at[GROUPS - 1], sem.at[1]),
    ]
    for copy in copies:
        copy.start()
    for copy in copies:
        copy.wait()


def last(*args):
    return run(
        last_kernel,
        "last",
        1 << 26,
        in_specs=[VMEM] * 18 + [ANY],
        out_specs=ANY,
        out_shape=OUT,
        input_output_aliases={18: 0},
        scratch_shapes=[vmem(3, BS, BAND, F32), pltpu.SemaphoreType.DMA((2,))],
    )(*args)


def shards(a_blocks, a_index, p_blocks, p_index):
    operands = [pltpu.with_memory_space_constraint(x, pltpu.HBM) for x in (a_index.T, p_index.T, a_blocks, p_blocks)]
    axes = ("row", "col")
    devices, line = lax.axis_size(axes), lax.axis_size("col")
    intra, inter, final, low7, k7, p0, out, *first = edge(operands)
    within = [(d, d ^ 1) for d in range(devices)]
    most = [(s, t) for s, t in within if s % line < line - 2]
    others = [(s, t) for s, t in within if s % line >= line - 2]
    across = [(d, (d + 1 if d % 2 else d - 1) % devices) for d in range(devices)]
    from_most = lax.ppermute(intra, axes, most)
    out, *second, inter, final = inner(1, operands, out, inter, final)
    from_across = lax.ppermute(inter, axes, across)
    from_final = lax.ppermute(final, axes, others)
    out, *third = inner(2, operands, out)
    return last(from_across, from_most, from_final, low7, k7, p0, *first, *second, *third, out)


def solution(mesh):
    blocks = P(("row", "col"), None, None)
    index = P(("row", "col"), None)
    return jax.shard_map(
        shards, mesh=mesh, in_specs=(blocks, index, blocks, index), out_specs=blocks, check_vma=False
    )
```

```python
import functools

import jax
import jax.numpy as jnp
from jax import lax
from jax.experimental import pallas as pl
from jax.experimental.pallas import tpu as pltpu
from jax.sharding import PartitionSpec as P

BS = 64
KA = 8
RATIO = 4
GROUPS = 8
ROWS = RATIO * GROUPS
HALF = 2 * BS
WIDE = 4 * BS
BAND = 5 * BS
F32, BF16 = jnp.float32, jnp.bfloat16
SMEM = pl.BlockSpec(memory_space=pltpu.SMEM)
VMEM = pl.BlockSpec(memory_space=pltpu.VMEM)
ANY = pl.BlockSpec(memory_space=pl.ANY)


def low_half(rows):
    return lax.broadcasted_iota(jnp.int32, (rows, HALF), 1) < BS


def dot(x, y):
    return jnp.dot(x, y, preferred_element_type=F32)


def dot_rows(x, y):
    return lax.dot_general(x, y, (((0,), (0,)), ((), ())), preferred_element_type=F32)


def pair(p_idx, row, block):
    first = ((p_idx[0, row] - row // RATIO) & 1).astype(F32)
    second = ((p_idx[1, row] - row // RATIO) & 1).astype(F32)
    low = low_half(BS)
    x = block.astype(F32)
    y = pltpu.roll(x, BS, 1)
    here = x * jnp.where(low, 1.0 - first, second) + y * jnp.where(low, 1.0 - second, first)
    there = y * jnp.where(low, second, 1.0 - first) + x * jnp.where(low, first, 1.0 - second)
    return here.astype(BF16), there


def centred(there):
    low = low_half(BS)
    zero = jnp.zeros_like(there)
    return jnp.concatenate([jnp.where(low, zero, there), jnp.where(low, there, zero)], 1).astype(BF16)


def column(a_idx, k, row):
    return row + ((a_idx[k, row] - row + RATIO) & 15)


def spread(a_row, places):
    low = low_half(BS)
    tiles = [jnp.zeros((BS, HALF), F32)] * 2
    for j in range(KA // 2):
        x = a_row[:, j * HALF : (j + 1) * HALF].astype(F32)
        y = pltpu.roll(x, BS, 1)
        for blocks, at in ((x, (2 * j, 2 * j + 1)), (y, (2 * j + 1, 2 * j))):
            place = jnp.where(low, places[at[0]], places[at[1]])
            for t in range(2):
                wanted = jnp.where(low, 2 * t, 2 * t + 1)
                tiles[t] = tiles[t] + jnp.where(place == wanted, blocks, 0.0)
    return jnp.concatenate(tiles, 1).astype(BF16)


def shifted(x):
    return pltpu.roll(jnp.concatenate([x, jnp.zeros((BS, HALF), F32)], 1), BS, 1)[:, :BAND]


def padded(x):
    return jnp.concatenate([x, jnp.zeros((BS, BS), F32)], 1)


def edge_body(a_idx, p_idx, a_last, p_ref, wait_rows, intra, inter, final, low7, k7, p0, table, p7, parts, halos):
    first = ROWS - 2 * RATIO
    zero = jnp.zeros((BS, HALF), BF16)
    table[2 * RATIO] = jnp.zeros((BS, WIDE), BF16)

    for i in range(RATIO):
        here, there = pair(p_idx, first + RATIO + i, p_ref[first + RATIO + i])
        table[RATIO + i] = centred(there)
        p7[i] = here
        here, _ = pair(p_idx, first + i, p_ref[first + i])
        table[i] = jnp.concatenate([here, zero], 1)
        here, _ = pair(p_idx, i, p_ref[i])
        p0[i] = here

    last = p7[...].reshape(4 * BS, HALF)
    turned = last.T
    wait_rows()

    for i in range(RATIO):
        row = ROWS - RATIO + i
        places = [column(a_idx, k, row) - RATIO - first for k in range(KA)]
        weights = jnp.concatenate([table[jnp.minimum(place, 2 * RATIO)] for place in places], 0)
        parts[i] = dot(a_last[i], weights).astype(BF16)
        halos[i] = spread(a_last[i], [place - 2 * RATIO for place in places])

    factor = dot(turned, halos[...].reshape(4 * BS, WIDE)).astype(BF16)
    tiles = dot(turned, parts[...].reshape(4 * BS, WIDE))
    low7[...] = tiles[:BS]
    k7[...] = factor[:BS]
    spill = tiles[BS:].astype(BF16)
    down = jnp.concatenate([p0[...].reshape(4 * BS, HALF), jnp.zeros((4 * BS, HALF), BF16)], 0)
    up = jnp.concatenate([last, spill[:, :HALF], spill[:, HALF:], factor[BS:, :HALF], factor[BS:, HALF:]], 0)
    second = lax.axis_index("col") & 1 == 1
    inter[...] = jnp.where(second, up, down)
    in_chip = jnp.where(second, down, up)
    intra[...] = in_chip
    final[...] = in_chip


def inner_body(a_idx, p_idx, a_ref, p_ref, wait_rows, out_hbm, rows, k0, table, pairs, products, out_sem):
    zero = jnp.zeros((BS, HALF), BF16)
    table[3 * ROWS] = jnp.zeros((BS, WIDE), BF16)

    for g in range(GROUPS):
        for i in range(RATIO):
            row = g * RATIO + i
            here, there = pair(p_idx, row, p_ref[row])
            table[row] = jnp.concatenate([here, zero], 1)
            table[ROWS + row] = centred(there)
            table[2 * ROWS + row] = jnp.concatenate([zero, here], 1)
            pairs[g, i * BS : (i + 1) * BS] = here

    wait_rows()

    def group(g):
        for i in range(RATIO):
            row = g * RATIO + i
            blocks = []
            for k in range(KA):
                at = column(a_idx, k, row)
                place = jnp.where(at < RATIO, 3 * ROWS, (at // RATIO - g) * ROWS + at - RATIO)
                blocks.append(table[place])
            products[g, i * BS : (i + 1) * BS] = dot(a_ref[row], jnp.concatenate(blocks, 0)).astype(BF16)

    for g in range(GROUPS - 1):
        group(g)
    before = None
    for g in range(GROUPS - 1):
        both = dot_rows(pairs[g], products[g])
        row = shifted(both[:BS])
        rows[g] = row if g == 0 else row + padded(before)
        before = both[BS:]
    rows[GROUPS - 1] = padded(before)
    whole = pl.ds(2, GROUPS - 3)
    copy = pltpu.make_async_copy(rows.at[whole], out_hbm.at[whole], out_sem)
    copy.start()
    h0 = jnp.concatenate([spread(a_ref[i], [column(a_idx, k, i) for k in range(KA)]) for i in range(RATIO)], 0)
    k0[...] = dot_rows(pairs[0], h0).astype(BF16)
    copy.wait()


def turn():
    return jnp.where(jnp.logical_and(lax.axis_index("col") == 0, lax.axis_index("row") > 0), 0, 1)


def late():
    return lax.axis_index("col") >= lax.axis_size("col") - 2


vmem = lambda *shape: pltpu.VMEM(shape[:-1], shape[-1])
PAYLOAD = vmem(8 * BS, HALF, BF16)
EDGE_SHAPES = [PAYLOAD] * 3 + [vmem(BS, WIDE, F32), vmem(BS, WIDE, BF16), vmem(RATIO, BS, HALF, BF16)]
OUT = jax.ShapeDtypeStruct((GROUPS, BS, BAND), F32)
INNER_SHAPES = [OUT, vmem(GROUPS, BS, BAND, F32), vmem(HALF, WIDE, BF16)]
INNER_SPECS = [ANY] + [VMEM] * 2
FETCH_SCRATCH = [
    pltpu.SMEM((KA, ROWS), jnp.int32),
    pltpu.SMEM((2, ROWS), jnp.int32),
    vmem(ROWS, BS, KA * BS, BF16),
    vmem(ROWS, BS, HALF, BF16),
    pltpu.SemaphoreType.DMA((4,)),
]
INNER_SCRATCH = [
    vmem(3 * ROWS + 1, BS, WIDE, BF16),
    vmem(GROUPS, 4 * BS, HALF, BF16),
    vmem(GROUPS - 1, 4 * BS, WIDE, BF16),
    pltpu.SemaphoreType.DMA,
]


def run(kernel, name, flops, **settings):
    return pl.pallas_call(
        kernel,
        compiler_params=pltpu.CompilerParams(vmem_limit_bytes=20 << 20),
        cost_estimate=pl.CostEstimate(flops=flops, bytes_accessed=1 << 20, transcendentals=0),
        name=name,
        **settings,
    )


def fetch(sources, places, sem):
    copies = [pltpu.make_async_copy(x, y, sem.at[n]) for n, (x, y) in enumerate(zip(sources, places, strict=True))]
    for copy in copies:
        copy.start()
    return copies


def inner_groups(sources, inner_out, scratch):
    a_idx, p_idx, a_ref, p_ref, sem, *rest = scratch
    a_idx_hbm, p_idx_hbm, a_hbm, p_hbm = sources
    copies = fetch((p_hbm, a_idx_hbm, p_idx_hbm, a_hbm), (p_ref, a_idx, p_idx, a_ref), sem)
    for copy in copies[:3]:
        copy.wait()
    inner_body(a_idx, p_idx, a_ref, p_ref, copies[3].wait, *inner_out, *rest)


def edge_kernel(a_idx_hbm, p_idx_hbm, a_hbm, p_hbm, *refs):
    edge_out, (a_idx, p_idx, a_last, p_ends, sem, *rest) = refs[:6], refs[6:]
    near = pl.ds(0, RATIO)
    far = pl.ds(ROWS - 2 * RATIO, 2 * RATIO)
    copies = fetch(
        (p_idx_hbm, a_idx_hbm, p_hbm.at[far], p_hbm.at[near], a_hbm.at[pl.ds(ROWS - RATIO, RATIO)]),
        (p_idx, a_idx, p_ends.at[far], p_ends.at[near], a_last),
        sem,
    )
    for copy in copies[:4]:
        copy.wait()
    edge_body(a_idx, p_idx, a_last, p_ends, copies[4].wait, *edge_out, *rest)


def edge(operands):
    return run(
        edge_kernel,
        "edge",
        1 << 28,
        in_specs=[ANY] * 4,
        out_specs=[VMEM] * 6,
        out_shape=EDGE_SHAPES,
        scratch_shapes=FETCH_SCRATCH[:2]
        + [
            vmem(RATIO, BS, KA * BS, BF16),
            vmem(ROWS, BS, HALF, BF16),
            pltpu.SemaphoreType.DMA((5,)),
            vmem(2 * RATIO + 1, BS, WIDE, BF16),
            vmem(RATIO, BS, HALF, BF16),
            vmem(RATIO, BS, WIDE, BF16),
            vmem(RATIO, BS, WIDE, BF16),
        ],
    )(*operands)


def inner_kernel(mine, given, a_idx_hbm, p_idx_hbm, a_hbm, p_hbm, *refs):
    inner_out = refs[given : given + 3]
    a_idx, p_idx, a_ref, p_ref, sem, *rest = refs[-9:]

    @pl.when(turn() == mine)
    def _():
        copies = fetch((p_hbm, a_idx_hbm, p_idx_hbm, a_hbm), (p_ref, a_idx, p_idx, a_ref), sem)
        for copy in copies[:3]:
            copy.wait()
        inner_body(a_idx, p_idx, a_ref, p_ref, copies[3].wait, *inner_out, *rest)


def inner(mine, operands, out=(), sent=()):
    given = len(out) + len(sent)
    return run(
        functools.partial(inner_kernel, mine, given),
        "inner",
        1 << 30,
        in_specs=[ANY] * (4 + given),
        out_specs=INNER_SPECS + [ANY] * len(sent),
        out_shape=INNER_SHAPES + [PAYLOAD] * len(sent),
        input_output_aliases={4: 0} if out else {4 + i: 3 + i for i in range(len(sent))},
        scratch_shapes=FETCH_SCRATCH + INNER_SCRATCH,
    )(*operands, *out, *sent)


def last_kernel(inter, intra, final, low7, k7, p0, *refs):
    starts, (_, out_hbm, rows, sem) = [refs[:2], refs[2:4]], refs[4:]
    core = lax.axis_index("col") & 1

    def finish(from_before, from_after, given, k0):
        both0 = dot(k0[...], from_before[: 4 * BS])
        lower7 = dot(k7[...], from_after)
        spill0 = from_before[4 * BS : 5 * BS].astype(F32)
        spill1 = from_before[5 * BS : 6 * BS].astype(F32)
        own = p0[...].reshape(4 * BS, HALF)
        spill1 += dot(from_before[6 * BS : 7 * BS], own[:HALF]) + dot(from_before[7 * BS :], own[HALF:])
        zero = jnp.zeros((BS, HALF), F32)
        rows[0] = given[0] + shifted(jnp.concatenate([both0[:BS], zero], 1))
        rows[0] += padded(jnp.concatenate([spill0, spill1], 1))
        rows[1] = given[1] + padded(jnp.concatenate([both0[BS:], zero], 1))
        rows[2] = given[GROUPS - 1] + shifted(low7[...] + jnp.concatenate([zero, lower7], 1))

    in_chip = jnp.where(late(), final[...], intra[...])
    between = inter[...]
    from_before = jnp.where(core == 0, between, in_chip)
    from_after = jnp.where(core == 0, in_chip[: 4 * BS], between[: 4 * BS])
    for mine in range(2):

        @pl.when(turn() == mine)
        def _(mine=mine):
            finish(from_before, from_after, *starts[mine])

    copies = [
        pltpu.make_async_copy(rows.at[pl.ds(0, 2)], out_hbm.at[pl.ds(0, 2)], sem.at[0]),
        pltpu.make_async_copy(rows.at[2], out_hbm.at[GROUPS - 1], sem.at[1]),
    ]
    for copy in copies:
        copy.start()
    for copy in copies:
        copy.wait()


def last(*args):
    return run(
        last_kernel,
        "last",
        1 << 26,
        in_specs=[VMEM] * 10 + [ANY],
        out_specs=ANY,
        out_shape=OUT,
        input_output_aliases={10: 0},
        scratch_shapes=[vmem(3, BS, BAND, F32), pltpu.SemaphoreType.DMA((2,))],
    )(*args)


def shards(a_blocks, a_index, p_blocks, p_index):
    operands = [pltpu.with_memory_space_constraint(x, pltpu.HBM) for x in (a_index.T, p_index.T, a_blocks, p_blocks)]
    axes = ("row", "col")
    devices, line = lax.axis_size(axes), lax.axis_size("col")
    intra, inter, final, low7, k7, p0 = edge(operands)
    within = [(d, d ^ 1) for d in range(devices)]
    most = [(s, t) for s, t in within if s % line < line - 2]
    others = [(s, t) for s, t in within if s % line >= line - 2]
    across = [(d, (d + 1 if d % 2 else d - 1) % devices) for d in range(devices)]
    from_most = lax.ppermute(intra, axes, most)
    out, *first, inter, final = inner(0, operands, sent=(inter, final))
    from_across = lax.ppermute(inter, axes, across)
    from_final = lax.ppermute(final, axes, others)
    out, *second = inner(1, operands, out=(out,))
    return last(from_across, from_most, from_final, low7, k7, p0, *first, *second, out)


def solution(mesh):
    blocks = P(("row", "col"), None, None)
    index = P(("row", "col"), None)
    return jax.shard_map(
        shards, mesh=mesh, in_specs=(blocks, index, blocks, index), out_specs=blocks, check_vma=False
    )
```

```python
import jax
import jax.numpy as jnp
from jax import lax
from jax.experimental import pallas as pl
from jax.experimental.pallas import tpu as pltpu
from jax.sharding import PartitionSpec as P

BS = 64
KA = 8
RATIO = 4
GROUPS = 8
ROWS = RATIO * GROUPS
HALF = 2 * BS
WIDE = 4 * BS
BAND = 5 * BS
F32, BF16 = jnp.float32, jnp.bfloat16
SMEM = pl.BlockSpec(memory_space=pltpu.SMEM)
VMEM = pl.BlockSpec(memory_space=pltpu.VMEM)
ANY = pl.BlockSpec(memory_space=pl.ANY)


def low_half(rows):
    return lax.broadcasted_iota(jnp.int32, (rows, HALF), 1) < BS


def dot(x, y):
    return jnp.dot(x, y, preferred_element_type=F32)


def dot_rows(x, y):
    return lax.dot_general(x, y, (((0,), (0,)), ((), ())), preferred_element_type=F32)


def pair(p_idx, row, block):
    first = ((p_idx[0, row] - row // RATIO) & 1).astype(F32)
    second = ((p_idx[1, row] - row // RATIO) & 1).astype(F32)
    low = low_half(BS)
    x = block.astype(F32)
    y = pltpu.roll(x, BS, 1)
    here = x * jnp.where(low, 1.0 - first, second) + y * jnp.where(low, 1.0 - second, first)
    there = y * jnp.where(low, second, 1.0 - first) + x * jnp.where(low, first, 1.0 - second)
    return here.astype(BF16), there


def centred(there):
    low = low_half(BS)
    zero = jnp.zeros_like(there)
    return jnp.concatenate([jnp.where(low, zero, there), jnp.where(low, there, zero)], 1).astype(BF16)


def column(a_idx, k, row):
    return row + ((a_idx[k, row] - row + RATIO) & 15)


def spread(a_row, places):
    low = low_half(BS)
    tiles = [jnp.zeros((BS, HALF), F32)] * 2
    for j in range(KA // 2):
        x = a_row[:, j * HALF : (j + 1) * HALF].astype(F32)
        y = pltpu.roll(x, BS, 1)
        for blocks, at in ((x, (2 * j, 2 * j + 1)), (y, (2 * j + 1, 2 * j))):
            place = jnp.where(low, places[at[0]], places[at[1]])
            for t in range(2):
                wanted = jnp.where(low, 2 * t, 2 * t + 1)
                tiles[t] = tiles[t] + jnp.where(place == wanted, blocks, 0.0)
    return jnp.concatenate(tiles, 1).astype(BF16)


def shifted(x):
    return pltpu.roll(jnp.concatenate([x, jnp.zeros((BS, HALF), F32)], 1), BS, 1)[:, :BAND]


def padded(x):
    return jnp.concatenate([x, jnp.zeros((BS, BS), F32)], 1)


def edge_body(a_idx, p_idx, a_last, p_ref, wait_rows, intra, inter, final, low7, k7, p0, table, p7, parts, halos):
    first = ROWS - 2 * RATIO
    zero = jnp.zeros((BS, HALF), BF16)
    table[2 * RATIO] = jnp.zeros((BS, WIDE), BF16)

    for i in range(RATIO):
        here, there = pair(p_idx, first + RATIO + i, p_ref[first + RATIO + i])
        table[RATIO + i] = centred(there)
        p7[i] = here
        here, _ = pair(p_idx, first + i, p_ref[first + i])
        table[i] = jnp.concatenate([here, zero], 1)
        here, _ = pair(p_idx, i, p_ref[i])
        p0[i] = here

    last = p7[...].reshape(4 * BS, HALF)
    turned = last.T
    wait_rows()

    for i in range(RATIO):
        row = ROWS - RATIO + i
        places = [column(a_idx, k, row) - RATIO - first for k in range(KA)]
        weights = jnp.concatenate([table[jnp.minimum(place, 2 * RATIO)] for place in places], 0)
        parts[i] = dot(a_last[i], weights).astype(BF16)
        halos[i] = spread(a_last[i], [place - 2 * RATIO for place in places])

    factor = dot(turned, halos[...].reshape(4 * BS, WIDE)).astype(BF16)
    tiles = dot(turned, parts[...].reshape(4 * BS, WIDE))
    low7[...] = tiles[:BS]
    k7[...] = factor[:BS]
    spill = tiles[BS:].astype(BF16)
    down = jnp.concatenate([p0[...].reshape(4 * BS, HALF), jnp.zeros((4 * BS, HALF), BF16)], 0)
    up = jnp.concatenate([last, spill[:, :HALF], spill[:, HALF:], factor[BS:, :HALF], factor[BS:, HALF:]], 0)
    second = lax.axis_index("col") & 1 == 1
    inter[...] = jnp.where(second, up, down)
    in_chip = jnp.where(second, down, up)
    intra[...] = in_chip
    final[...] = in_chip


def inner_body(a_idx, p_idx, a_ref, p_ref, copies, rows, k0, table, pairs, products):
    zero = jnp.zeros((BS, HALF), BF16)
    table[3 * ROWS] = jnp.zeros((BS, WIDE), BF16)
    copies[0].wait()
    for g in range(GROUPS):
        for i in range(RATIO):
            row = g * RATIO + i
            here, there = pair(p_idx, row, p_ref[row])
            table[row] = jnp.concatenate([here, zero], 1)
            table[ROWS + row] = centred(there)
            table[2 * ROWS + row] = jnp.concatenate([zero, here], 1)
            pairs[g, i * BS : (i + 1) * BS] = here

    copies[1].wait()

    def group(g):
        for i in range(RATIO):
            row = g * RATIO + i
            blocks = []
            for k in range(KA):
                at = column(a_idx, k, row)
                place = jnp.where(at < RATIO, 3 * ROWS, (at // RATIO - g) * ROWS + at - RATIO)
                blocks.append(table[place])
            products[g, i * BS : (i + 1) * BS] = dot(a_ref[row], jnp.concatenate(blocks, 0)).astype(BF16)

    for g in range(GROUPS - 1):
        group(g)
    before = None
    for g in range(GROUPS - 1):
        both = dot_rows(pairs[g], products[g])
        row = shifted(both[:BS])
        rows[g] = row if g == 0 else row + padded(before)
        before = both[BS:]
    rows[GROUPS - 1] = padded(before)
    h0 = jnp.concatenate([spread(a_ref[i], [column(a_idx, k, i) for k in range(KA)]) for i in range(RATIO)], 0)
    k0[...] = dot_rows(pairs[0], h0).astype(BF16)


def late():
    return lax.axis_index("col") >= lax.axis_size("col") - 2


vmem = lambda *shape: pltpu.VMEM(shape[:-1], shape[-1])
PAYLOAD = vmem(8 * BS, HALF, BF16)
EDGE_SHAPES = [PAYLOAD] * 3 + [vmem(BS, WIDE, F32), vmem(BS, WIDE, BF16), vmem(RATIO, BS, HALF, BF16)]
OUT = jax.ShapeDtypeStruct((GROUPS, BS, BAND), F32)
FETCH_SCRATCH = [pltpu.SMEM((KA, ROWS), jnp.int32), pltpu.SMEM((2, ROWS), jnp.int32)]


def run(kernel, name, flops, **settings):
    return pl.pallas_call(
        kernel,
        compiler_params=pltpu.CompilerParams(vmem_limit_bytes=20 << 20),
        cost_estimate=pl.CostEstimate(flops=flops, bytes_accessed=1 << 20, transcendentals=0),
        name=name,
        **settings,
    )


def fetch(sources, places, sem):
    copies = [pltpu.make_async_copy(x, y, sem.at[n]) for n, (x, y) in enumerate(zip(sources, places, strict=True))]
    for copy in copies:
        copy.start()
    return copies


def inner_groups(sources, inner_out, scratch):
    a_idx, p_idx, a_ref, p_ref, sem, *rest = scratch
    a_idx_hbm, p_idx_hbm, a_hbm, p_hbm = sources
    copies = fetch((p_hbm, a_idx_hbm, p_idx_hbm, a_hbm), (p_ref, a_idx, p_idx, a_ref), sem)
    for copy in copies[:3]:
        copy.wait()
    inner_body(a_idx, p_idx, a_ref, p_ref, copies[3].wait, *inner_out, *rest)


def edge_kernel(a_idx_hbm, p_idx_hbm, a_hbm, p_hbm, *refs):
    edge_out, (a_idx, p_idx, a_last, p_ends, sem, *rest) = refs[:6], refs[6:]
    near = pl.ds(0, RATIO)
    far = pl.ds(ROWS - 2 * RATIO, 2 * RATIO)
    copies = fetch(
        (p_idx_hbm, a_idx_hbm, p_hbm.at[far], p_hbm.at[near], a_hbm.at[pl.ds(ROWS - RATIO, RATIO)]),
        (p_idx, a_idx, p_ends.at[far], p_ends.at[near], a_last),
        sem,
    )
    for copy in copies[:4]:
        copy.wait()
    edge_body(a_idx, p_idx, a_last, p_ends, copies[4].wait, *edge_out, *rest)


def edge(operands):
    return run(
        edge_kernel,
        "edge",
        1 << 28,
        in_specs=[ANY] * 4,
        out_specs=[VMEM] * 6,
        out_shape=EDGE_SHAPES,
        scratch_shapes=FETCH_SCRATCH[:2]
        + [
            vmem(RATIO, BS, KA * BS, BF16),
            vmem(ROWS, BS, HALF, BF16),
            pltpu.SemaphoreType.DMA((5,)),
            vmem(2 * RATIO + 1, BS, WIDE, BF16),
            vmem(RATIO, BS, HALF, BF16),
            vmem(RATIO, BS, WIDE, BF16),
            vmem(RATIO, BS, WIDE, BF16),
        ],
    )(*operands)


def inner_kernel(a_idx_from, p_idx_from, a_ref, p_ref, *refs):
    inner_out, (a_idx, p_idx, sem, *rest) = refs[:2], refs[2:]
    copies = fetch((p_idx_from, a_idx_from), (p_idx, a_idx), sem)
    inner_body(a_idx, p_idx, a_ref, p_ref, copies, *inner_out, *rest)


def inner(operands):
    return run(
        inner_kernel,
        "inner",
        1 << 30,
        in_specs=[VMEM] * 4,
        out_specs=[VMEM, VMEM],
        out_shape=[vmem(GROUPS, BS, BAND, F32), vmem(HALF, WIDE, BF16)],
        scratch_shapes=FETCH_SCRATCH[:2]
        + [
            pltpu.SemaphoreType.DMA((2,)),
            vmem(3 * ROWS + 1, BS, WIDE, BF16),
            vmem(GROUPS, 4 * BS, HALF, BF16),
            vmem(GROUPS - 1, 4 * BS, WIDE, BF16),
        ],
    )(*operands)


def last_kernel(intra, inter, final, low7, k7, p0, given, k0, out_hbm, rows, sem):
    def out_copy(source, at, size, n):
        return pltpu.make_async_copy(source, out_hbm.at[pl.ds(at, size)], sem.at[n])

    whole = out_copy(given.at[pl.ds(2, GROUPS - 3)], 2, GROUPS - 3, 0)
    whole.start()
    core = lax.axis_index("col") & 1
    in_chip = jnp.where(late(), final[...], intra[...])
    between = inter[...]
    from_before = jnp.where(core == 0, between, in_chip)
    from_after = jnp.where(core == 0, in_chip[: 4 * BS], between[: 4 * BS])
    both0 = dot(k0[...], from_before[: 4 * BS])
    lower7 = dot(k7[...], from_after)
    spill0 = from_before[4 * BS : 5 * BS].astype(F32)
    spill1 = from_before[5 * BS : 6 * BS].astype(F32)
    own = p0[...].reshape(4 * BS, HALF)
    spill1 += dot(from_before[6 * BS : 7 * BS], own[:HALF]) + dot(from_before[7 * BS :], own[HALF:])
    zero = jnp.zeros((BS, HALF), F32)
    rows[0] = given[0] + shifted(jnp.concatenate([both0[:BS], zero], 1)) + padded(jnp.concatenate([spill0, spill1], 1))
    rows[1] = given[1] + padded(jnp.concatenate([both0[BS:], zero], 1))
    rows[2] = given[GROUPS - 1] + shifted(low7[...] + jnp.concatenate([zero, lower7], 1))
    copies = [out_copy(rows.at[pl.ds(0, 2)], 0, 2, 1), out_copy(rows.at[pl.ds(2, 1)], GROUPS - 1, 1, 2)]
    for copy in copies:
        copy.start()
    for copy in [whole] + copies:
        copy.wait()


def last(*args):
    return run(
        last_kernel,
        "last",
        1 << 26,
        in_specs=[VMEM] * 8,
        out_specs=ANY,
        out_shape=OUT,
        scratch_shapes=[vmem(3, BS, BAND, F32), pltpu.SemaphoreType.DMA((3,))],
    )(*args)


def shards(a_blocks, a_index, p_blocks, p_index):
    operands = a_index.T, p_index.T, a_blocks, p_blocks
    in_hbm = [pltpu.with_memory_space_constraint(x, pltpu.HBM) for x in operands]
    in_vmem = [pltpu.with_memory_space_constraint(x, pltpu.VMEM) for x in operands]
    axes = ("row", "col")
    devices, line = lax.axis_size(axes), lax.axis_size("col")
    intra, inter, final, low7, k7, p0 = edge(in_hbm)
    within = [(d, d ^ 1) for d in range(devices)]
    most = [(s, t) for s, t in within if s % line < line - 2]
    others = [(s, t) for s, t in within if s % line >= line - 2]
    across = [(d, (d + 1 if d % 2 else d - 1) % devices) for d in range(devices)]
    from_most = lax.ppermute(intra, axes, most)
    from_across = lax.ppermute(inter, axes, across)
    from_final = lax.ppermute(final, axes, others)
    rows, k0 = inner(in_vmem)
    return last(from_most, from_across, from_final, low7, k7, p0, rows, k0)


def solution(mesh):
    blocks = P(("row", "col"), None, None)
    index = P(("row", "col"), None)
    return jax.shard_map(
        shards, mesh=mesh, in_specs=(blocks, index, blocks, index), out_specs=blocks, check_vma=False
    )
```

```python
import functools

import jax
import jax.numpy as jnp
from jax import lax
from jax.experimental import pallas as pl
from jax.experimental.pallas import tpu as pltpu
from jax.sharding import PartitionSpec as P

BS = 64
KA = 8
RATIO = 4
GROUPS = 8
ROWS = RATIO * GROUPS
HALF = 2 * BS
WIDE = 4 * BS
BAND = 5 * BS
F32, BF16 = jnp.float32, jnp.bfloat16
SMEM = pl.BlockSpec(memory_space=pltpu.SMEM)
VMEM = pl.BlockSpec(memory_space=pltpu.VMEM)
ANY = pl.BlockSpec(memory_space=pl.ANY)


def low_half(rows):
    return lax.broadcasted_iota(jnp.int32, (rows, HALF), 1) < BS


def dot(x, y):
    return jnp.dot(x, y, preferred_element_type=F32)


def dot_rows(x, y):
    return lax.dot_general(x, y, (((0,), (0,)), ((), ())), preferred_element_type=F32)


def pair(p_idx, row, block):
    first = ((p_idx[0, row] - row // RATIO) & 1).astype(F32)
    second = ((p_idx[1, row] - row // RATIO) & 1).astype(F32)
    low = low_half(BS)
    x = block.astype(F32)
    y = pltpu.roll(x, BS, 1)
    here = x * jnp.where(low, 1.0 - first, second) + y * jnp.where(low, 1.0 - second, first)
    there = y * jnp.where(low, second, 1.0 - first) + x * jnp.where(low, first, 1.0 - second)
    return here.astype(BF16), there


def centred(there):
    low = low_half(BS)
    zero = jnp.zeros_like(there)
    return jnp.concatenate([jnp.where(low, zero, there), jnp.where(low, there, zero)], 1).astype(BF16)


def column(a_idx, k, row):
    return row + ((a_idx[k, row] - row + RATIO) & 15)


def spread(a_row, places):
    low = low_half(BS)
    tiles = [jnp.zeros((BS, HALF), F32)] * 2
    for j in range(KA // 2):
        x = a_row[:, j * HALF : (j + 1) * HALF].astype(F32)
        y = pltpu.roll(x, BS, 1)
        for blocks, at in ((x, (2 * j, 2 * j + 1)), (y, (2 * j + 1, 2 * j))):
            place = jnp.where(low, places[at[0]], places[at[1]])
            for t in range(2):
                wanted = jnp.where(low, 2 * t, 2 * t + 1)
                tiles[t] = tiles[t] + jnp.where(place == wanted, blocks, 0.0)
    return jnp.concatenate(tiles, 1).astype(BF16)


def shifted(x):
    return pltpu.roll(jnp.concatenate([x, jnp.zeros((BS, HALF), F32)], 1), BS, 1)[:, :BAND]


def padded(x):
    return jnp.concatenate([x, jnp.zeros((BS, BS), F32)], 1)


def edge_body(a_idx, p_idx, a_last, p_ref, wait_rows, intra, inter, final, low7, k7, p0, table, p7, parts, halos):
    first = ROWS - 2 * RATIO
    zero = jnp.zeros((BS, HALF), BF16)
    table[2 * RATIO] = jnp.zeros((BS, WIDE), BF16)

    for i in range(RATIO):
        here, there = pair(p_idx, first + RATIO + i, p_ref[first + RATIO + i])
        table[RATIO + i] = centred(there)
        p7[i] = here
        here, _ = pair(p_idx, first + i, p_ref[first + i])
        table[i] = jnp.concatenate([here, zero], 1)
        here, _ = pair(p_idx, i, p_ref[i])
        p0[i] = here

    last = p7[...].reshape(4 * BS, HALF)
    turned = last.T
    wait_rows()

    for i in range(RATIO):
        row = ROWS - RATIO + i
        places = [column(a_idx, k, row) - RATIO - first for k in range(KA)]
        weights = jnp.concatenate([table[jnp.minimum(place, 2 * RATIO)] for place in places], 0)
        parts[i] = dot(a_last[i], weights).astype(BF16)
        halos[i] = spread(a_last[i], [place - 2 * RATIO for place in places])

    factor = dot(turned, halos[...].reshape(4 * BS, WIDE)).astype(BF16)
    tiles = dot(turned, parts[...].reshape(4 * BS, WIDE))
    low7[...] = tiles[:BS]
    k7[...] = factor[:BS]
    spill = tiles[BS:].astype(BF16)
    down = jnp.concatenate([p0[...].reshape(4 * BS, HALF), jnp.zeros((4 * BS, HALF), BF16)], 0)
    up = jnp.concatenate([last, spill[:, :HALF], spill[:, HALF:], factor[BS:, :HALF], factor[BS:, HALF:]], 0)
    second = lax.axis_index("col") & 1 == 1
    inter[...] = jnp.where(second, up, down)
    in_chip = jnp.where(second, down, up)
    intra[...] = in_chip
    final[...] = in_chip


def inner_body(a_idx, p_idx, a_ref, p_ref, copies, rows, k0, table, pairs, products):
    zero = jnp.zeros((BS, HALF), BF16)
    table[3 * ROWS] = jnp.zeros((BS, WIDE), BF16)
    copies[0].wait()
    for g in range(GROUPS):
        for i in range(RATIO):
            row = g * RATIO + i
            here, there = pair(p_idx, row, p_ref[row])
            table[row] = jnp.concatenate([here, zero], 1)
            table[ROWS + row] = centred(there)
            table[2 * ROWS + row] = jnp.concatenate([zero, here], 1)
            pairs[g, i * BS : (i + 1) * BS] = here

    copies[1].wait()

    def group(g):
        for i in range(RATIO):
            row = g * RATIO + i
            blocks = []
            for k in range(KA):
                at = column(a_idx, k, row)
                place = jnp.where(at < RATIO, 3 * ROWS, (at // RATIO - g) * ROWS + at - RATIO)
                blocks.append(table[place])
            products[g, i * BS : (i + 1) * BS] = dot(a_ref[row], jnp.concatenate(blocks, 0)).astype(BF16)

    for g in range(GROUPS - 1):
        group(g)
    before = None
    for g in range(GROUPS - 1):
        both = dot_rows(pairs[g], products[g])
        row = shifted(both[:BS])
        rows[g] = row if g == 0 else row + padded(before)
        before = both[BS:]
    rows[GROUPS - 1] = padded(before)
    h0 = jnp.concatenate([spread(a_ref[i], [column(a_idx, k, i) for k in range(KA)]) for i in range(RATIO)], 0)
    k0[...] = dot_rows(pairs[0], h0).astype(BF16)


def turn():
    return jnp.where(jnp.logical_and(lax.axis_index("col") == 0, lax.axis_index("row") > 0), 0, 1)


def late():
    return lax.axis_index("col") >= lax.axis_size("col") - 2


vmem = lambda *shape: pltpu.VMEM(shape[:-1], shape[-1])
PAYLOAD = vmem(8 * BS, HALF, BF16)
EDGE_SHAPES = [PAYLOAD] * 3 + [vmem(BS, WIDE, F32), vmem(BS, WIDE, BF16), vmem(RATIO, BS, HALF, BF16)]
OUT = jax.ShapeDtypeStruct((GROUPS, BS, BAND), F32)
FETCH_SCRATCH = [pltpu.SMEM((KA, ROWS), jnp.int32), pltpu.SMEM((2, ROWS), jnp.int32)]


def run(kernel, name, flops, **settings):
    return pl.pallas_call(
        kernel,
        compiler_params=pltpu.CompilerParams(vmem_limit_bytes=20 << 20),
        cost_estimate=pl.CostEstimate(flops=flops, bytes_accessed=1 << 20, transcendentals=0),
        name=name,
        **settings,
    )


def fetch(sources, places, sem):
    copies = [pltpu.make_async_copy(x, y, sem.at[n]) for n, (x, y) in enumerate(zip(sources, places, strict=True))]
    for copy in copies:
        copy.start()
    return copies


def inner_groups(sources, inner_out, scratch):
    a_idx, p_idx, a_ref, p_ref, sem, *rest = scratch
    a_idx_hbm, p_idx_hbm, a_hbm, p_hbm = sources
    copies = fetch((p_hbm, a_idx_hbm, p_idx_hbm, a_hbm), (p_ref, a_idx, p_idx, a_ref), sem)
    for copy in copies[:3]:
        copy.wait()
    inner_body(a_idx, p_idx, a_ref, p_ref, copies[3].wait, *inner_out, *rest)


def edge_kernel(a_idx_hbm, p_idx_hbm, a_hbm, p_hbm, *refs):
    edge_out, (a_idx, p_idx, a_last, p_ends, sem, *rest) = refs[:6], refs[6:]
    near = pl.ds(0, RATIO)
    far = pl.ds(ROWS - 2 * RATIO, 2 * RATIO)
    copies = fetch(
        (p_idx_hbm, a_idx_hbm, p_hbm.at[far], p_hbm.at[near], a_hbm.at[pl.ds(ROWS - RATIO, RATIO)]),
        (p_idx, a_idx, p_ends.at[far], p_ends.at[near], a_last),
        sem,
    )
    for copy in copies[:4]:
        copy.wait()
    edge_body(a_idx, p_idx, a_last, p_ends, copies[4].wait, *edge_out, *rest)


def edge(operands):
    return run(
        edge_kernel,
        "edge",
        1 << 28,
        in_specs=[ANY] * 4,
        out_specs=[VMEM] * 6,
        out_shape=EDGE_SHAPES,
        scratch_shapes=FETCH_SCRATCH[:2]
        + [
            vmem(RATIO, BS, KA * BS, BF16),
            vmem(ROWS, BS, HALF, BF16),
            pltpu.SemaphoreType.DMA((5,)),
            vmem(2 * RATIO + 1, BS, WIDE, BF16),
            vmem(RATIO, BS, HALF, BF16),
            vmem(RATIO, BS, WIDE, BF16),
            vmem(RATIO, BS, WIDE, BF16),
        ],
    )(*operands)


def inner_kernel(mine, handed, a_idx_from, p_idx_from, a_ref, p_ref, *refs):
    inner_out = refs[handed : handed + 2]
    a_idx, p_idx, sem, *rest = refs[-6:]

    @pl.when(turn() == mine)
    def _():
        copies = fetch((p_idx_from, a_idx_from), (p_idx, a_idx), sem)
        inner_body(a_idx, p_idx, a_ref, p_ref, copies, *inner_out, *rest)


def inner(mine, operands, *sent):
    return run(
        functools.partial(inner_kernel, mine, len(sent)),
        "inner",
        1 << 30,
        in_specs=[VMEM] * 4 + [ANY] * len(sent),
        out_specs=[VMEM, VMEM] + [ANY] * len(sent),
        out_shape=[vmem(GROUPS, BS, BAND, F32), vmem(HALF, WIDE, BF16)] + [PAYLOAD] * len(sent),
        input_output_aliases={4 + i: 2 + i for i in range(len(sent))},
        scratch_shapes=FETCH_SCRATCH
        + [
            pltpu.SemaphoreType.DMA((2,)),
            vmem(3 * ROWS + 1, BS, WIDE, BF16),
            vmem(GROUPS, 4 * BS, HALF, BF16),
            vmem(GROUPS - 1, 4 * BS, WIDE, BF16),
        ],
    )(*operands, *sent)


def last_kernel(intra, inter, final, low7, k7, p0, *refs):
    starts, (out_hbm, rows, sem) = [refs[:2], refs[2:4]], refs[4:]

    def out_copy(source, at, size, n):
        return pltpu.make_async_copy(source, out_hbm.at[pl.ds(at, size)], sem.at[n])

    def finish(given, k0):
        whole = out_copy(given.at[pl.ds(2, GROUPS - 3)], 2, GROUPS - 3, 0)
        whole.start()
        core = lax.axis_index("col") & 1
        in_chip = jnp.where(late(), final[...], intra[...])
        between = inter[...]
        from_before = jnp.where(core == 0, between, in_chip)
        from_after = jnp.where(core == 0, in_chip[: 4 * BS], between[: 4 * BS])
        both0 = dot(k0[...], from_before[: 4 * BS])
        lower7 = dot(k7[...], from_after)
        spill0 = from_before[4 * BS : 5 * BS].astype(F32)
        spill1 = from_before[5 * BS : 6 * BS].astype(F32)
        own = p0[...].reshape(4 * BS, HALF)
        spill1 += dot(from_before[6 * BS : 7 * BS], own[:HALF]) + dot(from_before[7 * BS :], own[HALF:])
        zero = jnp.zeros((BS, HALF), F32)
        rows[0] = given[0] + shifted(jnp.concatenate([both0[:BS], zero], 1)) + padded(jnp.concatenate([spill0, spill1], 1))
        rows[1] = given[1] + padded(jnp.concatenate([both0[BS:], zero], 1))
        rows[2] = given[GROUPS - 1] + shifted(low7[...] + jnp.concatenate([zero, lower7], 1))
        copies = [out_copy(rows.at[pl.ds(0, 2)], 0, 2, 1), out_copy(rows.at[pl.ds(2, 1)], GROUPS - 1, 1, 2)]
        for copy in copies:
            copy.start()
        for copy in [whole] + copies:
            copy.wait()

    for mine in range(2):

        @pl.when(turn() == mine)
        def _(mine=mine):
            finish(*starts[mine])


def last(*args):
    return run(
        last_kernel,
        "last",
        1 << 26,
        in_specs=[VMEM] * 10,
        out_specs=ANY,
        out_shape=OUT,
        scratch_shapes=[vmem(3, BS, BAND, F32), pltpu.SemaphoreType.DMA((3,))],
    )(*args)


def shards(a_blocks, a_index, p_blocks, p_index):
    operands = a_index.T, p_index.T, a_blocks, p_blocks
    in_hbm = [pltpu.with_memory_space_constraint(x, pltpu.HBM) for x in operands]
    in_vmem = [pltpu.with_memory_space_constraint(x, pltpu.VMEM) for x in operands]
    axes = ("row", "col")
    devices, line = lax.axis_size(axes), lax.axis_size("col")
    intra, inter, final, low7, k7, p0 = edge(in_hbm)
    within = [(d, d ^ 1) for d in range(devices)]
    most = [(s, t) for s, t in within if s % line < line - 2]
    others = [(s, t) for s, t in within if s % line >= line - 2]
    across = [(d, (d + 1 if d % 2 else d - 1) % devices) for d in range(devices)]
    from_most = lax.ppermute(intra, axes, most)
    *first, inter, final = inner(0, in_vmem, inter, final)
    from_across = lax.ppermute(inter, axes, across)
    from_final = lax.ppermute(final, axes, others)
    second = inner(1, in_vmem)
    return last(from_most, from_across, from_final, low7, k7, p0, *first, *second)


def solution(mesh):
    blocks = P(("row", "col"), None, None)
    index = P(("row", "col"), None)
    return jax.shard_map(
        shards, mesh=mesh, in_specs=(blocks, index, blocks, index), out_specs=blocks, check_vma=False
    )
```

```python
import jax
import jax.numpy as jnp
from jax import lax
from jax.experimental import pallas as pl
from jax.experimental.pallas import tpu as pltpu
from jax.sharding import PartitionSpec as P

BS = 64
KA = 8
RATIO = 4
GROUPS = 8
ROWS = RATIO * GROUPS
HALF = 2 * BS
WIDE = 4 * BS
BAND = 5 * BS
F32, BF16 = jnp.float32, jnp.bfloat16
SMEM = pl.BlockSpec(memory_space=pltpu.SMEM)
VMEM = pl.BlockSpec(memory_space=pltpu.VMEM)
ANY = pl.BlockSpec(memory_space=pl.ANY)


def low_half(rows):
    return lax.broadcasted_iota(jnp.int32, (rows, HALF), 1) < BS


def dot(x, y):
    return jnp.dot(x, y, preferred_element_type=F32)


def dot_rows(x, y):
    return lax.dot_general(x, y, (((0,), (0,)), ((), ())), preferred_element_type=F32)


def pair(p_idx, row, block):
    first = ((p_idx[0, row] - row // RATIO) & 1).astype(F32)
    second = ((p_idx[1, row] - row // RATIO) & 1).astype(F32)
    low = low_half(BS)
    x = block.astype(F32)
    y = pltpu.roll(x, BS, 1)
    here = x * jnp.where(low, 1.0 - first, second) + y * jnp.where(low, 1.0 - second, first)
    there = y * jnp.where(low, second, 1.0 - first) + x * jnp.where(low, first, 1.0 - second)
    return here.astype(BF16), there


def centred(there):
    low = low_half(BS)
    zero = jnp.zeros_like(there)
    return jnp.concatenate([jnp.where(low, zero, there), jnp.where(low, there, zero)], 1).astype(BF16)


def column(a_idx, k, row):
    return row + ((a_idx[k, row] - row + RATIO) & 15)


def spread(a_row, places):
    low = low_half(BS)
    tiles = [jnp.zeros((BS, HALF), F32)] * 2
    for j in range(KA // 2):
        x = a_row[:, j * HALF : (j + 1) * HALF].astype(F32)
        y = pltpu.roll(x, BS, 1)
        for blocks, at in ((x, (2 * j, 2 * j + 1)), (y, (2 * j + 1, 2 * j))):
            place = jnp.where(low, places[at[0]], places[at[1]])
            for t in range(2):
                wanted = jnp.where(low, 2 * t, 2 * t + 1)
                tiles[t] = tiles[t] + jnp.where(place == wanted, blocks, 0.0)
    return jnp.concatenate(tiles, 1).astype(BF16)


def shifted(x):
    return pltpu.roll(jnp.concatenate([x, jnp.zeros((BS, HALF), F32)], 1), BS, 1)[:, :BAND]


def padded(x):
    return jnp.concatenate([x, jnp.zeros((BS, BS), F32)], 1)


def edge_body(a_idx, p_idx, a_last, p_ref, wait_rows, intra, inter, final, low7, k7, p0, table, p7, parts, halos):
    first = ROWS - 2 * RATIO
    zero = jnp.zeros((BS, HALF), BF16)
    table[2 * RATIO] = jnp.zeros((BS, WIDE), BF16)

    for i in range(RATIO):
        here, there = pair(p_idx, first + RATIO + i, p_ref[first + RATIO + i])
        table[RATIO + i] = centred(there)
        p7[i] = here
        here, _ = pair(p_idx, first + i, p_ref[first + i])
        table[i] = jnp.concatenate([here, zero], 1)
        here, _ = pair(p_idx, i, p_ref[i])
        p0[i] = here

    last = p7[...].reshape(4 * BS, HALF)
    turned = last.T
    wait_rows()

    for i in range(RATIO):
        row = ROWS - RATIO + i
        places = [column(a_idx, k, row) - RATIO - first for k in range(KA)]
        weights = jnp.concatenate([table[jnp.minimum(place, 2 * RATIO)] for place in places], 0)
        parts[i] = dot(a_last[i], weights).astype(BF16)
        halos[i] = spread(a_last[i], [place - 2 * RATIO for place in places])

    factor = dot(turned, halos[...].reshape(4 * BS, WIDE)).astype(BF16)
    tiles = dot(turned, parts[...].reshape(4 * BS, WIDE))
    low7[...] = tiles[:BS]
    k7[...] = factor[:BS]
    spill = tiles[BS:].astype(BF16)
    down = jnp.concatenate([p0[...].reshape(4 * BS, HALF), jnp.zeros((4 * BS, HALF), BF16)], 0)
    up = jnp.concatenate([last, spill[:, :HALF], spill[:, HALF:], factor[BS:, :HALF], factor[BS:, HALF:]], 0)
    second = lax.axis_index("col") & 1 == 1
    inter[...] = jnp.where(second, up, down)
    in_chip = jnp.where(second, down, up)
    intra[...] = in_chip
    final[...] = in_chip


def inner_body(groups, a_idx, p_idx, a_ref, p_ref, copies, rows, table, pairs, products, earlier=None):
    zero = jnp.zeros((BS, HALF), BF16)
    table[3 * ROWS] = jnp.zeros((BS, WIDE), BF16)
    copies[0].wait()
    for g in range(GROUPS):
        for row in range(g * RATIO, (g + 1) * RATIO):
            if not {g - 1, g, g + 1} & set(groups):
                continue
            here, there = pair(p_idx, row, p_ref[row])
            if g + 1 in groups:
                table[row] = jnp.concatenate([here, zero], 1)
            if g in groups:
                table[ROWS + row] = centred(there)
                pairs[g, (row % RATIO) * BS : (row % RATIO + 1) * BS] = here
            if g - 1 in groups:
                table[2 * ROWS + row] = jnp.concatenate([zero, here], 1)
    copies[1].wait()
    for g in groups:
        for i in range(RATIO):
            row = g * RATIO + i
            blocks = []
            for k in range(KA):
                at = column(a_idx, k, row)
                place = (at // RATIO - g) * ROWS + at - RATIO
                blocks.append(table[jnp.where(at < RATIO, 3 * ROWS, place) if g == 0 else place])
            products[g, i * BS : (i + 1) * BS] = dot(a_ref[row], jnp.concatenate(blocks, 0)).astype(BF16)
    before = None
    for i in range(GROUPS):
        terms = [] if before is None else [padded(before)]
        before = None
        if i in groups:
            both = dot_rows(pairs[i], products[i])
            before = both[BS:]
            terms.append(shifted(both[:BS]))
        if earlier is not None and len(terms) + (i in (0, GROUPS - 1)) < 2:
            terms.append(earlier[i])
        if terms:
            rows[i] = sum(terms)


def factor0(a_idx, a_ref, pairs):
    h0 = jnp.concatenate([spread(a_ref[i], [column(a_idx, k, i) for k in range(KA)]) for i in range(RATIO)], 0)
    return dot_rows(pairs[0], h0).astype(BF16)


FIRST, SECOND = (1, 2, 3, 4, 5), (0, 6)


def early():
    return jnp.logical_and(lax.axis_index("col") == 0, lax.axis_index("row") > 0)


def late():
    return lax.axis_index("col") >= lax.axis_size("col") - 2


vmem = lambda *shape: pltpu.VMEM(shape[:-1], shape[-1])
PAYLOAD = vmem(8 * BS, HALF, BF16)
EDGE_SHAPES = [PAYLOAD] * 3 + [vmem(BS, WIDE, F32), vmem(BS, WIDE, BF16), vmem(RATIO, BS, HALF, BF16)]
OUT = jax.ShapeDtypeStruct((GROUPS, BS, BAND), F32)
FETCH_SCRATCH = [pltpu.SMEM((KA, ROWS), jnp.int32), pltpu.SMEM((2, ROWS), jnp.int32)]


def run(kernel, name, flops, **settings):
    return pl.pallas_call(
        kernel,
        compiler_params=pltpu.CompilerParams(vmem_limit_bytes=20 << 20),
        cost_estimate=pl.CostEstimate(flops=flops, bytes_accessed=1 << 20, transcendentals=0),
        name=name,
        **settings,
    )


def fetch(sources, places, sem):
    copies = [pltpu.make_async_copy(x, y, sem.at[n]) for n, (x, y) in enumerate(zip(sources, places, strict=True))]
    for copy in copies:
        copy.start()
    return copies


def inner_groups(sources, inner_out, scratch):
    a_idx, p_idx, a_ref, p_ref, sem, *rest = scratch
    a_idx_hbm, p_idx_hbm, a_hbm, p_hbm = sources
    copies = fetch((p_hbm, a_idx_hbm, p_idx_hbm, a_hbm), (p_ref, a_idx, p_idx, a_ref), sem)
    for copy in copies[:3]:
        copy.wait()
    inner_body(a_idx, p_idx, a_ref, p_ref, copies[3].wait, *inner_out, *rest)


def edge_kernel(a_idx_hbm, p_idx_hbm, a_hbm, p_hbm, *refs):
    edge_out, (a_idx, p_idx, a_last, p_ends, sem, *rest) = refs[:6], refs[6:]
    near = pl.ds(0, RATIO)
    far = pl.ds(ROWS - 2 * RATIO, 2 * RATIO)
    copies = fetch(
        (p_idx_hbm, a_idx_hbm, p_hbm.at[far], p_hbm.at[near], a_hbm.at[pl.ds(ROWS - RATIO, RATIO)]),
        (p_idx, a_idx, p_ends.at[far], p_ends.at[near], a_last),
        sem,
    )
    for copy in copies[:4]:
        copy.wait()
    edge_body(a_idx, p_idx, a_last, p_ends, copies[4].wait, *edge_out, *rest)


def edge(operands):
    return run(
        edge_kernel,
        "edge",
        1 << 28,
        in_specs=[ANY] * 4,
        out_specs=[VMEM] * 6,
        out_shape=EDGE_SHAPES,
        scratch_shapes=FETCH_SCRATCH[:2]
        + [
            vmem(RATIO, BS, KA * BS, BF16),
            vmem(ROWS, BS, HALF, BF16),
            pltpu.SemaphoreType.DMA((5,)),
            vmem(2 * RATIO + 1, BS, WIDE, BF16),
            vmem(RATIO, BS, HALF, BF16),
            vmem(RATIO, BS, WIDE, BF16),
            vmem(RATIO, BS, WIDE, BF16),
        ],
    )(*operands)


INNER_SCRATCH = FETCH_SCRATCH + [
    pltpu.SemaphoreType.DMA((2,)),
    vmem(3 * ROWS + 1, BS, WIDE, BF16),
    vmem(GROUPS, 4 * BS, HALF, BF16),
    vmem(GROUPS - 1, 4 * BS, WIDE, BF16),
]


def ahead_kernel(a_idx_from, p_idx_from, a_ref, p_ref, _, __, rows, *refs):
    a_idx, p_idx, sem, *rest = refs[2:]

    @pl.when(early())
    def _():
        copies = fetch((p_idx_from, a_idx_from), (p_idx, a_idx), sem)
        inner_body(FIRST, a_idx, p_idx, a_ref, p_ref, copies, rows, *rest)


def ahead(operands, *sent):
    return run(
        ahead_kernel,
        "ahead",
        1 << 30,
        in_specs=[VMEM] * 4 + [ANY] * 2,
        out_specs=[VMEM] + [ANY] * 2,
        out_shape=[vmem(GROUPS, BS, BAND, F32)] + [PAYLOAD] * 2,
        input_output_aliases={4: 1, 5: 2},
        scratch_shapes=INNER_SCRATCH,
    )(*operands, *sent)


def inner_kernel(a_idx_from, p_idx_from, a_ref, p_ref, earlier, rows, k0, *refs):
    a_idx, p_idx, sem, table, pairs, products = refs
    copies = fetch((p_idx_from, a_idx_from), (p_idx, a_idx), sem)
    for chosen, groups, on in ((early(), SECOND, earlier), (jnp.logical_not(early()), tuple(range(GROUPS - 1)), None)):

        @pl.when(chosen)
        def _(groups=groups, on=on):
            inner_body(groups, a_idx, p_idx, a_ref, p_ref, copies, rows, table, pairs, products, on)

    k0[...] = factor0(a_idx, a_ref, pairs)


def inner(operands, earlier):
    return run(
        inner_kernel,
        "inner",
        1 << 30,
        in_specs=[VMEM] * 5,
        out_specs=[VMEM] * 2,
        out_shape=[vmem(GROUPS, BS, BAND, F32), vmem(HALF, WIDE, BF16)],
        scratch_shapes=INNER_SCRATCH,
    )(*operands, earlier)


def last_kernel(intra, inter, final, low7, k7, p0, given, k0, out_hbm, rows, sem):
    def out_copy(source, at, size, n):
        return pltpu.make_async_copy(source, out_hbm.at[pl.ds(at, size)], sem.at[n])

    whole = out_copy(given.at[pl.ds(2, GROUPS - 3)], 2, GROUPS - 3, 0)
    whole.start()
    core = lax.axis_index("col") & 1
    in_chip = jnp.where(late(), final[...], intra[...])
    between = inter[...]
    from_before = jnp.where(core == 0, between, in_chip)
    from_after = jnp.where(core == 0, in_chip[: 4 * BS], between[: 4 * BS])
    both0 = dot(k0[...], from_before[: 4 * BS])
    lower7 = dot(k7[...], from_after)
    spill0 = from_before[4 * BS : 5 * BS].astype(F32)
    spill1 = from_before[5 * BS : 6 * BS].astype(F32)
    own = p0[...].reshape(4 * BS, HALF)
    spill1 += dot(from_before[6 * BS : 7 * BS], own[:HALF]) + dot(from_before[7 * BS :], own[HALF:])
    zero = jnp.zeros((BS, HALF), F32)
    rows[0] = given[0] + shifted(jnp.concatenate([both0[:BS], zero], 1)) + padded(jnp.concatenate([spill0, spill1], 1))
    rows[1] = given[1] + padded(jnp.concatenate([both0[BS:], zero], 1))
    rows[2] = given[GROUPS - 1] + shifted(low7[...] + jnp.concatenate([zero, lower7], 1))
    copies = [out_copy(rows.at[pl.ds(0, 2)], 0, 2, 1), out_copy(rows.at[pl.ds(2, 1)], GROUPS - 1, 1, 2)]
    for copy in copies:
        copy.start()
    for copy in [whole] + copies:
        copy.wait()


def last(*args):
    return run(
        last_kernel,
        "last",
        1 << 26,
        in_specs=[VMEM] * 8,
        out_specs=ANY,
        out_shape=OUT,
        scratch_shapes=[vmem(3, BS, BAND, F32), pltpu.SemaphoreType.DMA((3,))],
    )(*args)


def shards(a_blocks, a_index, p_blocks, p_index):
    operands = a_index.T, p_index.T, a_blocks, p_blocks
    in_hbm = [pltpu.with_memory_space_constraint(x, pltpu.HBM) for x in operands]
    in_vmem = [pltpu.with_memory_space_constraint(x, pltpu.VMEM) for x in operands]
    axes = ("row", "col")
    devices, line = lax.axis_size(axes), lax.axis_size("col")
    intra, inter, final, low7, k7, p0 = edge(in_hbm)
    within = [(d, d ^ 1) for d in range(devices)]
    most = [(s, t) for s, t in within if s % line < line - 2]
    others = [(s, t) for s, t in within if s % line >= line - 2]
    across = [(d, (d + 1 if d % 2 else d - 1) % devices) for d in range(devices)]
    from_most = lax.ppermute(intra, axes, most)
    earlier, inter, final = ahead(in_vmem, inter, final)
    from_across = lax.ppermute(inter, axes, across)
    from_final = lax.ppermute(final, axes, others)
    rows, k0 = inner(in_vmem, earlier)
    return last(from_most, from_across, from_final, low7, k7, p0, rows, k0)


def solution(mesh):
    blocks = P(("row", "col"), None, None)
    index = P(("row", "col"), None)
    return jax.shard_map(
        shards, mesh=mesh, in_specs=(blocks, index, blocks, index), out_specs=blocks, check_vma=False
    )
```

```python
import jax
import jax.numpy as jnp
from jax import lax
from jax.experimental import pallas as pl
from jax.experimental.pallas import tpu as pltpu
from jax.sharding import PartitionSpec as P

BS = 64
KA = 8
RATIO = 4
GROUPS = 8
ROWS = RATIO * GROUPS
HALF = 2 * BS
WIDE = 4 * BS
BAND = 5 * BS
F32, BF16 = jnp.float32, jnp.bfloat16
SMEM = pl.BlockSpec(memory_space=pltpu.SMEM)
VMEM = pl.BlockSpec(memory_space=pltpu.VMEM)
ANY = pl.BlockSpec(memory_space=pl.ANY)


def low_half(rows):
    return lax.broadcasted_iota(jnp.int32, (rows, HALF), 1) < BS


def dot(x, y):
    return jnp.dot(x, y, preferred_element_type=F32)


def dot_rows(x, y):
    return lax.dot_general(x, y, (((0,), (0,)), ((), ())), preferred_element_type=F32)


def pair(p_idx, row, block):
    first = ((p_idx[0, row] - row // RATIO) & 1).astype(F32)
    second = ((p_idx[1, row] - row // RATIO) & 1).astype(F32)
    low = low_half(BS)
    x = block.astype(F32)
    y = pltpu.roll(x, BS, 1)
    here = x * jnp.where(low, 1.0 - first, second) + y * jnp.where(low, 1.0 - second, first)
    there = y * jnp.where(low, second, 1.0 - first) + x * jnp.where(low, first, 1.0 - second)
    return here.astype(BF16), there


def centred(there):
    low = low_half(BS)
    zero = jnp.zeros_like(there)
    return jnp.concatenate([jnp.where(low, zero, there), jnp.where(low, there, zero)], 1).astype(BF16)


def column(a_idx, k, row):
    return row + ((a_idx[k, row] - row + RATIO) & 15)


def spread(a_row, places):
    low = low_half(BS)
    tiles = [jnp.zeros((BS, HALF), F32)] * 2
    for j in range(KA // 2):
        x = a_row[:, j * HALF : (j + 1) * HALF].astype(F32)
        y = pltpu.roll(x, BS, 1)
        for blocks, at in ((x, (2 * j, 2 * j + 1)), (y, (2 * j + 1, 2 * j))):
            place = jnp.where(low, places[at[0]], places[at[1]])
            for t in range(2):
                wanted = jnp.where(low, 2 * t, 2 * t + 1)
                tiles[t] = tiles[t] + jnp.where(place == wanted, blocks, 0.0)
    return jnp.concatenate(tiles, 1).astype(BF16)


def shifted(x):
    return pltpu.roll(jnp.concatenate([x, jnp.zeros((BS, HALF), F32)], 1), BS, 1)[:, :BAND]


def padded(x):
    return jnp.concatenate([x, jnp.zeros((BS, BS), F32)], 1)


def edge_body(a_idx, p_idx, a_last, p_ref, wait_rows, intra, inter, low7, k7, p0, table, p7, parts, halos):
    first = ROWS - 2 * RATIO
    zero = jnp.zeros((BS, HALF), BF16)
    table[2 * RATIO] = jnp.zeros((BS, WIDE), BF16)

    for i in range(RATIO):
        here, there = pair(p_idx, first + RATIO + i, p_ref[first + RATIO + i])
        table[RATIO + i] = centred(there)
        p7[i] = here
        here, _ = pair(p_idx, first + i, p_ref[first + i])
        table[i] = jnp.concatenate([here, zero], 1)
        here, _ = pair(p_idx, i, p_ref[i])
        p0[i] = here

    last = p7[...].reshape(4 * BS, HALF)
    turned = last.T
    wait_rows()

    for i in range(RATIO):
        row = ROWS - RATIO + i
        places = [column(a_idx, k, row) - RATIO - first for k in range(KA)]
        weights = jnp.concatenate([table[jnp.minimum(place, 2 * RATIO)] for place in places], 0)
        parts[i] = dot(a_last[i], weights).astype(BF16)
        halos[i] = spread(a_last[i], [place - 2 * RATIO for place in places])

    factor = dot(turned, halos[...].reshape(4 * BS, WIDE)).astype(BF16)
    tiles = dot(turned, parts[...].reshape(4 * BS, WIDE))
    low7[...] = tiles[:BS]
    k7[...] = factor[:BS]
    spill = tiles[BS:].astype(BF16)
    down = jnp.concatenate([p0[...].reshape(4 * BS, HALF), jnp.zeros((4 * BS, HALF), BF16)], 0)
    up = jnp.concatenate([last, spill[:, :HALF], spill[:, HALF:], factor[BS:, :HALF], factor[BS:, HALF:]], 0)
    second = lax.axis_index("col") & 1 == 1
    inter[...] = jnp.where(second, up, down)
    intra[...] = jnp.where(second, down, up)


def inner_body(groups, a_idx, p_idx, a_ref, p_ref, copies, rows, table, pairs, products, earlier=None):
    zero = jnp.zeros((BS, HALF), BF16)
    table[3 * ROWS] = jnp.zeros((BS, WIDE), BF16)
    copies[0].wait()
    for g in range(GROUPS):
        for row in range(g * RATIO, (g + 1) * RATIO):
            if not {g - 1, g, g + 1} & set(groups):
                continue
            here, there = pair(p_idx, row, p_ref[row])
            if g + 1 in groups:
                table[row] = jnp.concatenate([here, zero], 1)
            if g in groups:
                table[ROWS + row] = centred(there)
                pairs[g, (row % RATIO) * BS : (row % RATIO + 1) * BS] = here
            if g - 1 in groups:
                table[2 * ROWS + row] = jnp.concatenate([zero, here], 1)
    copies[1].wait()
    for g in groups:
        for i in range(RATIO):
            row = g * RATIO + i
            blocks = []
            for k in range(KA):
                at = column(a_idx, k, row)
                place = (at // RATIO - g) * ROWS + at - RATIO
                blocks.append(table[jnp.where(at < RATIO, 3 * ROWS, place) if g == 0 else place])
            products[g, i * BS : (i + 1) * BS] = dot(a_ref[row], jnp.concatenate(blocks, 0)).astype(BF16)
    before = None
    for i in range(GROUPS):
        terms = [] if before is None else [padded(before)]
        before = None
        if i in groups:
            both = dot_rows(pairs[i], products[i])
            before = both[BS:]
            terms.append(shifted(both[:BS]))
        if earlier is not None and len(terms) + (i in (0, GROUPS - 1)) < 2:
            terms.append(earlier[i])
        if terms:
            rows[i] = sum(terms)


def factor0(a_idx, a_ref, pairs):
    h0 = jnp.concatenate([spread(a_ref[i], [column(a_idx, k, i) for k in range(KA)]) for i in range(RATIO)], 0)
    return dot_rows(pairs[0], h0).astype(BF16)


FIRST, SECOND = (1, 2, 3, 4), (0, 5, 6)


def early():
    return jnp.logical_and(lax.axis_index("col") == 0, lax.axis_index("row") > 0)


def late():
    return lax.axis_index("col") >= lax.axis_size("col") - 2


vmem = lambda *shape: pltpu.VMEM(shape[:-1], shape[-1])
PAYLOAD = vmem(8 * BS, HALF, BF16)
EDGE_SHAPES = [PAYLOAD] * 2 + [vmem(BS, WIDE, F32), vmem(BS, WIDE, BF16), vmem(RATIO, BS, HALF, BF16)]
OUT = jax.ShapeDtypeStruct((GROUPS, BS, BAND), F32)
FETCH_SCRATCH = [pltpu.SMEM((KA, ROWS), jnp.int32), pltpu.SMEM((2, ROWS), jnp.int32)]


def run(kernel, name, flops, **settings):
    return pl.pallas_call(
        kernel,
        compiler_params=pltpu.CompilerParams(vmem_limit_bytes=20 << 20),
        cost_estimate=pl.CostEstimate(flops=flops, bytes_accessed=1 << 20, transcendentals=0),
        name=name,
        **settings,
    )


def fetch(sources, places, sem):
    copies = [pltpu.make_async_copy(x, y, sem.at[n]) for n, (x, y) in enumerate(zip(sources, places, strict=True))]
    for copy in copies:
        copy.start()
    return copies


def inner_groups(sources, inner_out, scratch):
    a_idx, p_idx, a_ref, p_ref, sem, *rest = scratch
    a_idx_hbm, p_idx_hbm, a_hbm, p_hbm = sources
    copies = fetch((p_hbm, a_idx_hbm, p_idx_hbm, a_hbm), (p_ref, a_idx, p_idx, a_ref), sem)
    for copy in copies[:3]:
        copy.wait()
    inner_body(a_idx, p_idx, a_ref, p_ref, copies[3].wait, *inner_out, *rest)


def edge_kernel(a_idx_hbm, p_idx_hbm, a_hbm, p_hbm, *refs):
    edge_out, (a_idx, p_idx, a_last, p_ends, sem, *rest) = refs[:5], refs[5:]
    near = pl.ds(0, RATIO)
    far = pl.ds(ROWS - 2 * RATIO, 2 * RATIO)
    copies = fetch(
        (p_idx_hbm, a_idx_hbm, p_hbm.at[far], p_hbm.at[near], a_hbm.at[pl.ds(ROWS - RATIO, RATIO)]),
        (p_idx, a_idx, p_ends.at[far], p_ends.at[near], a_last),
        sem,
    )
    for copy in copies[:4]:
        copy.wait()
    edge_body(a_idx, p_idx, a_last, p_ends, copies[4].wait, *edge_out, *rest)


def edge(operands):
    return run(
        edge_kernel,
        "edge",
        1 << 28,
        in_specs=[ANY] * 4,
        out_specs=[VMEM] * 5,
        out_shape=EDGE_SHAPES,
        scratch_shapes=FETCH_SCRATCH[:2]
        + [
            vmem(RATIO, BS, KA * BS, BF16),
            vmem(ROWS, BS, HALF, BF16),
            pltpu.SemaphoreType.DMA((5,)),
            vmem(2 * RATIO + 1, BS, WIDE, BF16),
            vmem(RATIO, BS, HALF, BF16),
            vmem(RATIO, BS, WIDE, BF16),
            vmem(RATIO, BS, WIDE, BF16),
        ],
    )(*operands)


INNER_SCRATCH = FETCH_SCRATCH + [
    pltpu.SemaphoreType.DMA((2,)),
    vmem(3 * ROWS + 1, BS, WIDE, BF16),
    vmem(GROUPS, 4 * BS, HALF, BF16),
    vmem(GROUPS - 1, 4 * BS, WIDE, BF16),
]


def ahead_kernel(a_idx_from, p_idx_from, a_ref, p_ref, _, rows, *refs):
    a_idx, p_idx, sem, *rest = refs[1:]

    @pl.when(early())
    def _():
        copies = fetch((p_idx_from, a_idx_from), (p_idx, a_idx), sem)
        inner_body(FIRST, a_idx, p_idx, a_ref, p_ref, copies, rows, *rest)


def ahead(operands, inter):
    return run(
        ahead_kernel,
        "ahead",
        1 << 30,
        in_specs=[VMEM] * 4 + [ANY],
        out_specs=[VMEM, ANY],
        out_shape=[vmem(GROUPS, BS, BAND, F32), PAYLOAD],
        input_output_aliases={4: 1},
        scratch_shapes=INNER_SCRATCH,
    )(*operands, inter)


def skipped_kernel(*refs):
    del refs


def skipped(inter):
    return run(
        skipped_kernel,
        "skipped",
        1,
        in_specs=[ANY],
        out_specs=[VMEM, VMEM, ANY],
        out_shape=[PAYLOAD, vmem(GROUPS, BS, BAND, F32), PAYLOAD],
        input_output_aliases={0: 2},
    )(inter)


def inner_kernel(a_idx_from, p_idx_from, a_ref, p_ref, earlier, rows, k0, *refs):
    a_idx, p_idx, sem, table, pairs, products = refs[-6:]
    copies = fetch((p_idx_from, a_idx_from), (p_idx, a_idx), sem)
    for chosen, groups, on in ((early(), SECOND, earlier), (jnp.logical_not(early()), tuple(range(GROUPS - 1)), None)):

        @pl.when(chosen)
        def _(groups=groups, on=on):
            inner_body(groups, a_idx, p_idx, a_ref, p_ref, copies, rows, table, pairs, products, on)

    k0[...] = factor0(a_idx, a_ref, pairs)


def inner(operands, earlier, *more):
    return run(
        inner_kernel,
        "inner",
        1 << 30,
        in_specs=[VMEM] * 5,
        out_specs=[VMEM] * (2 + len(more)),
        out_shape=[vmem(GROUPS, BS, BAND, F32), vmem(HALF, WIDE, BF16), *more],
        scratch_shapes=INNER_SCRATCH,
    )(*operands, earlier)


def last_kernel(intra, inter, final, low7, k7, p0, given, k0, out_hbm, rows, sem):
    def out_copy(source, at, size, n):
        return pltpu.make_async_copy(source, out_hbm.at[pl.ds(at, size)], sem.at[n])

    whole = out_copy(given.at[pl.ds(2, GROUPS - 3)], 2, GROUPS - 3, 0)
    whole.start()
    core = lax.axis_index("col") & 1
    in_chip = jnp.where(late(), final[...], intra[...])
    between = inter[...]
    from_before = jnp.where(core == 0, between, in_chip)
    from_after = jnp.where(core == 0, in_chip[: 4 * BS], between[: 4 * BS])
    both0 = dot(k0[...], from_before[: 4 * BS])
    lower7 = dot(k7[...], from_after)
    spill0 = from_before[4 * BS : 5 * BS].astype(F32)
    spill1 = from_before[5 * BS : 6 * BS].astype(F32)
    own = p0[...].reshape(4 * BS, HALF)
    spill1 += dot(from_before[6 * BS : 7 * BS], own[:HALF]) + dot(from_before[7 * BS :], own[HALF:])
    zero = jnp.zeros((BS, HALF), F32)
    rows[0] = given[0] + shifted(jnp.concatenate([both0[:BS], zero], 1)) + padded(jnp.concatenate([spill0, spill1], 1))
    rows[1] = given[1] + padded(jnp.concatenate([both0[BS:], zero], 1))
    rows[2] = given[GROUPS - 1] + shifted(low7[...] + jnp.concatenate([zero, lower7], 1))
    copies = [out_copy(rows.at[pl.ds(0, 2)], 0, 2, 1), out_copy(rows.at[pl.ds(2, 1)], GROUPS - 1, 1, 2)]
    for copy in copies:
        copy.start()
    for copy in [whole] + copies:
        copy.wait()


def last(*args):
    return run(
        last_kernel,
        "last",
        1 << 26,
        in_specs=[VMEM] * 8,
        out_specs=ANY,
        out_shape=OUT,
        scratch_shapes=[vmem(3, BS, BAND, F32), pltpu.SemaphoreType.DMA((3,))],
    )(*args)


def shards(a_blocks, a_index, p_blocks, p_index):
    operands = a_index.T, p_index.T, a_blocks, p_blocks
    in_hbm = [pltpu.with_memory_space_constraint(x, pltpu.HBM) for x in operands]
    in_vmem = [pltpu.with_memory_space_constraint(x, pltpu.VMEM) for x in operands]
    axes = ("row", "col")
    devices, line = lax.axis_size(axes), lax.axis_size("col")
    intra, inter, low7, k7, p0 = edge(in_hbm)
    within = [(d, d ^ 1) for d in range(devices)]
    most = [(s, t) for s, t in within if s % line < line - 2]
    others = [(s, t) for s, t in within if s % line >= line - 2]
    across = [(d, (d + 1 if d % 2 else d - 1) % devices) for d in range(devices)]

    def exchange_now(intra, inter):
        return lax.ppermute(intra, axes, most), *ahead(in_vmem, inter)

    def exchange_later(_, inter):
        return skipped(inter)

    def exchange_here(intra, earlier):
        return lax.ppermute(intra, axes, others), *inner(in_vmem, earlier)

    def exchanged(_, earlier):
        rows, k0, unused = inner(in_vmem, earlier, PAYLOAD)
        return unused, rows, k0

    from_most, earlier, inter = lax.cond(late(), exchange_later, exchange_now, intra, inter)
    from_across = lax.ppermute(inter, axes, across)
    from_final, rows, k0 = lax.cond(late(), exchange_here, exchanged, intra, earlier)
    return last(from_most, from_across, from_final, low7, k7, p0, rows, k0)


def solution(mesh):
    blocks = P(("row", "col"), None, None)
    index = P(("row", "col"), None)
    return jax.shard_map(
        shards, mesh=mesh, in_specs=(blocks, index, blocks, index), out_specs=blocks, check_vma=False
    )
```

```python
import functools

import jax
import jax.numpy as jnp
from jax import lax
from jax.experimental import pallas as pl
from jax.experimental.pallas import tpu as pltpu
from jax.sharding import PartitionSpec as P

BS = 64
KA = 8
RATIO = 4
GROUPS = 8
ROWS = RATIO * GROUPS
HALF = 2 * BS
WIDE = 4 * BS
BAND = 5 * BS
F32, BF16 = jnp.float32, jnp.bfloat16
SMEM = pl.BlockSpec(memory_space=pltpu.SMEM)
VMEM = pl.BlockSpec(memory_space=pltpu.VMEM)
ANY = pl.BlockSpec(memory_space=pl.ANY)


def low_half(rows):
    return lax.broadcasted_iota(jnp.int32, (rows, HALF), 1) < BS


def dot(x, y):
    return jnp.dot(x, y, preferred_element_type=F32)


def dot_rows(x, y):
    return lax.dot_general(x, y, (((0,), (0,)), ((), ())), preferred_element_type=F32)


def pair(p_idx, row, block):
    first = ((p_idx[0, row] - row // RATIO) & 1).astype(F32)
    second = ((p_idx[1, row] - row // RATIO) & 1).astype(F32)
    low = low_half(BS)
    x = block.astype(F32)
    y = pltpu.roll(x, BS, 1)
    here = x * jnp.where(low, 1.0 - first, second) + y * jnp.where(low, 1.0 - second, first)
    there = y * jnp.where(low, second, 1.0 - first) + x * jnp.where(low, first, 1.0 - second)
    return here.astype(BF16), there


def centred(there):
    low = low_half(BS)
    zero = jnp.zeros_like(there)
    return jnp.concatenate([jnp.where(low, zero, there), jnp.where(low, there, zero)], 1).astype(BF16)


def column(a_idx, k, row):
    return row + ((a_idx[k, row] - row + RATIO) & 15)


def spread(a_row, places):
    low = low_half(BS)
    tiles = [jnp.zeros((BS, HALF), F32)] * 2
    for j in range(KA // 2):
        x = a_row[:, j * HALF : (j + 1) * HALF].astype(F32)
        y = pltpu.roll(x, BS, 1)
        for blocks, at in ((x, (2 * j, 2 * j + 1)), (y, (2 * j + 1, 2 * j))):
            place = jnp.where(low, places[at[0]], places[at[1]])
            for t in range(2):
                wanted = jnp.where(low, 2 * t, 2 * t + 1)
                tiles[t] = tiles[t] + jnp.where(place == wanted, blocks, 0.0)
    return jnp.concatenate(tiles, 1).astype(BF16)


def shifted(x):
    return pltpu.roll(jnp.concatenate([x, jnp.zeros((BS, HALF), F32)], 1), BS, 1)[:, :BAND]


def padded(x):
    return jnp.concatenate([x, jnp.zeros((BS, BS), F32)], 1)


def edge_body(a_idx, p_idx, a_last, p_ref, wait_rows, intra, inter, final, low7, k7, p0, table, p7, parts, halos):
    first = ROWS - 2 * RATIO
    zero = jnp.zeros((BS, HALF), BF16)
    table[2 * RATIO] = jnp.zeros((BS, WIDE), BF16)

    for i in range(RATIO):
        here, there = pair(p_idx, first + RATIO + i, p_ref[first + RATIO + i])
        table[RATIO + i] = centred(there)
        p7[i] = here
        here, _ = pair(p_idx, first + i, p_ref[first + i])
        table[i] = jnp.concatenate([here, zero], 1)
        here, _ = pair(p_idx, i, p_ref[i])
        p0[i] = here

    last = p7[...].reshape(4 * BS, HALF)
    turned = last.T
    wait_rows()

    for i in range(RATIO):
        row = ROWS - RATIO + i
        places = [column(a_idx, k, row) - RATIO - first for k in range(KA)]
        weights = jnp.concatenate([table[jnp.minimum(place, 2 * RATIO)] for place in places], 0)
        parts[i] = dot(a_last[i], weights).astype(BF16)
        halos[i] = spread(a_last[i], [place - 2 * RATIO for place in places])

    factor = dot(turned, halos[...].reshape(4 * BS, WIDE)).astype(BF16)
    tiles = dot(turned, parts[...].reshape(4 * BS, WIDE))
    low7[...] = tiles[:BS]
    k7[...] = factor[:BS]
    spill = tiles[BS:].astype(BF16)
    down = jnp.concatenate([p0[...].reshape(4 * BS, HALF), jnp.zeros((4 * BS, HALF), BF16)], 0)
    up = jnp.concatenate([last, spill[:, :HALF], spill[:, HALF:], factor[BS:, :HALF], factor[BS:, HALF:]], 0)
    second = lax.axis_index("col") & 1 == 1
    across = jnp.where(second, up, down)
    inter[...] = across
    final[...] = across
    intra[...] = jnp.where(second, down, up)


def inner_body(a_idx, p_idx, a_ref, p_ref, copies, rows, k0, table, pairs, products):
    zero = jnp.zeros((BS, HALF), BF16)
    table[3 * ROWS] = jnp.zeros((BS, WIDE), BF16)
    copies[0].wait()
    for g in range(GROUPS):
        for i in range(RATIO):
            row = g * RATIO + i
            here, there = pair(p_idx, row, p_ref[row])
            table[row] = jnp.concatenate([here, zero], 1)
            table[ROWS + row] = centred(there)
            table[2 * ROWS + row] = jnp.concatenate([zero, here], 1)
            pairs[g, i * BS : (i + 1) * BS] = here

    copies[1].wait()

    def group(g):
        for i in range(RATIO):
            row = g * RATIO + i
            blocks = []
            for k in range(KA):
                at = column(a_idx, k, row)
                place = jnp.where(at < RATIO, 3 * ROWS, (at // RATIO - g) * ROWS + at - RATIO)
                blocks.append(table[place])
            products[g, i * BS : (i + 1) * BS] = dot(a_ref[row], jnp.concatenate(blocks, 0)).astype(BF16)

    for g in range(GROUPS - 1):
        group(g)
    before = None
    for g in range(GROUPS - 1):
        both = dot_rows(pairs[g], products[g])
        row = shifted(both[:BS])
        rows[g] = row if g == 0 else row + padded(before)
        before = both[BS:]
    rows[GROUPS - 1] = padded(before)
    h0 = jnp.concatenate([spread(a_ref[i], [column(a_idx, k, i) for k in range(KA)]) for i in range(RATIO)], 0)
    k0[...] = dot_rows(pairs[0], h0).astype(BF16)


def turn():
    return jnp.where(jnp.logical_and(lax.axis_index("col") < 2, lax.axis_index("row") > 0), 0, 1)


def joint():
    at = lax.axis_index(("row", "col"))
    return jnp.logical_or(at == 0, at == lax.axis_size(("row", "col")) - 1)


vmem = lambda *shape: pltpu.VMEM(shape[:-1], shape[-1])
PAYLOAD = vmem(8 * BS, HALF, BF16)
EDGE_SHAPES = [PAYLOAD] * 3 + [vmem(BS, WIDE, F32), vmem(BS, WIDE, BF16), vmem(RATIO, BS, HALF, BF16)]
OUT = jax.ShapeDtypeStruct((GROUPS, BS, BAND), F32)
FETCH_SCRATCH = [pltpu.SMEM((KA, ROWS), jnp.int32), pltpu.SMEM((2, ROWS), jnp.int32)]


def run(kernel, name, flops, **settings):
    return pl.pallas_call(
        kernel,
        compiler_params=pltpu.CompilerParams(vmem_limit_bytes=20 << 20),
        cost_estimate=pl.CostEstimate(flops=flops, bytes_accessed=1 << 20, transcendentals=0),
        name=name,
        **settings,
    )


def fetch(sources, places, sem):
    copies = [pltpu.make_async_copy(x, y, sem.at[n]) for n, (x, y) in enumerate(zip(sources, places, strict=True))]
    for copy in copies:
        copy.start()
    return copies


def inner_groups(sources, inner_out, scratch):
    a_idx, p_idx, a_ref, p_ref, sem, *rest = scratch
    a_idx_hbm, p_idx_hbm, a_hbm, p_hbm = sources
    copies = fetch((p_hbm, a_idx_hbm, p_idx_hbm, a_hbm), (p_ref, a_idx, p_idx, a_ref), sem)
    for copy in copies[:3]:
        copy.wait()
    inner_body(a_idx, p_idx, a_ref, p_ref, copies[3].wait, *inner_out, *rest)


def edge_kernel(a_idx_hbm, p_idx_hbm, a_hbm, p_hbm, *refs):
    edge_out, (a_idx, p_idx, a_last, p_ends, sem, *rest) = refs[:6], refs[6:]
    near = pl.ds(0, RATIO)
    far = pl.ds(ROWS - 2 * RATIO, 2 * RATIO)
    copies = fetch(
        (p_idx_hbm, a_idx_hbm, p_hbm.at[far], p_hbm.at[near], a_hbm.at[pl.ds(ROWS - RATIO, RATIO)]),
        (p_idx, a_idx, p_ends.at[far], p_ends.at[near], a_last),
        sem,
    )
    for copy in copies[:4]:
        copy.wait()
    edge_body(a_idx, p_idx, a_last, p_ends, copies[4].wait, *edge_out, *rest)


def edge(operands):
    return run(
        edge_kernel,
        "edge",
        1 << 28,
        in_specs=[ANY] * 4,
        out_specs=[VMEM] * 6,
        out_shape=EDGE_SHAPES,
        scratch_shapes=FETCH_SCRATCH[:2]
        + [
            vmem(RATIO, BS, KA * BS, BF16),
            vmem(ROWS, BS, HALF, BF16),
            pltpu.SemaphoreType.DMA((5,)),
            vmem(2 * RATIO + 1, BS, WIDE, BF16),
            vmem(RATIO, BS, HALF, BF16),
            vmem(RATIO, BS, WIDE, BF16),
            vmem(RATIO, BS, WIDE, BF16),
        ],
    )(*operands)


def inner_kernel(mine, handed, a_idx_from, p_idx_from, a_ref, p_ref, *refs):
    inner_out = refs[handed : handed + 2]
    a_idx, p_idx, sem, *rest = refs[-6:]

    @pl.when(turn() == mine)
    def _():
        copies = fetch((p_idx_from, a_idx_from), (p_idx, a_idx), sem)
        inner_body(a_idx, p_idx, a_ref, p_ref, copies, *inner_out, *rest)


def inner(mine, operands, *sent):
    return run(
        functools.partial(inner_kernel, mine, len(sent)),
        "inner",
        1 << 30,
        in_specs=[VMEM] * 4 + [ANY] * len(sent),
        out_specs=[VMEM, VMEM] + [ANY] * len(sent),
        out_shape=[vmem(GROUPS, BS, BAND, F32), vmem(HALF, WIDE, BF16)] + [PAYLOAD] * len(sent),
        input_output_aliases={4 + i: 2 + i for i in range(len(sent))},
        scratch_shapes=FETCH_SCRATCH
        + [
            pltpu.SemaphoreType.DMA((2,)),
            vmem(3 * ROWS + 1, BS, WIDE, BF16),
            vmem(GROUPS, 4 * BS, HALF, BF16),
            vmem(GROUPS - 1, 4 * BS, WIDE, BF16),
        ],
    )(*operands, *sent)


def last_kernel(inter, intra, final, low7, k7, p0, *refs):
    starts, (out_hbm, rows, sem) = [refs[:2], refs[2:4]], refs[4:]

    def out_copy(source, at, size, n):
        return pltpu.make_async_copy(source, out_hbm.at[pl.ds(at, size)], sem.at[n])

    def finish(given, k0):
        whole = out_copy(given.at[pl.ds(2, GROUPS - 3)], 2, GROUPS - 3, 0)
        whole.start()
        core = lax.axis_index("col") & 1
        in_chip = intra[...]
        between = jnp.where(joint(), final[...], inter[...])
        from_before = jnp.where(core == 0, between, in_chip)
        from_after = jnp.where(core == 0, in_chip[: 4 * BS], between[: 4 * BS])
        both0 = dot(k0[...], from_before[: 4 * BS])
        lower7 = dot(k7[...], from_after)
        spill0 = from_before[4 * BS : 5 * BS].astype(F32)
        spill1 = from_before[5 * BS : 6 * BS].astype(F32)
        own = p0[...].reshape(4 * BS, HALF)
        spill1 += dot(from_before[6 * BS : 7 * BS], own[:HALF]) + dot(from_before[7 * BS :], own[HALF:])
        zero = jnp.zeros((BS, HALF), F32)
        rows[0] = given[0] + shifted(jnp.concatenate([both0[:BS], zero], 1)) + padded(jnp.concatenate([spill0, spill1], 1))
        rows[1] = given[1] + padded(jnp.concatenate([both0[BS:], zero], 1))
        rows[2] = given[GROUPS - 1] + shifted(low7[...] + jnp.concatenate([zero, lower7], 1))
        copies = [out_copy(rows.at[pl.ds(0, 2)], 0, 2, 1), out_copy(rows.at[pl.ds(2, 1)], GROUPS - 1, 1, 2)]
        for copy in copies:
            copy.start()
        for copy in [whole] + copies:
            copy.wait()

    for mine in range(2):

        @pl.when(turn() == mine)
        def _(mine=mine):
            finish(*starts[mine])


def last(*args):
    return run(
        last_kernel,
        "last",
        1 << 26,
        in_specs=[VMEM] * 10,
        out_specs=ANY,
        out_shape=OUT,
        scratch_shapes=[vmem(3, BS, BAND, F32), pltpu.SemaphoreType.DMA((3,))],
    )(*args)


def shards(a_blocks, a_index, p_blocks, p_index):
    operands = a_index.T, p_index.T, a_blocks, p_blocks
    in_hbm = [pltpu.with_memory_space_constraint(x, pltpu.HBM) for x in operands]
    in_vmem = [pltpu.with_memory_space_constraint(x, pltpu.VMEM) for x in operands]
    axes = ("row", "col")
    devices = lax.axis_size(axes)
    intra, inter, final, low7, k7, p0 = edge(in_hbm)
    within = [(d, d ^ 1) for d in range(devices)]
    across = [(d, d + 1 if d % 2 else d - 1) for d in range(1, devices - 1)]
    closing = [(0, devices - 1), (devices - 1, 0)]
    *first, inter, intra, final = inner(0, in_vmem, inter, intra, final)
    from_across = lax.ppermute(inter, axes, across)
    from_within = lax.ppermute(intra, axes, within)
    from_closing = lax.ppermute(final, axes, closing)
    second = inner(1, in_vmem)
    return last(from_across, from_within, from_closing, low7, k7, p0, *first, *second)


def solution(mesh):
    blocks = P(("row", "col"), None, None)
    index = P(("row", "col"), None)
    return jax.shard_map(
        shards, mesh=mesh, in_specs=(blocks, index, blocks, index), out_specs=blocks, check_vma=False
    )
```

```python
import jax
import jax.numpy as jnp
from jax import lax
from jax.experimental import pallas as pl
from jax.experimental.pallas import tpu as pltpu
from jax.sharding import PartitionSpec as P

BS = 64
KA = 8
RATIO = 4
GROUPS = 8
ROWS = RATIO * GROUPS
HALF = 2 * BS
WIDE = 4 * BS
BAND = 5 * BS
F32, BF16 = jnp.float32, jnp.bfloat16
SMEM = pl.BlockSpec(memory_space=pltpu.SMEM)
VMEM = pl.BlockSpec(memory_space=pltpu.VMEM)
ANY = pl.BlockSpec(memory_space=pl.ANY)


def low_half(rows):
    return lax.broadcasted_iota(jnp.int32, (rows, HALF), 1) < BS


def dot(x, y):
    return jnp.dot(x, y, preferred_element_type=F32)


def dot_rows(x, y):
    return lax.dot_general(x, y, (((0,), (0,)), ((), ())), preferred_element_type=F32)


def pair(p_idx, row, block):
    first = ((p_idx[0, row] - row // RATIO) & 1).astype(F32)
    second = ((p_idx[1, row] - row // RATIO) & 1).astype(F32)
    low = low_half(BS)
    x = block.astype(F32)
    y = pltpu.roll(x, BS, 1)
    here = x * jnp.where(low, 1.0 - first, second) + y * jnp.where(low, 1.0 - second, first)
    there = y * jnp.where(low, second, 1.0 - first) + x * jnp.where(low, first, 1.0 - second)
    return here.astype(BF16), there


def centred(there):
    low = low_half(BS)
    zero = jnp.zeros_like(there)
    return jnp.concatenate([jnp.where(low, zero, there), jnp.where(low, there, zero)], 1).astype(BF16)


def column(a_idx, k, row):
    return row + ((a_idx[k, row] - row + RATIO) & 15)


def spread(a_row, places):
    low = low_half(BS)
    tiles = [jnp.zeros((BS, HALF), F32)] * 2
    for j in range(KA // 2):
        x = a_row[:, j * HALF : (j + 1) * HALF].astype(F32)
        y = pltpu.roll(x, BS, 1)
        for blocks, at in ((x, (2 * j, 2 * j + 1)), (y, (2 * j + 1, 2 * j))):
            place = jnp.where(low, places[at[0]], places[at[1]])
            for t in range(2):
                wanted = jnp.where(low, 2 * t, 2 * t + 1)
                tiles[t] = tiles[t] + jnp.where(place == wanted, blocks, 0.0)
    return jnp.concatenate(tiles, 1).astype(BF16)


def shifted(x):
    return pltpu.roll(jnp.concatenate([x, jnp.zeros((BS, HALF), F32)], 1), BS, 1)[:, :BAND]


def padded(x):
    return jnp.concatenate([x, jnp.zeros((BS, BS), F32)], 1)


def edge_body(a_idx, p_idx, a_last, p_ref, wait_rows, intra, inter, final, low7, k7, p0, table, p7, parts, halos):
    first = ROWS - 2 * RATIO
    zero = jnp.zeros((BS, HALF), BF16)
    table[2 * RATIO] = jnp.zeros((BS, WIDE), BF16)

    for i in range(RATIO):
        here, there = pair(p_idx, first + RATIO + i, p_ref[first + RATIO + i])
        table[RATIO + i] = centred(there)
        p7[i] = here
        here, _ = pair(p_idx, first + i, p_ref[first + i])
        table[i] = jnp.concatenate([here, zero], 1)
        here, _ = pair(p_idx, i, p_ref[i])
        p0[i] = here

    last = p7[...].reshape(4 * BS, HALF)
    turned = last.T
    wait_rows()

    for i in range(RATIO):
        row = ROWS - RATIO + i
        places = [column(a_idx, k, row) - RATIO - first for k in range(KA)]
        weights = jnp.concatenate([table[jnp.minimum(place, 2 * RATIO)] for place in places], 0)
        parts[i] = dot(a_last[i], weights).astype(BF16)
        halos[i] = spread(a_last[i], [place - 2 * RATIO for place in places])

    factor = dot(turned, halos[...].reshape(4 * BS, WIDE)).astype(BF16)
    tiles = dot(turned, parts[...].reshape(4 * BS, WIDE))
    low7[...] = tiles[:BS]
    k7[...] = factor[:BS]
    spill = tiles[BS:].astype(BF16)
    down = jnp.concatenate([p0[...].reshape(4 * BS, HALF), jnp.zeros((4 * BS, HALF), BF16)], 0)
    up = jnp.concatenate([last, spill[:, :HALF], spill[:, HALF:], factor[BS:, :HALF], factor[BS:, HALF:]], 0)
    second = lax.axis_index("col") & 1 == 1
    inter[...] = jnp.where(second, up, down)
    in_chip = jnp.where(second, down, up)
    intra[...] = in_chip
    final[...] = in_chip


def inner_body(groups, a_idx, p_idx, a_ref, p_ref, copies, rows, table, pairs, products, earlier=None):
    zero = jnp.zeros((BS, HALF), BF16)
    table[3 * ROWS] = jnp.zeros((BS, WIDE), BF16)
    copies[0].wait()
    for g in range(GROUPS):
        for row in range(g * RATIO, (g + 1) * RATIO):
            if not {g - 1, g, g + 1} & set(groups):
                continue
            here, there = pair(p_idx, row, p_ref[row])
            if g + 1 in groups:
                table[row] = jnp.concatenate([here, zero], 1)
            if g in groups:
                table[ROWS + row] = centred(there)
                pairs[g, (row % RATIO) * BS : (row % RATIO + 1) * BS] = here
            if g - 1 in groups:
                table[2 * ROWS + row] = jnp.concatenate([zero, here], 1)
    for copy in copies[1:]:
        copy.wait()
    for g in groups:
        for i in range(RATIO):
            row = g * RATIO + i
            blocks = []
            for k in range(KA):
                at = column(a_idx, k, row)
                place = (at // RATIO - g) * ROWS + at - RATIO
                blocks.append(table[jnp.where(at < RATIO, 3 * ROWS, place) if g == 0 else place])
            products[g, i * BS : (i + 1) * BS] = dot(a_ref[row], jnp.concatenate(blocks, 0)).astype(BF16)
    before = None
    for i in range(GROUPS):
        terms = [] if before is None else [padded(before)]
        before = None
        if i in groups:
            both = dot_rows(pairs[i], products[i])
            before = both[BS:]
            terms.append(shifted(both[:BS]))
        if earlier is not None and len(terms) + (i in (0, GROUPS - 1)) < 2:
            terms.append(earlier[i])
        if terms:
            rows[i] = sum(terms)


def factor0(a_idx, a_ref, pairs):
    h0 = jnp.concatenate([spread(a_ref[i], [column(a_idx, k, i) for k in range(KA)]) for i in range(RATIO)], 0)
    return dot_rows(pairs[0], h0).astype(BF16)


FIRST, SECOND = (1, 2, 3, 4, 5), (0, 6)


def early():
    return jnp.logical_and(lax.axis_index("col") == 0, lax.axis_index("row") > 0)


def late():
    return lax.axis_index("col") >= lax.axis_size("col") - 2


vmem = lambda *shape: pltpu.VMEM(shape[:-1], shape[-1])
PAYLOAD = vmem(8 * BS, HALF, BF16)
EDGE_SHAPES = [PAYLOAD] * 3 + [vmem(BS, WIDE, F32), vmem(BS, WIDE, BF16), vmem(RATIO, BS, HALF, BF16)]
OUT = jax.ShapeDtypeStruct((GROUPS, BS, BAND), F32)
FETCH_SCRATCH = [pltpu.SMEM((KA, ROWS), jnp.int32), pltpu.SMEM((2, ROWS), jnp.int32)]


def run(kernel, name, flops, **settings):
    return pl.pallas_call(
        kernel,
        compiler_params=pltpu.CompilerParams(vmem_limit_bytes=20 << 20),
        cost_estimate=pl.CostEstimate(flops=flops, bytes_accessed=1 << 20, transcendentals=0),
        name=name,
        **settings,
    )


def fetch(sources, places, sem):
    copies = [pltpu.make_async_copy(x, y, sem.at[n]) for n, (x, y) in enumerate(zip(sources, places, strict=True))]
    for copy in copies:
        copy.start()
    return copies


def inner_groups(sources, inner_out, scratch):
    a_idx, p_idx, a_ref, p_ref, sem, *rest = scratch
    a_idx_hbm, p_idx_hbm, a_hbm, p_hbm = sources
    copies = fetch((p_hbm, a_idx_hbm, p_idx_hbm, a_hbm), (p_ref, a_idx, p_idx, a_ref), sem)
    for copy in copies[:3]:
        copy.wait()
    inner_body(a_idx, p_idx, a_ref, p_ref, copies[3].wait, *inner_out, *rest)


def edge_kernel(a_idx_hbm, p_idx_hbm, a_hbm, p_hbm, *refs):
    edge_out, a_near, (a_idx, p_idx, a_last, p_ends, sem, *rest) = refs[:6], refs[6], refs[7:]
    near = pl.ds(0, RATIO)
    far = pl.ds(ROWS - 2 * RATIO, 2 * RATIO)
    copies = fetch(
        (p_idx_hbm, a_idx_hbm, p_hbm.at[far], p_hbm.at[near], a_hbm.at[pl.ds(ROWS - RATIO, RATIO)]),
        (p_idx, a_idx, p_ends.at[far], p_ends.at[near], a_last),
        sem,
    )
    whole = pltpu.make_async_copy(a_hbm, a_near, sem.at[5])

    @pl.when(early())
    def _():
        whole.start()

    for copy in copies[:4]:
        copy.wait()
    edge_body(a_idx, p_idx, a_last, p_ends, copies[4].wait, *edge_out, *rest)

    @pl.when(early())
    def _():
        whole.wait()


def edge(operands):
    return run(
        edge_kernel,
        "edge",
        1 << 28,
        in_specs=[ANY] * 4,
        out_specs=[VMEM] * 7,
        out_shape=EDGE_SHAPES + [vmem(ROWS, BS, KA * BS, BF16)],
        scratch_shapes=FETCH_SCRATCH[:2]
        + [
            vmem(RATIO, BS, KA * BS, BF16),
            vmem(ROWS, BS, HALF, BF16),
            pltpu.SemaphoreType.DMA((6,)),
            vmem(2 * RATIO + 1, BS, WIDE, BF16),
            vmem(RATIO, BS, HALF, BF16),
            vmem(RATIO, BS, WIDE, BF16),
            vmem(RATIO, BS, WIDE, BF16),
        ],
    )(*operands)


INNER_SCRATCH = FETCH_SCRATCH + [
    pltpu.SemaphoreType.DMA((2,)),
    vmem(3 * ROWS + 1, BS, WIDE, BF16),
    vmem(GROUPS, 4 * BS, HALF, BF16),
    vmem(GROUPS - 1, 4 * BS, WIDE, BF16),
]


def ahead_kernel(a_idx_from, p_idx_from, a_ref, p_ref, _, __, rows, *refs):
    a_idx, p_idx, sem, *rest = refs[2:]

    @pl.when(early())
    def _():
        copies = fetch((p_idx_from, a_idx_from), (p_idx, a_idx), sem)
        inner_body(FIRST, a_idx, p_idx, a_ref, p_ref, copies, rows, *rest)


def ahead(operands, *sent):
    return run(
        ahead_kernel,
        "ahead",
        1 << 30,
        in_specs=[VMEM] * 4 + [ANY] * 2,
        out_specs=[VMEM] + [ANY] * 2,
        out_shape=[vmem(GROUPS, BS, BAND, F32)] + [PAYLOAD] * 2,
        input_output_aliases={4: 1, 5: 2},
        scratch_shapes=INNER_SCRATCH,
    )(*operands, *sent)


def inner_kernel(a_idx_from, p_idx_from, a_near, p_ref, a_hbm, earlier, rows, k0, *refs):
    a_idx, p_idx, sem, table, pairs, products, a_ref, a_sem = refs
    copies = fetch((p_idx_from, a_idx_from), (p_idx, a_idx), sem)

    @pl.when(early())
    def _():
        inner_body(SECOND, a_idx, p_idx, a_near, p_ref, copies, rows, table, pairs, products, earlier)
        k0[...] = factor0(a_idx, a_near, pairs)

    @pl.when(jnp.logical_not(early()))
    def _():
        whole = pltpu.make_async_copy(a_hbm, a_ref, a_sem)
        whole.start()
        groups = tuple(range(GROUPS - 1))
        inner_body(groups, a_idx, p_idx, a_ref, p_ref, copies + [whole], rows, table, pairs, products)
        k0[...] = factor0(a_idx, a_ref, pairs)


def inner(operands, a_hbm, earlier):
    return run(
        inner_kernel,
        "inner",
        1 << 30,
        in_specs=[VMEM] * 4 + [ANY, VMEM],
        out_specs=[VMEM] * 2,
        out_shape=[vmem(GROUPS, BS, BAND, F32), vmem(HALF, WIDE, BF16)],
        scratch_shapes=INNER_SCRATCH + [vmem(ROWS, BS, KA * BS, BF16), pltpu.SemaphoreType.DMA],
    )(*operands, a_hbm, earlier)


def last_kernel(intra, inter, final, low7, k7, p0, given, k0, out_hbm, rows, sem):
    def out_copy(source, at, size, n):
        return pltpu.make_async_copy(source, out_hbm.at[pl.ds(at, size)], sem.at[n])

    whole = out_copy(given.at[pl.ds(2, GROUPS - 3)], 2, GROUPS - 3, 0)
    whole.start()
    core = lax.axis_index("col") & 1
    in_chip = jnp.where(late(), final[...], intra[...])
    between = inter[...]
    from_before = jnp.where(core == 0, between, in_chip)
    from_after = jnp.where(core == 0, in_chip[: 4 * BS], between[: 4 * BS])
    both0 = dot(k0[...], from_before[: 4 * BS])
    lower7 = dot(k7[...], from_after)
    spill0 = from_before[4 * BS : 5 * BS].astype(F32)
    spill1 = from_before[5 * BS : 6 * BS].astype(F32)
    own = p0[...].reshape(4 * BS, HALF)
    spill1 += dot(from_before[6 * BS : 7 * BS], own[:HALF]) + dot(from_before[7 * BS :], own[HALF:])
    zero = jnp.zeros((BS, HALF), F32)
    rows[0] = given[0] + shifted(jnp.concatenate([both0[:BS], zero], 1)) + padded(jnp.concatenate([spill0, spill1], 1))
    rows[1] = given[1] + padded(jnp.concatenate([both0[BS:], zero], 1))
    rows[2] = given[GROUPS - 1] + shifted(low7[...] + jnp.concatenate([zero, lower7], 1))
    copies = [out_copy(rows.at[pl.ds(0, 2)], 0, 2, 1), out_copy(rows.at[pl.ds(2, 1)], GROUPS - 1, 1, 2)]
    for copy in copies:
        copy.start()
    for copy in [whole] + copies:
        copy.wait()


def last(*args):
    return run(
        last_kernel,
        "last",
        1 << 26,
        in_specs=[VMEM] * 8,
        out_specs=ANY,
        out_shape=OUT,
        scratch_shapes=[vmem(3, BS, BAND, F32), pltpu.SemaphoreType.DMA((3,))],
    )(*args)


def shards(a_blocks, a_index, p_blocks, p_index):
    operands = a_index.T, p_index.T, a_blocks, p_blocks
    in_hbm = [pltpu.with_memory_space_constraint(x, pltpu.HBM) for x in operands]
    idx_p = [pltpu.with_memory_space_constraint(x, pltpu.VMEM) for x in (operands[0], operands[1], operands[3])]
    axes = ("row", "col")
    devices, line = lax.axis_size(axes), lax.axis_size("col")
    intra, inter, final, low7, k7, p0, a_near = edge(in_hbm)
    near = [idx_p[0], idx_p[1], a_near, idx_p[2]]
    within = [(d, d ^ 1) for d in range(devices)]
    most = [(s, t) for s, t in within if s % line < line - 2]
    others = [(s, t) for s, t in within if s % line >= line - 2]
    across = [(d, (d + 1 if d % 2 else d - 1) % devices) for d in range(devices)]
    from_most = lax.ppermute(intra, axes, most)
    earlier, inter, final = ahead(near, inter, final)
    from_across = lax.ppermute(inter, axes, across)
    from_final = lax.ppermute(final, axes, others)
    rows, k0 = inner(near, in_hbm[2], earlier)
    return last(from_most, from_across, from_final, low7, k7, p0, rows, k0)


def solution(mesh):
    blocks = P(("row", "col"), None, None)
    index = P(("row", "col"), None)
    return jax.shard_map(
        shards, mesh=mesh, in_specs=(blocks, index, blocks, index), out_specs=blocks, check_vma=False
    )
```

```python
import jax
import jax.numpy as jnp
from jax import lax
from jax.experimental import pallas as pl
from jax.experimental.pallas import tpu as pltpu
from jax.sharding import PartitionSpec as P

BS = 64
KA = 8
RATIO = 4
GROUPS = 8
ROWS = RATIO * GROUPS
HALF = 2 * BS
WIDE = 4 * BS
BAND = 5 * BS
F32, BF16 = jnp.float32, jnp.bfloat16
SMEM = pl.BlockSpec(memory_space=pltpu.SMEM)
VMEM = pl.BlockSpec(memory_space=pltpu.VMEM)
ANY = pl.BlockSpec(memory_space=pl.ANY)


def low_half(rows):
    return lax.broadcasted_iota(jnp.int32, (rows, HALF), 1) < BS


def dot(x, y):
    return jnp.dot(x, y, preferred_element_type=F32)


def dot_rows(x, y):
    return lax.dot_general(x, y, (((0,), (0,)), ((), ())), preferred_element_type=F32)


def pair(p_idx, row, block):
    first = ((p_idx[0, row] - row // RATIO) & 1).astype(F32)
    second = ((p_idx[1, row] - row // RATIO) & 1).astype(F32)
    low = low_half(BS)
    x = block.astype(F32)
    y = pltpu.roll(x, BS, 1)
    here = x * jnp.where(low, 1.0 - first, second) + y * jnp.where(low, 1.0 - second, first)
    there = y * jnp.where(low, second, 1.0 - first) + x * jnp.where(low, first, 1.0 - second)
    return here.astype(BF16), there


def centred(there):
    low = low_half(BS)
    zero = jnp.zeros_like(there)
    return jnp.concatenate([jnp.where(low, zero, there), jnp.where(low, there, zero)], 1).astype(BF16)


def column(a_idx, k, row):
    return row + ((a_idx[k, row] - row + RATIO) & 15)


def spread(a_row, places):
    low = low_half(BS)
    tiles = [jnp.zeros((BS, HALF), F32)] * 2
    for j in range(KA // 2):
        x = a_row[:, j * HALF : (j + 1) * HALF].astype(F32)
        y = pltpu.roll(x, BS, 1)
        for blocks, at in ((x, (2 * j, 2 * j + 1)), (y, (2 * j + 1, 2 * j))):
            place = jnp.where(low, places[at[0]], places[at[1]])
            for t in range(2):
                wanted = jnp.where(low, 2 * t, 2 * t + 1)
                tiles[t] = tiles[t] + jnp.where(place == wanted, blocks, 0.0)
    return jnp.concatenate(tiles, 1).astype(BF16)


def shifted(x):
    return pltpu.roll(jnp.concatenate([x, jnp.zeros((BS, HALF), F32)], 1), BS, 1)[:, :BAND]


def padded(x):
    return jnp.concatenate([x, jnp.zeros((BS, BS), F32)], 1)


def edge_body(a_idx, p_idx, a_last, p_ref, wait_rows, intra, inter, final, low7, k7, p0, table, p7, parts, halos):
    first = ROWS - 2 * RATIO
    zero = jnp.zeros((BS, HALF), BF16)
    table[2 * RATIO] = jnp.zeros((BS, WIDE), BF16)

    for i in range(RATIO):
        here, there = pair(p_idx, first + RATIO + i, p_ref[first + RATIO + i])
        table[RATIO + i] = centred(there)
        p7[i] = here
        here, _ = pair(p_idx, first + i, p_ref[first + i])
        table[i] = jnp.concatenate([here, zero], 1)
        here, _ = pair(p_idx, i, p_ref[i])
        p0[i] = here

    last = p7[...].reshape(4 * BS, HALF)
    turned = last.T
    wait_rows()

    for i in range(RATIO):
        row = ROWS - RATIO + i
        places = [column(a_idx, k, row) - RATIO - first for k in range(KA)]
        weights = jnp.concatenate([table[jnp.minimum(place, 2 * RATIO)] for place in places], 0)
        parts[i] = dot(a_last[i], weights).astype(BF16)
        halos[i] = spread(a_last[i], [place - 2 * RATIO for place in places])

    factor = dot(turned, halos[...].reshape(4 * BS, WIDE)).astype(BF16)
    tiles = dot(turned, parts[...].reshape(4 * BS, WIDE))
    low7[...] = tiles[:BS]
    k7[...] = factor[:BS]
    spill = tiles[BS:].astype(BF16)
    down = jnp.concatenate([p0[...].reshape(4 * BS, HALF), jnp.zeros((4 * BS, HALF), BF16)], 0)
    up = jnp.concatenate([last, spill[:, :HALF], spill[:, HALF:], factor[BS:, :HALF], factor[BS:, HALF:]], 0)
    second = lax.axis_index("col") & 1 == 1
    inter[...] = jnp.where(second, up, down)
    in_chip = jnp.where(second, down, up)
    intra[...] = in_chip
    final[...] = in_chip


def inner_body(groups, a_idx, p_idx, a_ref, p_ref, copies, rows, table, pairs, products, earlier=None):
    zero = jnp.zeros((BS, HALF), BF16)
    table[3 * ROWS] = jnp.zeros((BS, WIDE), BF16)
    copies[0].wait()
    for g in range(GROUPS):
        for row in range(g * RATIO, (g + 1) * RATIO):
            if not {g - 1, g, g + 1} & set(groups):
                continue
            here, there = pair(p_idx, row, p_ref[row])
            if g + 1 in groups:
                table[row] = jnp.concatenate([here, zero], 1)
            if g in groups:
                table[ROWS + row] = centred(there)
                pairs[g, (row % RATIO) * BS : (row % RATIO + 1) * BS] = here
            if g - 1 in groups:
                table[2 * ROWS + row] = jnp.concatenate([zero, here], 1)
    for copy in copies[1:]:
        copy.wait()
    for g in groups:
        for i in range(RATIO):
            row = g * RATIO + i
            blocks = []
            for k in range(KA):
                at = column(a_idx, k, row)
                place = (at // RATIO - g) * ROWS + at - RATIO
                blocks.append(table[jnp.where(at < RATIO, 3 * ROWS, place) if g == 0 else place])
            products[g, i * BS : (i + 1) * BS] = dot(a_ref[row], jnp.concatenate(blocks, 0)).astype(BF16)
    before = None
    for i in range(GROUPS):
        terms = [] if before is None else [padded(before)]
        before = None
        if i in groups:
            both = dot_rows(pairs[i], products[i])
            before = both[BS:]
            terms.append(shifted(both[:BS]))
        if earlier is not None and len(terms) + (i in (0, GROUPS - 1)) < 2:
            terms.append(earlier[i])
        if terms:
            rows[i] = sum(terms)


def factor0(a_idx, a_ref, pairs):
    h0 = jnp.concatenate([spread(a_ref[i], [column(a_idx, k, i) for k in range(KA)]) for i in range(RATIO)], 0)
    return dot_rows(pairs[0], h0).astype(BF16)


FIRST, SECOND = (1, 2, 3, 4, 5), (0, 6)


def early():
    return jnp.logical_and(lax.axis_index("col") == 0, lax.axis_index("row") > 0)


def late():
    return lax.axis_index("col") >= lax.axis_size("col") - 2


vmem = lambda *shape: pltpu.VMEM(shape[:-1], shape[-1])
PAYLOAD = vmem(8 * BS, HALF, BF16)
EDGE_SHAPES = [PAYLOAD] * 3 + [vmem(BS, WIDE, F32), vmem(BS, WIDE, BF16), vmem(RATIO, BS, HALF, BF16)]
OUT = jax.ShapeDtypeStruct((GROUPS, BS, BAND), F32)
FETCH_SCRATCH = [pltpu.SMEM((KA, ROWS), jnp.int32), pltpu.SMEM((2, ROWS), jnp.int32)]


def run(kernel, name, flops, **settings):
    return pl.pallas_call(
        kernel,
        compiler_params=pltpu.CompilerParams(vmem_limit_bytes=20 << 20),
        cost_estimate=pl.CostEstimate(flops=flops, bytes_accessed=1 << 20, transcendentals=0),
        name=name,
        **settings,
    )


def fetch(sources, places, sem):
    copies = [pltpu.make_async_copy(x, y, sem.at[n]) for n, (x, y) in enumerate(zip(sources, places, strict=True))]
    for copy in copies:
        copy.start()
    return copies


def inner_groups(sources, inner_out, scratch):
    a_idx, p_idx, a_ref, p_ref, sem, *rest = scratch
    a_idx_hbm, p_idx_hbm, a_hbm, p_hbm = sources
    copies = fetch((p_hbm, a_idx_hbm, p_idx_hbm, a_hbm), (p_ref, a_idx, p_idx, a_ref), sem)
    for copy in copies[:3]:
        copy.wait()
    inner_body(a_idx, p_idx, a_ref, p_ref, copies[3].wait, *inner_out, *rest)


def edge_kernel(a_idx_hbm, p_idx_hbm, a_hbm, p_hbm, *refs):
    edge_out, a_near, (a_idx, p_idx, a_last, p_ends, sem, *rest) = refs[:6], refs[6], refs[7:]
    near = pl.ds(0, RATIO)
    far = pl.ds(ROWS - 2 * RATIO, 2 * RATIO)
    copies = fetch(
        (p_idx_hbm, a_idx_hbm, p_hbm.at[far], p_hbm.at[near], a_hbm.at[pl.ds(ROWS - RATIO, RATIO)]),
        (p_idx, a_idx, p_ends.at[far], p_ends.at[near], a_last),
        sem,
    )
    whole = pltpu.make_async_copy(a_hbm, a_near, sem.at[5])

    @pl.when(early())
    def _():
        whole.start()

    for copy in copies[:4]:
        copy.wait()
    edge_body(a_idx, p_idx, a_last, p_ends, copies[4].wait, *edge_out, *rest)

    @pl.when(early())
    def _():
        whole.wait()


def edge(operands):
    return run(
        edge_kernel,
        "edge",
        1 << 28,
        in_specs=[ANY] * 4,
        out_specs=[VMEM] * 7,
        out_shape=EDGE_SHAPES + [vmem(ROWS, BS, KA * BS, BF16)],
        scratch_shapes=FETCH_SCRATCH[:2]
        + [
            vmem(RATIO, BS, KA * BS, BF16),
            vmem(ROWS, BS, HALF, BF16),
            pltpu.SemaphoreType.DMA((6,)),
            vmem(2 * RATIO + 1, BS, WIDE, BF16),
            vmem(RATIO, BS, HALF, BF16),
            vmem(RATIO, BS, WIDE, BF16),
            vmem(RATIO, BS, WIDE, BF16),
        ],
    )(*operands)


INNER_SCRATCH = FETCH_SCRATCH + [
    pltpu.SemaphoreType.DMA((2,)),
    vmem(3 * ROWS + 1, BS, WIDE, BF16),
    vmem(GROUPS, 4 * BS, HALF, BF16),
    vmem(GROUPS - 1, 4 * BS, WIDE, BF16),
]


def ahead_kernel(a_idx_from, p_idx_from, a_ref, p_ref, _, __, rows, *refs):
    a_idx, p_idx, sem, *rest = refs[2:]

    @pl.when(early())
    def _():
        copies = fetch((p_idx_from, a_idx_from), (p_idx, a_idx), sem)
        inner_body(FIRST, a_idx, p_idx, a_ref, p_ref, copies, rows, *rest)


def ahead(operands, *sent):
    return run(
        ahead_kernel,
        "ahead",
        1 << 30,
        in_specs=[VMEM] * 4 + [ANY] * 2,
        out_specs=[VMEM] + [ANY] * 2,
        out_shape=[vmem(GROUPS, BS, BAND, F32)] + [PAYLOAD] * 2,
        input_output_aliases={4: 1, 5: 2},
        scratch_shapes=INNER_SCRATCH,
    )(*operands, *sent)


def inner_kernel(a_idx_from, p_idx_from, a_near, p_ref, a_hbm, earlier, rows, k0, *refs):
    a_idx, p_idx, sem, table, pairs, products, a_ref, a_sem = refs
    copies = fetch((p_idx_from, a_idx_from), (p_idx, a_idx), sem)

    @pl.when(early())
    def _():
        inner_body(SECOND, a_idx, p_idx, a_near, p_ref, copies, rows, table, pairs, products, earlier)
        k0[...] = factor0(a_idx, a_near, pairs)

    @pl.when(jnp.logical_not(early()))
    def _():
        whole = pltpu.make_async_copy(a_hbm, a_ref, a_sem)
        whole.start()
        groups = tuple(range(GROUPS - 1))
        inner_body(groups, a_idx, p_idx, a_ref, p_ref, copies + [whole], rows, table, pairs, products)
        k0[...] = factor0(a_idx, a_ref, pairs)


def inner(operands, a_hbm, earlier):
    return run(
        inner_kernel,
        "inner",
        1 << 30,
        in_specs=[VMEM] * 4 + [ANY, VMEM],
        out_specs=[VMEM] * 2,
        out_shape=[vmem(GROUPS, BS, BAND, F32), vmem(HALF, WIDE, BF16)],
        scratch_shapes=INNER_SCRATCH + [vmem(ROWS, BS, KA * BS, BF16), pltpu.SemaphoreType.DMA],
    )(*operands, a_hbm, earlier)


def last_kernel(intra, inter, final, low7, k7, p0, given, k0, out_hbm, rows, sem):
    def out_copy(source, at, size, n):
        return pltpu.make_async_copy(source, out_hbm.at[pl.ds(at, size)], sem.at[n])

    whole = out_copy(given.at[pl.ds(2, GROUPS - 3)], 2, GROUPS - 3, 0)
    whole.start()
    core = lax.axis_index("col") & 1
    in_chip = jnp.where(late(), final[...], intra[...])
    between = inter[...]
    from_before = jnp.where(core == 0, between, in_chip)
    from_after = jnp.where(core == 0, in_chip[: 4 * BS], between[: 4 * BS])
    zero = jnp.zeros((BS, HALF), F32)
    lower7 = dot(k7[...], from_after)
    rows[2] = given[GROUPS - 1] + shifted(low7[...] + jnp.concatenate([zero, lower7], 1))
    copies = [whole, out_copy(rows.at[pl.ds(2, 1)], GROUPS - 1, 1, 1)]
    copies[1].start()
    both0 = dot(k0[...], from_before[: 4 * BS])
    rows[1] = given[1] + padded(jnp.concatenate([both0[BS:], zero], 1))
    copies.append(out_copy(rows.at[pl.ds(1, 1)], 1, 1, 2))
    copies[2].start()
    spill0 = from_before[4 * BS : 5 * BS].astype(F32)
    spill1 = from_before[5 * BS : 6 * BS].astype(F32)
    own = p0[...].reshape(4 * BS, HALF)
    spill1 += dot(from_before[6 * BS : 7 * BS], own[:HALF]) + dot(from_before[7 * BS :], own[HALF:])
    rows[0] = given[0] + shifted(jnp.concatenate([both0[:BS], zero], 1)) + padded(jnp.concatenate([spill0, spill1], 1))
    copies.append(out_copy(rows.at[pl.ds(0, 1)], 0, 1, 3))
    copies[3].start()
    for copy in copies:
        copy.wait()


def last(*args):
    return run(
        last_kernel,
        "last",
        1 << 26,
        in_specs=[VMEM] * 8,
        out_specs=ANY,
        out_shape=OUT,
        scratch_shapes=[vmem(3, BS, BAND, F32), pltpu.SemaphoreType.DMA((4,))],
    )(*args)


def shards(a_blocks, a_index, p_blocks, p_index):
    operands = a_index.T, p_index.T, a_blocks, p_blocks
    in_hbm = [pltpu.with_memory_space_constraint(x, pltpu.HBM) for x in operands]
    idx_p = [pltpu.with_memory_space_constraint(x, pltpu.VMEM) for x in (operands[0], operands[1], operands[3])]
    axes = ("row", "col")
    devices, line = lax.axis_size(axes), lax.axis_size("col")
    intra, inter, final, low7, k7, p0, a_near = edge(in_hbm)
    near = [idx_p[0], idx_p[1], a_near, idx_p[2]]
    within = [(d, d ^ 1) for d in range(devices)]
    most = [(s, t) for s, t in within if s % line < line - 2]
    others = [(s, t) for s, t in within if s % line >= line - 2]
    across = [(d, (d + 1 if d % 2 else d - 1) % devices) for d in range(devices)]
    from_most = lax.ppermute(intra, axes, most)
    earlier, inter, final = ahead(near, inter, final)
    from_across = lax.ppermute(inter, axes, across)
    from_final = lax.ppermute(final, axes, others)
    rows, k0 = inner(near, in_hbm[2], earlier)
    return last(from_most, from_across, from_final, low7, k7, p0, rows, k0)


def solution(mesh):
    blocks = P(("row", "col"), None, None)
    index = P(("row", "col"), None)
    return jax.shard_map(
        shards, mesh=mesh, in_specs=(blocks, index, blocks, index), out_specs=blocks, check_vma=False
    )
```
